32 devices in a mesh: dp: 8 (over y, x, core), mp: 4 (over z).
Axes of the slice: x: 2, y: 2, z: 4, core: 2. Of those that a mesh axis runs over, the one named last changes fastest.
Arguments:
- tokens: bfloat16 [3072, 768], P('dp'), may hold values from -6 to 6
- char_ids: int32 [8, 1536], P('dp'), may hold values from 0 to 999
- token_chars: int32 [8, 384], P('dp'), may hold values from 1 to 8, 1536 in all within a row
- groups: int32 [8], P('dp'), may hold values from 0 to 15
- qkv_weight: bfloat16 [768, 3, 768], P('dp', None, 'mp'), may hold values from -0.21875 to 0.21875
- out_weight: bfloat16 [768, 768], P('mp', 'dp'), may hold values from -6 to 6
- ffn_in: bfloat16 [768, 3072], P('dp', 'mp'), may hold values from -0.21875 to 0.21875
- ffn_out: bfloat16 [3072, 768], P('mp', 'dp'), may hold values from -0.109375 to 0.109375
- conv_weight: bfloat16 [4608, 768], P('dp', 'mp'), may hold values from -0.09375 to 0.09375
- gains: bfloat16 [4, 768], P(None, 'dp'), may hold values from 0.5 to 1.5
- ih_weight: bfloat16 [256, 2304], P(('dp', 'mp')), may hold values from -0.375 to 0.375
- hh_weight: bfloat16 [2304, 384], P(('dp', 'mp')), may hold values from -0.3125 to 0.3125
- gru_bias: bfloat16 [2, 1536], P(None, ('dp', 'mp')), may hold values from -3 to 3
- char_table: bfloat16 [1000, 256], P(None, ('dp', 'mp')), may hold values from -6 to 6
- group_table: bfloat16 [16, 256], P(None, ('dp', 'mp')), may hold values from -3 to 3
- token_cot: bfloat16 [3072, 768], P('dp'), may hold values from -6 to 6
- char_cot: bfloat16 [3072, 768], P('dp'), may hold values from -6 to 6
Outputs:
- token_out: bfloat16 [3072, 768], P('dp')
- char_out: bfloat16 [3072, 768], P('dp')
- token_grad: float32 [3072, 768], P('dp')
- qkv_grad: float32 [768, 3, 768], P('dp', None, 'mp')
- out_grad: float32 [768, 768], P('mp', 'dp')
- ffn_in_grad: float32 [768, 3072], P('dp', 'mp')
- ffn_out_grad: float32 [3072, 768], P('mp', 'dp')
- conv_grad: float32 [4608, 768], P('dp', 'mp')
- gain_grad: float32 [4, 768], P(None, 'dp')
- ih_grad: float32 [256, 2304], P(('dp', 'mp'))
- hh_grad: float32 [2304, 384], P(('dp', 'mp'))
- bias_grad: float32 [2, 1536], P(None, ('dp', 'mp'))
- table_grad: float32 [1000, 256], P(None, ('dp', 'mp'))
- group_grad: float32 [16, 256], P(None, ('dp', 'mp'))
The draws below stay inside these ranges and needn't reach their ends.
Inputs may be any that keep to these rules, and one draw needn't show every extreme that they name: Each row of token_chars sums to 1536 and holds the value 8 somewhere.
All inputs are finite; a program needn't handle non-finite values.
Results may differ from the reference program's by a relative error of at most 0.023.
Values may be sent and summed in bfloat16 or wider, within the bound.
No kernel may reach another device: no remote copies, remote signals or barrier semaphores. Data moves between devices by JAX's collectives and lax.ppermute only.
A program may use at most 192 MiB of HBM per device.

```python
import math
from functools import partial
import jax
import jax.numpy as jnp
import numpy as np
from jax import lax

D = 768
HEADS = 12
FF = 3072
H = 384
VC = 1000
CE = 256
MAXC = 8
GROUPS = 16
LEN = 384
CLEN = 1536
SEQS = 8
TOKENS = 3072


def set_ends(array, stream_key, smallest, largest):
    spot = [jax.random.randint(jax.random.fold_in(stream_key, axis), (), 0, length) for axis, length in enumerate(array.shape)]
    longest = array.shape.index(max(array.shape))
    neighbour = spot[:longest] + [(spot[longest] + 1) % array.shape[longest]] + spot[longest + 1:]
    return array.at[tuple(spot)].set(smallest).at[tuple(neighbour)].set(largest)


def steps_of(rng, extent, pieces, smallest, high):
    gain, own = 1.0, jax.random.fold_in(rng, 6)
    for axis_at, blocks in pieces:
        heights = jnp.exp(jax.random.uniform(jax.random.fold_in(own, axis_at), (blocks,), jnp.float32, smallest / len(pieces), high / len(pieces)))
        gain = gain * jnp.repeat(heights, extent[axis_at] // blocks).reshape([-1 if axis == axis_at else 1 for axis in range(len(extent))])
    return gain


def rank_bounds(count, slope):
    portions = [(1 << 20) // math.isqrt(rank ** slope) + 1 for rank in range(1, count + 1)]
    width = 1 + sum(portions) // (1 << 30)
    return np.cumsum(np.array([max(1, weight // width) for weight in portions]))


def ranked_ids(rng, extent, number_of, skew):
    listing = rank_bounds(number_of, skew)
    pick = jax.random.randint(jax.random.fold_in(rng, 1), extent, 0, int(listing[number_of - 1]))
    rank = jnp.searchsorted(jnp.asarray(listing, jnp.int32), pick, side="right")
    return jax.random.permutation(jax.random.fold_in(rng, 2), number_of)[rank].astype(jnp.int32)


def length_profile(number_of, total, reach, skew):
    loads = [(1 << 20) // math.isqrt(standing ** skew) + 1 for standing in range(2, number_of + 1)]
    surplus, given = total - reach - (number_of - 1), [1] * (number_of - 1)
    while surplus > 0:
        movable = [i for i in range(number_of - 1) if given[i] < reach]
        whole, budget = sum([loads[i] for i in movable]), surplus
        for i in movable:
            extra = min(reach - given[i], max(1, budget * loads[i] // whole), surplus)
            given[i] = given[i] + extra
            surplus = surplus - extra
    return np.array([reach] + given)


def ragged_sizes(stream_key, amount, total, most, slope):
    if amount == 2:
        one = jax.random.randint(stream_key, (), max(1, total - most), min(most, total - 1) + 1)
        return jnp.stack([one, total - one])
    tallies = jnp.asarray(length_profile(amount, total, most, slope), jnp.int32)
    pairs = (amount - 1) // 2
    donor, receiver = tallies[1:1 + 2 * pairs:2], tallies[2:2 + 2 * pairs:2]
    margin = jnp.minimum(donor - 1, most - receiver)
    shifted = jax.random.randint(jax.random.fold_in(stream_key, 1), (pairs,), 0, 1 << 20) % (margin + 1)
    tallies = tallies.at[1:1 + 2 * pairs:2].set(donor - shifted).at[2:2 + 2 * pairs:2].set(receiver + shifted)
    return tallies[jax.random.permutation(jax.random.fold_in(stream_key, 2), amount)]


def bell_draw(own_key, dims, scale, reach, split=(), kind=jnp.bfloat16):
    values = jax.random.normal(own_key, dims, jnp.float32) * scale
    if len(split) > 0:
        values = steps_of(own_key, dims, split, -0.22, 0.18) * values
    return jnp.clip(values, min=-reach, max=reach).astype(kind)


def setup_inputs(seed: int = 0) -> dict:
    arg_keys = jax.random.split(jax.random.key(seed), 18)
    tokens = bell_draw(arg_keys[0], (TOKENS, D), 1.0, 6.0, ((0, 8),))
    char_ids = set_ends(ranked_ids(arg_keys[1], (SEQS, CLEN), VC, 2), jax.random.fold_in(arg_keys[1], 3), 0, VC - 1).astype(jnp.int32)
    token_chars = jax.vmap(lambda own: ragged_sizes(own, LEN, CLEN, MAXC, 2))(jax.random.split(arg_keys[2], SEQS)).reshape((SEQS, LEN)).astype(jnp.int32)
    groups = set_ends(jax.random.randint(arg_keys[3], (SEQS,), 0, GROUPS), jax.random.fold_in(arg_keys[3], 1), 0, GROUPS - 1).astype(jnp.int32)
    qkv_weight = bell_draw(arg_keys[4], (D, 3, D), D ** -0.5, 0.21875, ((0, 8), (2, 4)))
    out_weight = bell_draw(arg_keys[5], (D, D), (max(1, LEN // 512)) ** -0.5, 6.0, ((0, 4), (1, 8)))
    ffn_in = bell_draw(arg_keys[6], (D, FF), D ** -0.5, 0.21875, ((0, 8), (1, 4)))
    ffn_out = bell_draw(arg_keys[7], (FF, D), FF ** -0.5, 0.109375, ((0, 4), (1, 8)))
    conv_weight = bell_draw(arg_keys[8], (6 * D, D), (6 * D) ** -0.5, 0.09375, ((0, 8), (1, 4)))
    gains = jnp.clip(1.0 + 0.1 * jax.random.normal(arg_keys[9], (4, D), jnp.float32), 0.5, 1.5).astype(jnp.bfloat16)
    ih_weight = bell_draw(arg_keys[10], (CE, 6 * H), CE ** -0.5, 0.375, ((0, 32),))
    hh_weight = bell_draw(arg_keys[11], (6 * H, H), H ** -0.5, 0.3125, ((0, 32),))
    gru_bias = bell_draw(arg_keys[12], (2, 4 * H), 0.5, 3.0, ((1, 32),))
    char_table = bell_draw(arg_keys[13], (VC, CE), 1.0, 6.0, ((1, 32),))
    group_table = bell_draw(arg_keys[14], (GROUPS, CE), 0.5, 3.0, ((1, 32),))
    token_cot = bell_draw(arg_keys[15], (TOKENS, D), 1.0, 6.0, ((0, 8),))
    char_cot = bell_draw(arg_keys[16], (TOKENS, D), 1.0, 6.0, ((0, 8),))
    return {"tokens": tokens, "char_ids": char_ids, "token_chars": token_chars, "groups": groups, "qkv_weight": qkv_weight, "out_weight": out_weight, "ffn_in": ffn_in, "ffn_out": ffn_out, "conv_weight": conv_weight, "gains": gains, "ih_weight": ih_weight, "hh_weight": hh_weight, "gru_bias": gru_bias, "char_table": char_table, "group_table": group_table, "token_cot": token_cot, "char_cot": char_cot}


@jax.custom_vjp
def low(v):
    return lax.optimization_barrier(v.astype(jnp.bfloat16)).astype(jnp.float32)

@jax.custom_vjp
def low_back(v):
    return v

def low_keep(v):
    return (low(v), None)

def low_pass(kept, grad):
    return (grad,)

def back_keep(v):
    return (v, None)

def back_low(kept, grad):
    return (low(grad),)
low.defvjp(low_keep, low_pass)
low_back.defvjp(back_keep, back_low)
NORM_EPS = 1e-05
HIGH_PREC = lax.Precision.HIGHEST

def matmul(left_op, right_op):
    return jnp.dot(left_op, right_op, precision=HIGH_PREC, preferred_element_type=jnp.float32)

def norm_rows(rows_in, gain_row):
    row_mean = lax.optimization_barrier(jnp.mean(rows_in, axis=-1, keepdims=True))
    centred = rows_in - row_mean
    spread = lax.optimization_barrier(jnp.mean(centred * centred, axis=-1, keepdims=True))
    return centred * lax.rsqrt(spread + NORM_EPS) * gain_row

def gelu_fn(rows_in):
    return jax.nn.gelu(rows_in, approximate=True)

def attend_block(query_rows, key_rows, values):
    scores = jnp.einsum('qhd,khd->hqk', query_rows, key_rows, precision=HIGH_PREC) * 0.125
    scores = low_back(scores)
    attn_probs = low(jax.nn.softmax(scores, axis=-1))
    return jnp.einsum('hqk,khd->qhd', attn_probs, values, precision=HIGH_PREC)

def gru_step(hidden_state, inputs_now, rec_weight, bias_row, live_col):
    unit_count = rec_weight.shape[1]
    recurrent = low_back(matmul(low(hidden_state), rec_weight.T))
    reset_gate = jax.nn.sigmoid(inputs_now[:, :unit_count] + bias_row[:unit_count] + recurrent[:, :unit_count])
    update = jax.nn.sigmoid(inputs_now[:, unit_count:2 * unit_count] + bias_row[unit_count:2 * unit_count] + recurrent[:, unit_count:2 * unit_count])
    carried = recurrent[:, 2 * unit_count:] + bias_row[3 * unit_count:]
    fresh_state = jnp.tanh(inputs_now[:, 2 * unit_count:] + bias_row[2 * unit_count:3 * unit_count] + reset_gate * carried)
    moved_state = (1.0 - update) * fresh_state + update * hidden_state
    return hidden_state + live_col * (moved_state - hidden_state)

def char_side(letters, counts, group_id, ih_w, hh_w, bias_w, table_w, group_w):
    seq_len = counts.shape[0]
    starts = (jnp.cumsum(counts) - counts).astype(jnp.int32)
    slot_ids = jnp.arange(MAXC, dtype=jnp.int32)
    live_slots = (slot_ids[None, :] < counts[:, None]).astype(jnp.float32)
    forward_pos = starts[:, None] + jnp.minimum(slot_ids[None, :], counts[:, None] - 1)
    backward_pos = starts[:, None] + jnp.maximum(counts[:, None] - 1 - slot_ids[None, :], 0)
    group_row = group_w[group_id]
    gate_width = 3 * H
    finals = []
    for direction, positions in ((0, forward_pos), (1, backward_pos)):
        embeds = low(table_w[letters[positions]] + group_row)
        gate_in = low_back(matmul(embeds.reshape(seq_len * MAXC, CE), ih_w[:, direction * gate_width:(direction + 1) * gate_width]))
        gate_in = gate_in.reshape(seq_len, MAXC, gate_width)
        rec_weight = hh_w[direction * gate_width:(direction + 1) * gate_width]
        hidden_state = jnp.zeros((seq_len, H), jnp.float32)
        for position in range(MAXC):
            hidden_state = gru_step(hidden_state, gate_in[:, position], rec_weight, bias_w[direction], live_slots[:, position:position + 1])
        finals.append(low(hidden_state))
    return jnp.concatenate(finals, 1)

def layer_one(tokens, letters, counts, group_id, qkv_w, out_w, in_w, down_w, conv_w, gain_w, ih_w, hh_w, bias_w, table_w, group_w):
    seq_len = tokens.shape[0]
    head_size = D // HEADS
    packed = low(low_back(matmul(tokens, qkv_w.reshape(D, 3 * D))))
    packed = packed.reshape(seq_len, 3, HEADS, head_size)
    queries = packed[:, 0]
    key_rows = packed[:, 1]
    values = packed[:, 2]
    block_rows = min(512, seq_len)
    attn = lax.map(jax.checkpoint(partial(attend_block, key_rows=key_rows, values=values)), queries.reshape(seq_len // block_rows, block_rows, HEADS, head_size))
    attn = low(low_back(attn.reshape(seq_len, D)))
    first_sum = tokens + low_back(matmul(attn, out_w))
    normed_one = norm_rows(first_sum, gain_w[0])
    hidden_pre = low_back(matmul(low(normed_one), in_w))
    hidden = low(gelu_fn(hidden_pre))
    second = normed_one + low_back(matmul(hidden, down_w))
    normed_two = norm_rows(second, gain_w[1])
    char_rows = char_side(letters, counts, group_id, ih_w, hh_w, bias_w, table_w, group_w)
    mixed_rows = jnp.concatenate([low(normed_two), char_rows], 1)
    blank_row = jnp.zeros((1, 2 * D), jnp.float32)
    earlier_rows = jnp.concatenate([blank_row, mixed_rows[:-1]], 0)
    later_rows = jnp.concatenate([mixed_rows[1:], blank_row], 0)
    joined_pre = low_back(matmul(jnp.concatenate([earlier_rows, mixed_rows, later_rows], 1), conv_w))
    joined_all = low(gelu_fn(joined_pre))
    return (norm_rows(normed_two + joined_all, gain_w[2]), norm_rows(char_rows + joined_all, gain_w[3]))

def reference(tokens, char_ids, token_chars, groups, qkv_weight, out_weight, ffn_in, ffn_out, conv_weight, gains, ih_weight, hh_weight, gru_bias, char_table, group_table, token_cot, char_cot):
    per_group = math.gcd(SEQS, 4)
    group_count = SEQS // per_group
    weights = tuple((weight_arr.astype(jnp.float32) for weight_arr in (qkv_weight, out_weight, ffn_in, ffn_out, conv_weight, gains, ih_weight, hh_weight, gru_bias, char_table, group_table)))
    zero_grads = tuple((jnp.zeros(weight_arr.shape, jnp.float32) for weight_arr in weights))
    stacked = (tokens.reshape(group_count, per_group, LEN, D), char_ids.reshape(group_count, per_group, CLEN), token_chars.reshape(group_count, per_group, LEN), groups.reshape(group_count, per_group), token_cot.reshape(group_count, per_group, LEN, D), char_cot.reshape(group_count, per_group, LEN, D))

    def one_group(carry, inputs):
        tokens_part, chars_part, counts_part, groups_part, token_cot_part, char_cot_part = inputs

        def forward(tokens_in, *params):

            def single(tokens_one, chars_one, counts_one, group_one):
                return layer_one(tokens_one, chars_one, counts_one, group_one, *params)
            return jax.vmap(single)(tokens_in, chars_part, counts_part, groups_part)
        outputs, pull = jax.vjp(forward, tokens_part.astype(jnp.float32), *weights)
        grads = pull((token_cot_part.astype(jnp.float32), char_cot_part.astype(jnp.float32)))
        carry = tuple((total_grad + new_grad for total_grad, new_grad in zip(carry, grads[1:])))
        return (carry, (outputs[0].astype(jnp.bfloat16), outputs[1].astype(jnp.bfloat16), grads[0]))
    totals, results = lax.scan(one_group, zero_grads, stacked)
    token_out = results[0].reshape(TOKENS, D)
    char_out = results[1].reshape(TOKENS, D)
    token_grad = results[2].reshape(TOKENS, D)
    return (token_out, char_out, token_grad, totals[0], totals[1], totals[2], totals[3], totals[4], totals[5], totals[6], totals[7], totals[8], totals[9], totals[10])
```

```python
import jax
import jax.numpy as jnp
from jax import lax
from jax.experimental import pallas as pl
from jax.experimental.pallas import tpu as pltpu
from jax.sharding import PartitionSpec as P

HEADS = 12
MAXC = 8
NORM_EPS = 1e-05
BF = jnp.bfloat16
F32 = jnp.float32
GROUP_LANE = 96
MB = 1 << 20


def dot(left, right, dims):
    return lax.dot_general(left, right, (dims, ((), ())), preferred_element_type=F32)


def product(left, right):
    return dot(left, right, ((1,), (0,)))


def product_tn(left, right):
    return dot(left, right, ((0,), (0,)))


def product_nt(left, right):
    return dot(left, right, ((1,), (1,)))


def swap(rows, axis, mask):
    size = lax.axis_size(axis)
    return lax.ppermute(rows, axis, [(i, i ^ mask) for i in range(size)])


def place(blocks, where, count, axis=0):
    number = len(blocks)
    first = blocks[0]
    shape = first.shape[:axis] + (count,) + first.shape[axis:]

    def body(where_ref, *refs):
        out, sems = refs[number], refs[number + 1]
        copies = [
            pltpu.make_async_copy(
                refs[i], out.at[(slice(None),) * axis + (where_ref[i],)], sems.at[i]
            )
            for i in range(number)
        ]
        for copy in copies:
            copy.start()
        for copy in copies:
            copy.wait()

    return pl.pallas_call(
        body,
        out_shape=jax.ShapeDtypeStruct(shape, first.dtype),
        in_specs=[pl.BlockSpec(memory_space=pltpu.SMEM)]
        + [pl.BlockSpec(memory_space=pl.ANY)] * number,
        out_specs=pl.BlockSpec(memory_space=pl.ANY),
        scratch_shapes=[pltpu.SemaphoreType.DMA((number,))],
        compiler_params=pltpu.CompilerParams(vmem_limit_bytes=MB),
    )(jnp.stack(where).astype(jnp.int32), *blocks)


def quick():
    return lax.axis_size("dp") == 8


def gather_mp(rows):
    size, own = lax.axis_size("mp"), lax.axis_index("mp")
    blocks = [rows] + [swap(rows, "mp", mask) for mask in range(1, size)]
    return place(blocks, [own ^ mask for mask in range(size)], size)


def gather_dp_from(blocks_of, axis):
    size, own = lax.axis_size("dp"), lax.axis_index("dp")
    masks = list(range(0, size, 2))
    blocks = [blocks_of] + [swap(blocks_of, "dp", mask) for mask in masks[1:]]
    other = [swap(block, "dp", 1) for block in blocks]
    where = [own ^ mask for mask in masks] + [own ^ mask ^ 1 for mask in masks]
    return place(blocks + other, where, size, axis)


def gather_dp(rows, axis=0):
    if not quick():
        return lax.all_gather(rows, "dp", axis=axis)
    return gather_dp_from(rows, axis)


def gather_all(rows):
    if not quick():
        full = lax.all_gather(rows, ("dp", "mp"), axis=0)
        return full.reshape((lax.axis_size("dp"), lax.axis_size("mp")) + rows.shape)
    return gather_dp_from(gather_mp(rows), 0)


def take(blocks, index, axis=0):
    return lax.dynamic_index_in_dim(blocks, index, axis, keepdims=False)


def scatter_mp(blocks):
    size, own = lax.axis_size("mp"), lax.axis_index("mp")
    total = take(blocks, own).astype(F32)
    for mask in range(1, size):
        total = total + swap(take(blocks, own ^ mask), "mp", mask).astype(F32)
    return total


def scatter_dp(blocks):
    size, own = lax.axis_size("dp"), lax.axis_index("dp")
    if not quick():
        return lax.psum_scatter(blocks.astype(F32), "dp", scatter_dimension=0)
    core, chip = own & 1, own >> 1
    pairs = blocks.reshape((size // 2, 2) + blocks.shape[1:])
    got = swap(take(pairs, 1 - core, 1), "dp", 1)
    both = (take(pairs, core, 1).astype(F32) + got.astype(F32)).astype(BF)
    total = take(both, chip).astype(F32)
    for mask in range(1, size // 2):
        total = total + swap(take(both, chip ^ mask), "dp", 2 * mask).astype(F32)
    return total


def norm_parts(rows_in):
    row_mean = jnp.mean(rows_in, axis=-1, keepdims=True)
    centred = rows_in - row_mean
    spread = jnp.mean(centred * centred, axis=-1, keepdims=True)
    scale = lax.rsqrt(spread + NORM_EPS)
    return centred * scale, scale


def norm_back(normal, scale, gain_row, cotangent):
    lifted = cotangent * gain_row
    inner = jnp.mean(lifted * normal, axis=-1, keepdims=True)
    grad = scale * (lifted - jnp.mean(lifted, axis=-1, keepdims=True) - normal * inner)
    return grad, jnp.sum(cotangent * normal, axis=0)


GELU_A = 0.7978845608028654
GELU_B = 0.044715


def gelu_fn(v):
    return 0.5 * v * (1.0 + jnp.tanh(GELU_A * (v + GELU_B * v * v * v)))


def gelu_grad(v):
    t = jnp.tanh(GELU_A * (v + GELU_B * v * v * v))
    return 0.5 * (1.0 + t) + 0.5 * v * (1.0 - t * t) * GELU_A * (1.0 + 3.0 * GELU_B * v * v)


def rows_earlier(rows_in):
    return jnp.concatenate([jnp.zeros_like(rows_in[:1]), rows_in[:-1]], 0)


def rows_later(rows_in):
    return jnp.concatenate([rows_in[1:], jnp.zeros_like(rows_in[:1])], 0)


def attend_forward(query_rows, key_rows, values):
    scores = (
        jnp.einsum("qhd,khd->hqk", query_rows, key_rows, preferred_element_type=F32) * 0.125
    )
    peak_score = jnp.max(scores, axis=-1, keepdims=True)
    raised = jnp.exp(scores - peak_score)
    row_total = jnp.sum(raised, axis=-1, keepdims=True)
    attn_probs = (raised / row_total).astype(BF)
    head_out = jnp.einsum("hqk,khd->qhd", attn_probs, values, preferred_element_type=F32)
    return head_out, (peak_score + jnp.log(row_total))[..., 0]


def attend_backward(query_rows, key_rows, values, log_sum, grad_out):
    scores = (
        jnp.einsum("qhd,khd->hqk", query_rows, key_rows, preferred_element_type=F32) * 0.125
    )
    attn_probs = jnp.exp(scores - log_sum[..., None])
    grad_probs = jnp.einsum("qhd,khd->hqk", grad_out, values, preferred_element_type=F32)
    inner_sum = jnp.sum(grad_probs * attn_probs, axis=-1, keepdims=True)
    grad_scores = (attn_probs * (grad_probs - inner_sum)).astype(BF)
    query_grad = 0.125 * jnp.einsum(
        "hqk,khd->qhd", grad_scores, key_rows, preferred_element_type=F32
    )
    key_grad = 0.125 * jnp.einsum(
        "hqk,qhd->khd", grad_scores, query_rows, preferred_element_type=F32
    )
    value_grad = jnp.einsum(
        "hqk,qhd->khd", attn_probs.astype(BF), grad_out, preferred_element_type=F32
    )
    return query_grad, key_grad, value_grad


def sigmoid(v):
    return 0.5 * jnp.tanh(0.5 * v) + 0.5


def one_hot(symbols, group, lanes, table_lanes):
    lane = lax.broadcasted_iota(jnp.int32, (symbols.shape[0], lanes), 1)
    hit = (lane == symbols) | (lane == table_lanes + GROUP_LANE + group)
    return hit.astype(F32).astype(BF)


def encoder_forward(symbols, group, char_pack, hh_full, bias_full, live, table_lanes):
    _, own_rows, _ = live.shape
    units = hh_full.shape[1]
    width = 3 * units
    lanes = table_lanes + 128
    embed = char_pack.shape[0]
    saved_shape = jax.ShapeDtypeStruct((2, MAXC, own_rows, units), BF)

    def body(group_ref, sym, pack, hh, bias, alive, final, emb, prev, rst, upd, car, fre, state):
        for way in range(2):
            hits = one_hot(sym[way], group_ref[0], lanes, table_lanes)
            rows = product_nt(hits, pack[:, 2 * width :]).astype(BF)
            emb[way] = rows.reshape(MAXC, own_rows, embed)
        state[...] = jnp.zeros_like(state)

        @pl.loop(0, MAXC)
        def _(slot):
            live_col = alive[slot]
            for way in range(2):
                hidden = state[way]
                low = hidden.astype(BF)
                prev[way, slot] = low
                gate = product(emb[way, slot], pack[:, way * width : (way + 1) * width])
                rec = product_nt(low, hh[way * width : (way + 1) * width])
                b_r = bias[way : way + 1, :units]
                b_z = bias[way : way + 1, units : 2 * units]
                b_n = bias[way : way + 1, 2 * units : 3 * units]
                b_c = bias[way : way + 1, 3 * units :]
                reset = sigmoid(gate[:, :units] + b_r + rec[:, :units])
                update = sigmoid(gate[:, units : 2 * units] + b_z + rec[:, units : 2 * units])
                carried = rec[:, 2 * units :] + b_c
                fresh = jnp.tanh(gate[:, 2 * units :] + b_n + reset * carried)
                rst[way, slot] = reset.astype(BF)
                upd[way, slot] = update.astype(BF)
                car[way, slot] = carried.astype(BF)
                fre[way, slot] = fresh.astype(BF)
                moved = (1.0 - update) * fresh + update * hidden
                state[way] = hidden + live_col * (moved - hidden)

        for way in range(2):
            final[:, way * units : (way + 1) * units] = state[way].astype(BF)

    vmem = pl.BlockSpec(memory_space=pltpu.VMEM)
    return pl.pallas_call(
        body,
        out_shape=[
            jax.ShapeDtypeStruct((own_rows, 2 * units), BF),
            jax.ShapeDtypeStruct((2, MAXC, own_rows, embed), BF),
        ]
        + [saved_shape] * 5,
        in_specs=[pl.BlockSpec(memory_space=pltpu.SMEM)] + [vmem] * 5,
        out_specs=[vmem] * 7,
        scratch_shapes=[pltpu.VMEM((2, own_rows, units), F32)],
        compiler_params=pltpu.CompilerParams(vmem_limit_bytes=40 * MB),
    )(group, symbols, char_pack, hh_full, bias_full, live)


def encoder_backward(
    grad_final, symbols, group, char_pack, hh_full, live, embeds, saved, table_lanes
):
    own_rows = live.shape[1]
    units = hh_full.shape[1]
    width = 3 * units
    lanes = table_lanes + 128
    embed = char_pack.shape[0]
    count = MAXC * own_rows

    def body(
        group_ref, grad_in, sym, pack, hh, alive, emb, prev, rst, upd, car, fre,
        pack_grad, hh_grad, bias_grad, grad, low, inner_low, sums,
    ):
        for way in range(2):
            grad[way] = grad_in[:, way * units : (way + 1) * units]
        sums[...] = jnp.zeros_like(sums)

        @pl.loop(0, MAXC)
        def _(step):
            slot = MAXC - 1 - step
            live_col = alive[slot]
            at = pl.ds(pl.multiple_of(slot * own_rows, 16), own_rows)
            for way in range(2):
                before = prev[way, slot].astype(F32)
                reset = rst[way, slot].astype(F32)
                update = upd[way, slot].astype(F32)
                carried = car[way, slot].astype(F32)
                fresh = fre[way, slot].astype(F32)
                g = grad[way]
                moved = live_col * g
                grad_fresh = moved * (1.0 - update)
                grad_update = moved * (before - fresh)
                grad_inner = grad_fresh * (1.0 - fresh * fresh)
                grad_carried = grad_inner * reset
                grad_reset = grad_carried * carried * (1.0 - reset)
                grad_z = grad_update * update * (1.0 - update)
                sums[way, 0] += grad_reset
                sums[way, 1] += grad_z
                sums[way, 2] += grad_inner
                sums[way, 3] += grad_carried
                low[way, at, :units] = grad_reset.astype(BF)
                low[way, at, units : 2 * units] = grad_z.astype(BF)
                low[way, at, 2 * units :] = grad_carried.astype(BF)
                inner_low[way, at, :] = grad_inner.astype(BF)
                back = product(low[way, at, :], hh[way * width : (way + 1) * width])
                grad[way] = g - moved + moved * update + back

        table_total = jnp.zeros((embed, lanes), F32)
        for way in range(2):
            for part in range(4):
                bias_grad[way, part : part + 1, :] = jnp.sum(sums[way, part], 0, keepdims=True)
            rows = emb[way].reshape(count, embed)
            gates = low[way, :, : 2 * units]
            inner = inner_low[way]
            left = way * width
            pack_grad[:, left : left + 2 * units] = product_tn(rows, gates).astype(BF)
            pack_grad[:, left + 2 * units : left + width] = product_tn(rows, inner).astype(BF)
            embed_grad = product_nt(gates, pack[:, left : left + 2 * units]) + product_nt(
                inner, pack[:, left + 2 * units : left + width]
            )
            hits = one_hot(sym[way], group_ref[0], lanes, table_lanes)
            table_total = table_total + product_tn(embed_grad.astype(BF), hits)
            hh_grad[left : left + width] = product_tn(
                low[way], prev[way].reshape(count, units)
            ).astype(BF)
        pack_grad[:, 2 * width :] = table_total.astype(BF)

    vmem = pl.BlockSpec(memory_space=pltpu.VMEM)
    return pl.pallas_call(
        body,
        out_shape=[
            jax.ShapeDtypeStruct(char_pack.shape, BF),
            jax.ShapeDtypeStruct(hh_full.shape, BF),
            jax.ShapeDtypeStruct((2, 4, units), F32),
        ],
        in_specs=[pl.BlockSpec(memory_space=pltpu.SMEM)] + [vmem] * 11,
        out_specs=[vmem] * 3,
        scratch_shapes=[
            pltpu.VMEM((2, own_rows, units), F32),
            pltpu.VMEM((2, count, width), BF),
            pltpu.VMEM((2, count, units), BF),
            pltpu.VMEM((2, 4, own_rows, units), F32),
        ],
        compiler_params=pltpu.CompilerParams(vmem_limit_bytes=48 * MB),
    )(group, grad_final, symbols, char_pack, hh_full, live, embeds, *saved)


def per_device(
    tokens,
    char_ids,
    token_chars,
    groups,
    qkv_weight,
    out_weight,
    ffn_in,
    ffn_out,
    conv_weight,
    gains,
    ih_weight,
    hh_weight,
    gru_bias,
    char_table,
    group_table,
    token_cot,
    char_cot,
):
    dp_size, mp_size = lax.axis_size("dp"), lax.axis_size("mp")
    mp_index = lax.axis_index("mp")
    seq_len, model = tokens.shape
    local = out_weight.shape[0]
    head_size = model // HEADS
    heads = local // head_size
    own_rows = seq_len // mp_size

    def own_part(rows):
        return lax.dynamic_slice_in_dim(rows, mp_index * own_rows, own_rows, 0)

    qkv_full = gather_dp(jnp.transpose(qkv_weight, (1, 0, 2)), 1).reshape(3, model, local)

    ih_rows, ih_cols = ih_weight.shape
    symbols_n = char_table.shape[0]
    table_lanes = -(-symbols_n // 128) * 128
    vocab = jnp.pad(char_table.T, ((0, 0), (0, table_lanes - symbols_n)))
    group_count = group_table.shape[0]
    units = hh_weight.shape[1]
    bias_cols = gru_bias.shape[1]
    gain_cols = gains.shape[1]
    if quick():
        head = jnp.concatenate(
            [
                jnp.pad(gru_bias, ((0, 2), (0, GROUP_LANE - bias_cols))),
                jnp.pad(gains, ((0, 0), (0, GROUP_LANE - gain_cols))),
            ],
            0,
        )
    else:
        head = jnp.zeros((ih_rows, GROUP_LANE), BF)
    misc = jnp.concatenate(
        [head, group_table.T, jnp.zeros((ih_rows, 128 - GROUP_LANE - group_count), BF)], 1
    )
    char_pack4 = gather_all(jnp.concatenate([ih_weight, vocab, misc], 1))
    embed_dim = dp_size * mp_size * ih_rows
    char_pack = char_pack4.reshape(embed_dim, -1)
    misc_at = ih_cols + table_lanes
    if quick():
        small = char_pack4[:, :, :, misc_at:]
        bias_full = jnp.transpose(small[:, :, :2, :bias_cols], (2, 0, 1, 3)).reshape(2, -1)
        gain_full = jnp.transpose(small[:, 0, 4:, :gain_cols], (1, 0, 2)).reshape(4, -1)
    else:
        bias_full = lax.all_gather(gru_bias, ("dp", "mp"), axis=1, tiled=True)
        gain_full = lax.all_gather(gains, "dp", axis=1, tiled=True)
    bias_full = bias_full.astype(F32)
    gain_rows = gain_full.astype(F32)
    hh_full = gather_all(hh_weight).reshape(-1, units)

    out_full = gather_dp(gather_mp(out_weight.T), 1).reshape(mp_size, model, local)
    ffn_full = gather_dp(jnp.stack([ffn_in, ffn_out.T]), 1)
    in_full = ffn_full[0].reshape(model, -1)
    down_full = ffn_full[1].reshape(model, -1)
    conv_full = gather_dp(conv_weight).reshape(3, 2 * model, local)

    packed = [product(tokens, qkv_full[i]).astype(BF) for i in range(3)]
    queries, key_rows, values = [part.reshape(seq_len, heads, head_size) for part in packed]
    head_out, log_sum = attend_forward(queries, key_rows, values)
    attn_low = head_out.reshape(seq_len, local).astype(BF)
    attn_all = gather_mp(attn_low)
    first_sum = tokens.astype(F32)
    for part in range(mp_size):
        first_sum = first_sum + product_nt(attn_all[part], out_full[part])
    normal_one, _ = norm_parts(first_sum)
    normed_one = normal_one * gain_rows[0]
    normed_low = normed_one.astype(BF)
    hidden_pre = product(normed_low, in_full)
    hidden = gelu_fn(hidden_pre).astype(BF)
    down = product_nt(hidden, down_full).astype(BF)
    second = own_part(normed_one) + scatter_mp(down.reshape(mp_size, own_rows, model))
    normal_two, scale_two = norm_parts(second)
    normed_two = gather_mp((normal_two * gain_rows[1]).astype(BF)).reshape(seq_len, model)

    counts = token_chars[0]
    starts = jnp.cumsum(counts) - counts
    own_counts = own_part(counts)
    own_starts = own_part(starts)
    slots = jnp.arange(MAXC, dtype=jnp.int32)[:, None]
    ahead = own_starts[None, :] + jnp.minimum(slots, own_counts[None, :] - 1)
    behind = own_starts[None, :] + jnp.maximum(own_counts[None, :] - 1 - slots, 0)
    positions = jnp.stack([ahead, behind]).reshape(2, MAXC * own_rows, 1)
    spot = lax.broadcasted_iota(jnp.int32, (1, 1, char_ids.shape[1]), 2)
    symbols = jnp.sum(jnp.where(positions == spot, char_ids[0], 0), axis=-1, keepdims=True)
    live = (slots < own_counts[None, :]).astype(F32)[:, :, None]
    final, embeds, *saved = encoder_forward(
        symbols, groups, char_pack, hh_full, bias_full, live, table_lanes
    )
    char_rows = gather_mp(final).reshape(seq_len, model)

    mixed = jnp.concatenate([normed_two, char_rows], 1)
    earlier, later = rows_earlier(mixed), rows_later(mixed)
    joined_pre = (
        product(earlier, conv_full[0]) + product(mixed, conv_full[1]) + product(later, conv_full[2])
    )
    joined = gather_mp(gelu_fn(joined_pre).astype(BF))
    joined = jnp.concatenate([joined[i] for i in range(mp_size)], 1).astype(F32)
    token_sum = normed_two.astype(F32) + joined
    char_sum = char_rows.astype(F32) + joined
    normal_three, scale_three = norm_parts(token_sum)
    normal_four, scale_four = norm_parts(char_sum)
    token_out = (normal_three * gain_rows[2]).astype(BF)
    char_out = (normal_four * gain_rows[3]).astype(BF)

    grad_token_sum, gain_three = norm_back(
        normal_three, scale_three, gain_rows[2], token_cot.astype(F32)
    )
    grad_char_sum, gain_four = norm_back(
        normal_four, scale_four, gain_rows[3], char_cot.astype(F32)
    )
    share = 1.0 / mp_size
    grad_joined = lax.dynamic_slice_in_dim(
        grad_token_sum + grad_char_sum, mp_index * local, local, 1
    )
    grad_pre = (grad_joined * gelu_grad(joined_pre)).astype(BF)
    grad_mixed = (
        product_nt(grad_pre, conv_full[1])
        + rows_later(product_nt(grad_pre, conv_full[0]))
        + rows_earlier(product_nt(grad_pre, conv_full[2]))
    ).astype(BF)
    mixed_token = scatter_mp(grad_mixed[:, :model].reshape(mp_size, own_rows, model))
    mixed_char = scatter_mp(grad_mixed[:, model:].reshape(mp_size, own_rows, model))
    conv_grad = jnp.concatenate(
        [product_tn(part, grad_pre).astype(BF) for part in (earlier, mixed, later)], 0
    )
    conv_grad = scatter_dp(conv_grad.reshape(dp_size, -1, local))

    grad_second, gain_two = norm_back(
        normal_two, scale_two, gain_rows[1], own_part(grad_token_sum) + mixed_token
    )
    second_low = gather_mp(grad_second.astype(BF)).reshape(seq_len, model)
    grad_hidden = (product(second_low, down_full) * gelu_grad(hidden_pre)).astype(BF)
    grad_in = product_nt(grad_hidden, in_full).astype(BF)
    grad_normed_one = grad_second + scatter_mp(grad_in.reshape(mp_size, own_rows, model))
    down_grad = scatter_dp(product_tn(second_low, hidden).astype(BF).reshape(dp_size, -1, hidden.shape[1]))
    in_grad = scatter_dp(product_tn(normed_low, grad_hidden).astype(BF).reshape(dp_size, -1, hidden.shape[1]))

    own_normal, own_scale = norm_parts(own_part(first_sum))
    grad_first, gain_one = norm_back(own_normal, own_scale, gain_rows[0], grad_normed_one)
    first_low = gather_mp(grad_first.astype(BF)).reshape(seq_len, model)
    out_grad = scatter_dp(product_tn(first_low, attn_low).astype(BF).reshape(dp_size, -1, local))
    grad_attn = (
        product(first_low, take(out_full, mp_index)).astype(BF).reshape(seq_len, heads, head_size)
    )
    grad_packed = [
        part.reshape(seq_len, local).astype(BF)
        for part in attend_backward(queries, key_rows, values, log_sum, grad_attn)
    ]
    qkv_grad = jnp.stack([product_tn(tokens, part).astype(BF) for part in grad_packed], 0)
    qkv_grad = jnp.transpose(qkv_grad.reshape(3, dp_size, -1, local), (1, 0, 2, 3))
    qkv_grad = scatter_dp(qkv_grad)
    token_part = sum(product_nt(grad_packed[i], qkv_full[i]) for i in range(3)).astype(BF)
    token_own = grad_first + scatter_mp(token_part.reshape(mp_size, own_rows, model))
    token_grad = gather_mp(token_own.astype(BF)).reshape(seq_len, model).astype(F32)

    grad_final = own_part(grad_char_sum) + mixed_char
    pack_grad, hh_grad, bias_grad = encoder_backward(
        grad_final, symbols, groups, char_pack, hh_full, live, embeds, saved, table_lanes
    )
    bias_grad = bias_grad.reshape(2, -1)
    gain_grad = jnp.stack([gain_one, gain_two, gain_three * share, gain_four * share])
    if quick():
        bias_blocks = jnp.transpose(
            bias_grad.reshape(2, dp_size, mp_size, bias_cols), (1, 2, 0, 3)
        )
        pack4 = pack_grad.reshape(char_pack4.shape)
        hh4 = hh_grad.reshape((dp_size, mp_size) + hh_weight.shape)
        pack_own = scatter_mp(scatter_dp(pack4).astype(BF))
        hh_own = scatter_mp(scatter_dp(hh4).astype(BF))
        ih_grad = pack_own[:, :ih_cols]
        table_grad = pack_own[:, ih_cols : ih_cols + symbols_n].T
        group_at = misc_at + GROUP_LANE
        group_grad = pack_own[:, group_at : group_at + group_count].T
        gain_blocks = jnp.transpose(gain_grad.reshape(4, dp_size, gain_cols), (1, 0, 2))
        tail = jnp.concatenate(
            [
                jnp.pad(bias_blocks, ((0, 0), (0, 0), (0, 2), (0, 128 - bias_cols))),
                jnp.pad(
                    jnp.broadcast_to(
                        gain_blocks[:, None], (dp_size, mp_size) + gains.shape
                    ),
                    ((0, 0), (0, 0), (0, 0), (0, 128 - gain_cols)),
                ),
            ],
            2,
        )
        tail_own = scatter_mp(scatter_dp(tail.astype(BF)).astype(BF))
        bias_own = tail_own[:2, :bias_cols]
        gain_own = tail_own[4:, :gain_cols]
    else:
        both = ("dp", "mp")

        def spread(rows, axis):
            return lax.psum_scatter(
                rows.astype(F32), both, scatter_dimension=axis, tiled=True
            )

        table_at = ih_cols + symbols_n
        group_at = misc_at + GROUP_LANE
        ih_grad = spread(pack_grad[:, :ih_cols], 0)
        hh_own = spread(hh_grad, 0)
        table_grad = spread(pack_grad[:, ih_cols:table_at].T, 1)
        group_grad = spread(pack_grad[:, group_at : group_at + group_count].T, 1)
        bias_own = spread(bias_grad, 1)
        gain_own = lax.psum_scatter(
            lax.psum(gain_grad, "mp"), "dp", scatter_dimension=1, tiled=True
        )
    return (
        token_out,
        char_out,
        token_grad,
        jnp.transpose(qkv_grad, (1, 0, 2)),
        out_grad.T,
        in_grad,
        down_grad.T,
        conv_grad,
        gain_own,
        ih_grad,
        hh_own,
        bias_own,
        table_grad,
        group_grad,
    )


def solution(mesh):
    return jax.shard_map(
        per_device,
        mesh=mesh,
        in_specs=(
            P("dp", None),
            P("dp", None),
            P("dp", None),
            P("dp"),
            P("dp", None, "mp"),
            P("mp", "dp"),
            P("dp", "mp"),
            P("mp", "dp"),
            P("dp", "mp"),
            P(None, "dp"),
            P(("dp", "mp"), None),
            P(("dp", "mp"), None),
            P(None, ("dp", "mp")),
            P(None, ("dp", "mp")),
            P(None, ("dp", "mp")),
            P("dp", None),
            P("dp", None),
        ),
        out_specs=(
            P("dp", None),
            P("dp", None),
            P("dp", None),
            P("dp", None, "mp"),
            P("mp", "dp"),
            P("dp", "mp"),
            P("mp", "dp"),
            P("dp", "mp"),
            P(None, "dp"),
            P(("dp", "mp"), None),
            P(("dp", "mp"), None),
            P(None, ("dp", "mp")),
            P(None, ("dp", "mp")),
            P(None, ("dp", "mp")),
        ),
        check_vma=False,
    )
```

```python
import jax
import jax.numpy as jnp
from jax import lax
from jax.experimental import pallas as pl
from jax.experimental.pallas import tpu as pltpu
from jax.sharding import PartitionSpec as P

COST_SCALE = 4.0
COSTS = {
    "attention_kernel": 2.2, "middle_kernel": 3.3, "joining_kernel": 1.5, "turn_kernel": 3.3,
    "char_half_kernel": 0.8, "conv_grad_kernel": 1.5, "feed_back_kernel": 1.3,
    "layer_split_kernel": 1.6, "encoder_forward": 10.0, "encoder_backward": 13.0,
    "attention_back_kernel": 2.8, "qkv_split_kernel": 1.3, "layer_final_kernel": 1.5,
}
HEADS = 12
MAXC = 8
NORM_EPS = 1e-05
BF = jnp.bfloat16
F32 = jnp.float32
GROUP_LANE = 96
MB = 1 << 20


def dot(left, right, dims):
    return lax.dot_general(left, right, (dims, ((), ())), preferred_element_type=F32)


def product(left, right):
    return dot(left, right, ((1,), (0,)))


def product_tn(left, right):
    return dot(left, right, ((0,), (0,)))


def product_nt(left, right):
    return dot(left, right, ((1,), (1,)))


def swap(rows, axis, mask):
    size = lax.axis_size(axis)
    return lax.ppermute(rows, axis, [(i, i ^ mask) for i in range(size)])


def quick():
    return lax.axis_size("dp") == 8


def take(blocks, index, axis=0):
    return lax.dynamic_index_in_dim(blocks, index, axis, keepdims=False)


def share_mp(block):
    return [block] + [swap(block, "mp", m) for m in range(1, lax.axis_size("mp"))]


def pass_on(blocks):
    return [blocks[0]] + [swap(blocks[m], "mp", m) for m in range(1, len(blocks))]


def share_dp(block):
    even = [block] + [swap(block, "dp", a) for a in range(2, lax.axis_size("dp"), 2)]
    blocks = []
    for got in even:
        blocks += [got, swap(got, "dp", 1)]
    return blocks


def sum_dp(keep, send):
    got = swap(send, "dp", 1)
    first, *others = merge_kernel(keep, got)
    return [first] + [swap(block, "dp", 2 * i + 2) for i, block in enumerate(others)]


GELU_A = 0.7978845608028654
GELU_B = 0.044715


def gelu_both(v):
    t = jnp.tanh(GELU_A * (v + GELU_B * v * v * v))
    up = 0.5 * (1.0 + t)
    slope = up + 0.5 * v * (1.0 - t * t) * (GELU_A + 3.0 * GELU_A * GELU_B * v * v)
    return v * up, slope


def norm_parts(rows_in):
    row_mean = jnp.mean(rows_in, axis=-1, keepdims=True)
    centred = rows_in - row_mean
    spread = jnp.mean(centred * centred, axis=-1, keepdims=True)
    scale = lax.rsqrt(spread + NORM_EPS)
    return centred * scale, scale


def norm_back(normal, scale, gain_row, cotangent):
    lifted = cotangent * gain_row
    inner = jnp.mean(lifted * normal, axis=-1, keepdims=True)
    grad = scale * (lifted - jnp.mean(lifted, axis=-1, keepdims=True) - normal * inner)
    return grad, jnp.sum(cotangent * normal, axis=0, keepdims=True)


def shape(dims, dtype=BF):
    return jax.ShapeDtypeStruct(dims, dtype)


class Order:
    def __init__(self, axis):
        self.axis = axis

    def __getitem__(self, mask):
        return lax.axis_index(self.axis) ^ mask


def local_kernel(body, outs, args, scratch=(), limit=2.0, scalars=0, after=()):
    vmem = pl.BlockSpec(memory_space=pltpu.VMEM)
    smem = pl.BlockSpec(memory_space=pltpu.SMEM)
    idle = pl.BlockSpec(memory_space=pl.ANY)
    number, skip = len(args), len(after)

    def run(*refs):
        body(*refs[:number], *refs[number + skip :])

    return pl.pallas_call(
        run,
        out_shape=outs,
        in_specs=[smem] * scalars + [vmem] * (number - scalars) + [idle] * skip,
        out_specs=[vmem] * len(outs),
        scratch_shapes=list(scratch),
        compiler_params=pltpu.CompilerParams(vmem_limit_bytes=int(limit * MB)),
        name=body.__qualname__.split(".")[0],
        cost_estimate=pl.CostEstimate(
            flops=int(1e9 * COST_SCALE * COSTS.get(body.__qualname__.split(".")[0], 0.5)), bytes_accessed=0, transcendentals=0
        ),
    )(*args, *after)


def block_rows(ref, at, rows):
    return ref[pl.ds(pl.multiple_of(at * rows, 16), rows), :]


def spill(order, total, outs, rows):
    for m, out in enumerate(outs):
        out[...] = block_rows(total, order[m], rows).astype(BF)


def fill(order, blocks, full, rows):
    for m, block in enumerate(blocks):
        full[pl.ds(pl.multiple_of(order[m] * rows, 16), rows), :] = block[...]


def attention_kernel(tokens, blocks, heads):
    seq, model = tokens.shape
    number = len(blocks)
    _, rows, local = blocks[0].shape
    size = local // heads
    half = seq // 2

    def body(x, *refs):
        order = Order("dp")
        blk = refs[:number]
        w, packed, probs, attn, sent = refs[number:]
        for i in range(3):
            for a in range(number):
                if number == 1:
                    w[i] = blk[a][i]
                else:
                    w[i, pl.ds(pl.multiple_of(order[a] * rows, 16), rows), :] = blk[a][i]
            packed[i] = product(x[...], w[i]).astype(BF)
        for h in range(heads):
            at = slice(h * size, (h + 1) * size)
            scores = product_nt(packed[0, :, at], packed[1, :, at]) * 0.125
            raised = jnp.exp(scores - jnp.max(scores, axis=-1, keepdims=True))
            total = jnp.sum(raised, axis=-1, keepdims=True)
            prob = (raised / total).astype(BF)
            probs[h] = prob
            attn[:, at] = product(prob, packed[2, :, at]).astype(BF)
        sent[:, :local] = attn[:half]
        sent[:, local:] = attn[half:]

    return local_kernel(
        body,
        [
            shape((3, model, local)),
            shape((3, seq, local)),
            shape((heads, seq, seq)),
            shape((seq, local)),
            shape((half, 2 * local)),
        ],
        (tokens, *blocks),
        limit=2,
    )


def middle_kernel(blocks, tokens, out_full, gain_rows, in_full, down_full):
    seq, model = tokens.shape
    number = len(blocks)
    rows = seq // number
    local = out_full.shape[2]
    half = seq // 2
    hid = in_full.shape[1]

    def body(*refs):
        order = Order("mp")
        blk = refs[:number]
        x, wo, g, wi, wd = refs[number : number + 5]
        low, hidden, slope, normal_own, scale_own = refs[number + 5 : number + 10]
        outs = refs[number + 10 : 2 * number + 10]
        total, scales = refs[2 * number + 10 :]
        for top in range(2):
            at = slice(top * half, (top + 1) * half)
            lanes = slice(top * local, (top + 1) * local)
            acc = x[at].astype(F32)
            for m in range(number):
                acc = acc + product_nt(blk[m][:, lanes], wo[m])
            normal, scale = norm_parts(acc)
            total[at] = normal
            scales[at] = scale
            low[at] = (normal * g[0:1]).astype(BF)
        normal_own[...] = block_rows(total, order[0], rows)
        scale_own[...] = block_rows(scales, order[0], rows)
        value, steep = gelu_both(product(low[...], wi[...]))
        hidden[...] = value.astype(BF)
        slope[...] = steep.astype(BF)
        total[...] = product_nt(hidden[...], wd[...])
        spill(order, total, outs, rows)

    return local_kernel(
        body,
        [
            shape((seq, model)),
            shape((seq, hid)),
            shape((seq, hid)),
            shape((rows, model), F32),
            shape((rows, 1), F32),
        ]
        + [shape((rows, model))] * number,
        (*blocks, tokens, out_full, gain_rows, in_full, down_full),
        [pltpu.VMEM((seq, model), F32), pltpu.VMEM((seq, 1), F32)],
        limit=3.21,
    )


def second_kernel(parts, normal_one, gain_rows):
    rows, model = normal_one.shape
    number = len(parts)

    def body(*refs):
        n1, g, normal, scale, low = refs[number:]
        total = n1[...] * g[0:1]
        for part in refs[:number]:
            total = total + part[...].astype(F32)
        xh, r = norm_parts(total)
        normal[...] = xh
        scale[...] = r
        low[...] = (xh * g[1:2]).astype(BF)

    return local_kernel(
        body,
        [shape((rows, model), F32), shape((rows, 1), F32), shape((rows, model))],
        (*parts, normal_one, gain_rows),
        limit=1,
    )


def joining_kernel(token_blocks, char_blocks, conv_full):
    number = len(token_blocks)
    rows, model = token_blocks[0].shape
    seq = number * rows
    local = conv_full.shape[2]
    half = seq // 2

    def body(*refs):
        order = Order("mp")
        tok, chars, conv = refs[:number], refs[number : 2 * number], refs[2 * number]
        mixed, slope, sent, low = refs[2 * number + 1 :]
        for m in range(number):
            at = pl.ds(pl.multiple_of(order[m] * rows, 16), rows)
            mixed[at, :model] = tok[m][...]
            mixed[at, model:] = chars[m][...]
        line = lax.broadcasted_iota(jnp.int32, (seq, 1), 0)
        before = pltpu.roll(product(mixed[...], conv[0]), 1, 0)
        after = pltpu.roll(product(mixed[...], conv[2]), seq - 1, 0)
        pre = product(mixed[...], conv[1])
        pre = pre + jnp.where(line == 0, 0.0, before) + jnp.where(line == seq - 1, 0.0, after)
        value, steep = gelu_both(pre)
        slope[...] = steep.astype(BF)
        low[...] = value.astype(BF)
        sent[:, :local] = low[:half]
        sent[:, local:] = low[half:]

    return local_kernel(
        body,
        [shape((seq, 2 * model)), shape((seq, local)), shape((half, 2 * local))],
        (*token_blocks, *char_blocks, conv_full),
        [pltpu.VMEM((seq, local), BF)],
        limit=2.5,
    )


def turn_kernel(blocks, mixed, token_cot, char_cot, gain_rows, slope, conv_full):
    number = len(blocks)
    seq, model = token_cot.shape
    rows = seq // number
    local = conv_full.shape[2]
    half = seq // 2

    def body(*refs):
        order = Order("mp")
        blk = refs[:number]
        mix, cot_t, cot_c, g, steep, conv = refs[number : number + 6]
        token_out, char_out, own_t, own_c, pre3, gain_t, gain_c = refs[number + 6 : number + 13]
        outs = refs[number + 13 : 2 * number + 13]
        stack, joined, total, picked = refs[2 * number + 13 :]
        for m in range(number):
            stack[order[m]] = blk[m][...]
        for j in range(number):
            at = slice(j * local, (j + 1) * local)
            joined[:half, at] = stack[j, :, :local]
            joined[half:, at] = stack[j, :, local:]
        both = joined[...].astype(F32)
        xh, r = norm_parts(mix[:, :model].astype(F32) + both)
        token_out[...] = (xh * g[2:3]).astype(BF)
        grad_t, gain = norm_back(xh, r, g[2:3], cot_t[...].astype(F32))
        gain_t[...] = gain * (1.0 / number)
        total[...] = grad_t
        own_t[...] = block_rows(total, order[0], rows)
        xh, r = norm_parts(mix[:, model:].astype(F32) + both)
        char_out[...] = (xh * g[3:4]).astype(BF)
        grad_c, gain = norm_back(xh, r, g[3:4], cot_c[...].astype(F32))
        gain_c[...] = gain * (1.0 / number)
        grad_t = total[...] + grad_c
        total[...] = grad_c
        own_c[...] = block_rows(total, order[0], rows)
        for j in range(number):

            @pl.when(order[0] == j)
            def _():
                picked[...] = grad_t[:, j * local : (j + 1) * local]

        grad = (picked[...] * steep[...].astype(F32)).astype(BF).astype(F32)
        line = lax.broadcasted_iota(jnp.int32, (seq, 1), 0)
        pre3[0] = jnp.where(line == seq - 1, 0.0, pltpu.roll(grad, seq - 1, 0)).astype(BF)
        pre3[1] = grad.astype(BF)
        pre3[2] = jnp.where(line == 0, 0.0, pltpu.roll(grad, 1, 0)).astype(BF)
        total[...] = (
            product_nt(pre3[0], conv[0, :model])
            + product_nt(pre3[1], conv[1, :model])
            + product_nt(pre3[2], conv[2, :model])
        )
        spill(order, total, outs, rows)

    return local_kernel(
        body,
        [shape((seq, model))] * 2
        + [shape((rows, model), F32)] * 2
        + [shape((3, seq, local)), shape((1, model), F32), shape((1, model), F32)]
        + [shape((rows, model))] * number,
        (*blocks, mixed, token_cot, char_cot, gain_rows, slope, conv_full),
        [
            pltpu.VMEM((number, half, 2 * local), BF),
            pltpu.VMEM((seq, model), BF),
            pltpu.VMEM((seq, model), F32),
            pltpu.VMEM((seq, local), F32),
        ],
        limit=7.28,
    )


def char_half_kernel(number, pre3, conv_full):
    _, seq, _ = pre3.shape
    model = conv_full.shape[1] // 2
    rows = seq // number

    def body(pre, conv, *refs):
        order = Order("mp")
        outs, total = refs[:number], refs[number]
        total[...] = (
            product_nt(pre[0], conv[0, model:])
            + product_nt(pre[1], conv[1, model:])
            + product_nt(pre[2], conv[2, model:])
        )
        spill(order, total, outs, rows)

    return local_kernel(
        body,
        [shape((rows, model))] * number,
        (pre3, conv_full),
        [pltpu.VMEM((seq, model), F32)],
        limit=2,
    )


def conv_grad_kernel(mixed, pre3):
    local = pre3.shape[2]
    wide = mixed.shape[1]

    def body(mix, pre, grad):
        for k in range(3):
            grad[k] = product_tn(mix[...], pre[k]).astype(BF)

    return local_kernel(body, [shape((3, wide, local))], (mixed, pre3),
        limit=2,
    )[0]


def norm_back_kernel(parts, residual, normal, scale, gain_rows, row, gain_parts=()):
    rows, model = residual.shape
    number = len(parts)
    extra = len(gain_parts)

    def body(*refs):
        res, xh, r, g = refs[number : number + 4]
        others = refs[number + 4 : number + 4 + extra]
        grad, low, gain = refs[number + 4 + extra :]
        total = res[...]
        for part in refs[:number]:
            total = total + part[...].astype(F32)
        out, own = norm_back(xh[...], r[...], g[row : row + 1], total)
        gain[...] = own
        grad[...] = out
        low[:rows] = out.astype(BF)
        if extra:
            line = lax.broadcasted_iota(jnp.int32, (16, model), 0)
            tail = jnp.where(line == 0, own, 0.0)
            for i, other in enumerate(others):
                tail = jnp.where(line == i + 1, other[...], tail)
            low[rows:] = tail.astype(BF)

    return local_kernel(
        body,
        [
            shape((rows, model), F32),
            shape((rows + (16 if extra else 0), model)),
            shape((1, model), F32),
        ],
        (*parts, residual, normal, scale, gain_rows, *gain_parts),
        limit=1,
    )


def feed_back_kernel(blocks, slope, in_full, down_full):
    number = len(blocks)
    rows, model = blocks[0].shape
    seq = number * rows
    hid = slope.shape[1]

    def body(*refs):
        order = Order("mp")
        blk = refs[:number]
        steep, wi, wd, full, grad = refs[number : number + 5]
        outs, total = refs[number + 5 : 2 * number + 5], refs[2 * number + 5]
        fill(order, blk, full, rows)
        grad[...] = (product(full[...], wd[...]) * steep[...].astype(F32)).astype(BF)
        total[...] = product_nt(grad[...], wi[...])
        spill(order, total, outs, rows)

    return local_kernel(
        body,
        [shape((seq, model)), shape((seq, hid))] + [shape((rows, model))] * number,
        (*blocks, slope, in_full, down_full),
        [pltpu.VMEM((seq, model), F32)],
        limit=2.5,
    )


def feed_grad_kernel(second_low, hidden, normed_low, grad_hidden):
    model = second_low.shape[1]
    hid = hidden.shape[1]

    def body(second, hide, low, grad, out):
        out[0] = product_tn(low[...], grad[...]).astype(BF)
        out[1] = product_tn(second[...], hide[...]).astype(BF)

    return local_kernel(
        body,
        [shape((2, model, hid))],
        (second_low, hidden, normed_low, grad_hidden),
        limit=3,
    )[0]


def layer_split_kernel(second_low, hidden, normed_low, grad_hidden, conv_grad, owners):
    model = second_low.shape[1]
    hid = hidden.shape[1]
    taps, wide, local = conv_grad.shape
    rows = model // owners
    conv_rows = taps * wide // owners
    half, part = hid // 2, conv_rows // 2

    def body(second, hide, low, grad, conv, keep, send, whole):
        order = Order("dp")
        whole[:model] = product_tn(low[...], grad[...]).astype(BF)
        whole[model:] = product_tn(second[...], hide[...]).astype(BF)
        for b in range(owners):
            out = send if b % 2 else keep
            for i in range(2):
                at = pl.ds(pl.multiple_of(i * model + order[b] * rows, 16), rows)
                for h in range(2):
                    to = (2 * i + h) * rows
                    out[b // 2, to : to + rows, :] = whole[at, h * half : (h + 1) * half]
            for h in range(2):
                at = pl.ds(pl.multiple_of(order[b] * conv_rows + h * part, 16), part)
                out[b // 2, 4 * rows :, h * local : (h + 1) * local] = conv[at, :]

    return local_kernel(
        body,
        [shape((owners // 2, 4 * rows + part, half))] * 2,
        (second_low, hidden, normed_low, grad_hidden, conv_grad.reshape(taps * wide, local)),
        [pltpu.VMEM((2 * model, hid), BF)],
        limit=6,
    )


def layer_final_kernel(blocks, local, rows):
    high, half = blocks[0].shape
    number = len(blocks)
    part = high - 4 * rows

    def body(*refs):
        grad_in, grad_down, grad_conv = refs[number:]
        total = refs[0][...].astype(F32)
        for ref in refs[1:number]:
            total = total + ref[...].astype(F32)
        for i, out in enumerate((grad_in, grad_down)):
            for h in range(2):
                at = (2 * i + h) * rows
                out[:, h * half : (h + 1) * half] = total[at : at + rows]
        for h in range(2):
            grad_conv[:, h * part : (h + 1) * part] = total[
                4 * rows :, h * local : (h + 1) * local
            ].T

    return local_kernel(
        body,
        [shape((rows, 2 * half), F32)] * 2 + [shape((local, 2 * part), F32)],
        tuple(blocks),
        limit=4,
    )


def attention_back_kernel(blocks, out_own, packed, probs, weights):
    number = len(blocks)
    high, model = blocks[0].shape
    rows = high - 16
    seq = number * rows
    heads = probs.shape[0]
    local = packed.shape[2]
    size = local // heads

    def body(*refs):
        order = Order("mp")
        blk = refs[:number]
        wo, pack, prob, w, full, grads, gains = refs[number : number + 7]
        outs = refs[number + 7 : 2 * number + 7]
        total, grad_attn = refs[2 * number + 7 :]
        sums = jnp.zeros((16, model), F32)
        for m in range(number):
            full[pl.ds(pl.multiple_of(order[m] * rows, 16), rows), :] = blk[m][:rows]
            sums = sums + blk[m][rows:].astype(F32)
        gains[...] = sums
        grad_attn[...] = product(full[...], wo[0]).astype(BF)
        for h in range(heads):
            at = slice(h * size, (h + 1) * size)
            p = prob[h].astype(F32)
            grad_probs = product_nt(grad_attn[:, at], pack[2, :, at])
            inner = jnp.sum(grad_probs * p, axis=-1, keepdims=True)
            scores = (p * (grad_probs - inner)).astype(BF)
            grads[0, :, at] = (product(scores, pack[1, :, at]) * 0.125).astype(BF)
            grads[1, :, at] = (product_tn(scores, pack[0, :, at]) * 0.125).astype(BF)
            grads[2, :, at] = product_tn(prob[h], grad_attn[:, at]).astype(BF)
        total[...] = (
            product_nt(grads[0], w[0]) + product_nt(grads[1], w[1]) + product_nt(grads[2], w[2])
        )
        spill(order, total, outs, rows)

    return local_kernel(
        body,
        [shape((seq, model)), shape((3, seq, local)), shape((16, model), F32)]
        + [shape((rows, model))] * number,
        (*blocks, out_own, packed, probs, weights),
        [pltpu.VMEM((seq, model), F32), pltpu.VMEM((seq, local), BF)],
        limit=3,
    )


def qkv_grad_kernel(tokens, grads, first_low, attn):
    model = tokens.shape[1]
    local = attn.shape[1]

    def body(x, g, first, a, out):
        for i in range(3):
            out[i] = product_tn(x[...], g[i]).astype(BF)
        out[3] = product_tn(first[...], a[...]).astype(BF)

    return local_kernel(
        body,
        [shape((4, model, local))],
        (tokens, grads, first_low, attn),
        limit=2,
        scalars=0,
    )[0]


def qkv_split_kernel(tokens, grads, first_low, attn, gains, gain_count, owners):
    model = tokens.shape[1]
    local = attn.shape[1]
    rows = model // owners

    def body(x, g, first, a, gain, keep, send, whole, small):
        order = Order("dp")
        for i in range(3):
            whole[i] = product_tn(x[...], g[i]).astype(BF)
        whole[3] = product_tn(first[...], a[...]).astype(BF)
        small[...] = jnp.zeros_like(small)
        for d in range(owners):
            small[d, :gain_count, :rows] = gain[:gain_count, d * rows : (d + 1) * rows]
        for b in range(owners):
            out = send if b % 2 else keep
            at = pl.ds(pl.multiple_of(order[b] * rows, 16), rows)
            for i in range(4):
                to, lane = i // 2 * rows, i % 2 * local
                out[b // 2, to : to + rows, lane : lane + local] = whole[i, at, :]
            out[b // 2, 2 * rows :, :] = small[order[b]].astype(BF)

    return local_kernel(
        body,
        [shape((owners // 2, 2 * rows + 16, 2 * local))] * 2,
        (tokens, grads, first_low, attn, gains),
        [pltpu.VMEM((4, model, local), BF), pltpu.VMEM((owners, 16, 2 * local), F32)],
        limit=4,
    )


def qkv_final_kernel(blocks, gain_shape):
    high, wide = blocks[0].shape
    rows, local = (high - 16) // 2, wide // 2
    number = len(blocks)
    gain_count, gain_cols = gain_shape

    def body(*refs):
        qkv, out, gain = refs[number:]
        total = refs[0][...].astype(F32)
        for ref in refs[1:number]:
            total = total + ref[...].astype(F32)
        qkv[0] = total[:rows, :local]
        qkv[1] = total[:rows, local:]
        qkv[2] = total[rows : 2 * rows, :local]
        out[...] = total[rows : 2 * rows, local:].T
        gain[...] = total[2 * rows : 2 * rows + gain_count, :gain_cols]

    return local_kernel(
        body,
        [shape((3, rows, local), F32), shape((local, rows), F32), shape(gain_shape, F32)],
        tuple(blocks),
        limit=3,
    )


def char_final_kernel(blocks, shapes):
    high, wide = blocks[0].shape
    rows = high // 2
    number = len(blocks)
    ih_cols, symbols, groups, bias_shape, hh_shape = shapes
    misc = wide - 128
    units = hh_shape[1]

    def body(*refs):
        ih, table, group, bias, hh = refs[number:]
        total = refs[0][...].astype(F32)
        for ref in refs[1:number]:
            total = total + ref[...].astype(F32)
        ih[...] = total[:rows, :ih_cols]
        table[...] = total[:rows, ih_cols : ih_cols + symbols]
        last = total[:rows, misc:]
        group[...] = last[:, GROUP_LANE : GROUP_LANE + groups]
        bias[...] = last[: bias_shape[0], : bias_shape[1]]
        for g in range(hh_shape[0] // rows):
            hh[g * rows : (g + 1) * rows, :] = total[rows:, g * units : (g + 1) * units]

    return local_kernel(
        body,
        [
            shape((rows, ih_cols), F32),
            shape((rows, symbols), F32),
            shape((rows, groups), F32),
            shape(bias_shape, F32),
            shape(hh_shape, F32),
        ],
        tuple(blocks),
    )


def sum_kernel(residual, parts):
    number = len(parts)

    def body(*refs):
        total = refs[0][...]
        for ref in refs[1 : number + 1]:
            total = total + ref[...].astype(F32)
        refs[number + 1][...] = total.astype(BF)

    return local_kernel(body, [shape(residual.shape)], (residual, *parts))[0]


def stack_kernel(blocks):
    number = len(blocks)

    def body(*refs):
        for i in range(number):
            refs[number][i] = refs[i][...]

    return local_kernel(body, [shape((number,) + blocks[0].shape)], tuple(blocks))[0]


def merge_kernel(keep, got):
    number = keep.shape[0]
    dims = keep.shape[1:]

    def body(keep, got, *outs):
        for i, out in enumerate(outs):
            out[...] = (keep[i].astype(F32) + got[i].astype(F32)).astype(BF)

    return local_kernel(body, [shape(dims)] * number, (keep, got), limit=4)


def pack_kernel(ih, hh, bias, table, group, out, gains):
    rows, ih_cols = ih.shape
    hh_rows, units = hh.shape
    symbols, groups = table.shape[1], group.shape[1]
    lanes = -(-symbols // 128) * 128
    misc = ih_cols + lanes
    wide = misc + 128
    half, local = out.shape[0] // 2, out.shape[1]

    def body(ih, hh, bias, table, group, out, gains, pack, head, top, low):
        top[...] = jnp.zeros_like(top)
        top[:rows, :ih_cols] = ih[...].astype(F32)
        top[:rows, ih_cols : ih_cols + symbols] = table[...].astype(F32)
        top[: bias.shape[0], misc : misc + bias.shape[1]] = bias[...].astype(F32)
        top[:rows, misc + GROUP_LANE : misc + GROUP_LANE + groups] = group[...].astype(F32)
        steps = hh[...].astype(F32)
        for g in range(hh_rows // rows):
            top[rows:, g * units : (g + 1) * units] = steps[g * rows : (g + 1) * rows]
        pack[...] = top[...].astype(BF)
        low[...] = jnp.zeros_like(low)
        low[:half, :local] = out[:half].astype(F32)
        low[:half, local:] = out[half:].astype(F32)
        low[half : half + gains.shape[0], : gains.shape[1]] = gains[...].astype(F32)
        head[...] = low[...].astype(BF)

    return local_kernel(
        body,
        [shape((2 * rows, wide)), shape((half + 16, 2 * local))],
        (ih, hh, bias, table, group, out, gains),
        [pltpu.VMEM((2 * rows, wide), F32), pltpu.VMEM((half + 16, 2 * local), F32)],
    )


def pack_feed_kernel(ffn_in, ffn_down, after):
    def body(wi, wd, out):
        out[0] = wi[...]
        out[1] = wd[...]

    return local_kernel(body, [shape((2,) + ffn_in.shape)], (ffn_in, ffn_down), after=after)[0]


def pack_conv_kernel(conv, after):
    local, rows = conv.shape
    half = rows // 2

    def body(conv, out):
        taps = conv[...].astype(F32).T.astype(BF)
        out[:, :local] = taps[:half]
        out[:, local:] = taps[half:]

    return local_kernel(body, [shape((half, 2 * local))], (conv,), limit=3, after=after)[0]


def unpack_feed_kernel(blocks):
    number = len(blocks)
    _, rows, hid = blocks[0].shape

    def body(*refs):
        order = Order("dp")
        for a in range(number):
            at = pl.ds(pl.multiple_of(order[a] * rows, 16), rows)
            for i in range(2):
                refs[number + i][at, :] = refs[a][i]

    return local_kernel(body, [shape((number * rows, hid))] * 2, tuple(blocks))


def unpack_conv_kernel(blocks):
    number = len(blocks)
    half, wide = blocks[0].shape
    local = wide // 2

    def body(*refs):
        order = Order("dp")
        for a in range(number):
            for h in range(2):
                at = pl.ds(pl.multiple_of((order[a] * 2 + h) * half, 16), half)
                refs[number][at, :] = refs[a][:, h * local : (h + 1) * local]

    return local_kernel(body, [shape((number * wide // local * half, local))], tuple(blocks))[0]


def unpack_out_kernel(blocks, gain_shape):
    number = len(blocks)
    depth, high, wide = blocks[0].shape
    half, local = high - 16, wide // 2
    gain_count, gain_cols = gain_shape

    def body(*refs):
        order = Order("dp")
        out, gain, stack = refs[number:]
        for a in range(number):
            for h in range(2):
                at = pl.ds(pl.multiple_of((order[a] * 2 + h) * half, 16), half)
                for m in range(depth):
                    out[m, at, :] = refs[a][m, :half, h * local : (h + 1) * local]
            stack[order[a]] = refs[a][0, half:].astype(F32)
        for d in range(number):
            gain[:, d * gain_cols : (d + 1) * gain_cols] = stack[d, :gain_count, :gain_cols]

    return local_kernel(
        body,
        [shape((depth, number * 2 * half, local)), shape((gain_count, number * gain_cols), F32)],
        tuple(blocks),
        [pltpu.VMEM((number, 16, wide), F32)],
    )


def unpack_char_kernel(blocks, units, bias_shape, misc):
    number = len(blocks)
    depth, high, wide = blocks[0].shape
    rows = high // 2
    groups = wide // units
    ways, bias_cols = bias_shape
    total = number * depth

    def body(*refs):
        order8, order = Order("dp"), Order("mp")
        pack, hh, bias, steps, small = refs[number:]
        for a in range(number):
            for m in range(depth):
                whole = refs[a][m].astype(F32)
                at = (a * depth + m) * rows
                if m % 2 == 0:
                    before = whole[:rows]
                else:
                    pack[at - rows : at + rows, :] = jnp.concatenate(
                        [before, whole[:rows]], 0
                    ).astype(BF)
                place = order8[a] * depth + order[m]
                small[place] = whole[:rows, misc:]
                steps[place] = jnp.concatenate(
                    [whole[rows:, g * units : (g + 1) * units] for g in range(groups)], 0
                )
        hh[...] = steps[...].reshape(total * groups * rows, units).astype(BF)
        for k in range(total):
            bias[:, k * bias_cols : (k + 1) * bias_cols] = small[k, :ways, :bias_cols]

    return local_kernel(
        body,
        [
            shape((total * rows, wide)),
            shape((total * groups * rows, units)),
            shape((ways, total * bias_cols), F32),
        ],
        tuple(blocks),
        [
            pltpu.VMEM((total, groups * rows, units), F32),
            pltpu.VMEM((total, rows, wide - misc), F32),
        ],
        limit=6,
    )


def widen_kernel(blocks):
    number = len(blocks)
    rows, model = blocks[0].shape

    def body(*refs):
        order = Order("mp")
        out = refs[number]
        for m in range(number):
            at = pl.ds(pl.multiple_of(order[m] * rows, 16), rows)
            out[at, :] = refs[m][...].astype(F32)

    return local_kernel(
        body, [shape((number * rows, model), F32)], tuple(blocks), limit=1.49
    )[0]


def sigmoid(v):
    return 0.5 * jnp.tanh(0.5 * v) + 0.5


def one_hot(symbols, group, lanes, table_lanes):
    lane = lax.broadcasted_iota(jnp.int32, (symbols.shape[0], lanes), 1)
    hit = (lane == symbols) | (lane == table_lanes + GROUP_LANE + group)
    return hit.astype(F32).astype(BF)


def encoder_forward(group, letters, counts, char_pack, hh_full, bias_full, table_lanes, own_rows):
    units = hh_full.shape[1]
    width = 3 * units
    lanes = table_lanes + 128
    embed = char_pack.shape[0]
    count = MAXC * own_rows
    seq = counts.shape[1]
    chars = letters.shape[1]
    saved_shape = shape((2, MAXC, own_rows, units))

    def body(
        group_ref, let, cnt, pack, hh, bias,
        final, emb, prev, rst, upd, car, fre, sym, alive, state,
    ):
        mine = lax.axis_index("mp") * own_rows + lax.broadcasted_iota(jnp.int32, (own_rows, seq), 0)
        line = lax.broadcasted_iota(jnp.int32, (own_rows, seq), 1)
        sizes = cnt[...].astype(F32)
        start = jnp.sum(jnp.where(line < mine, sizes, 0.0), axis=1, keepdims=True)
        size = jnp.sum(jnp.where(line == mine, sizes, 0.0), axis=1, keepdims=True)
        spot = lax.broadcasted_iota(jnp.int32, (own_rows, chars), 1).astype(F32)
        values = let[...].astype(F32)
        for slot in range(MAXC):
            alive[slot] = jnp.where(size > slot, 1.0, 0.0)
            for way in range(2):
                if way == 0:
                    at = start + jnp.minimum(float(slot), size - 1.0)
                else:
                    at = start + jnp.maximum(size - 1.0 - slot, 0.0)
                found = jnp.sum(jnp.where(spot == at, values, 0.0), axis=1, keepdims=True)
                sym[way, slot * own_rows : (slot + 1) * own_rows, :] = found.astype(jnp.int32)
        for way in range(2):
            hits = one_hot(sym[way], group_ref[0], lanes, table_lanes)
            rows = product_nt(hits, pack[:, 2 * width :]).astype(BF)
            emb[way] = rows.reshape(MAXC, own_rows, embed)
        state[...] = jnp.zeros_like(state)

        @pl.loop(0, MAXC)
        def _(slot):
            live_col = alive[slot]
            for way in range(2):
                hidden = state[way]
                low = hidden.astype(BF)
                prev[way, slot] = low
                gate = product(emb[way, slot], pack[:, way * width : (way + 1) * width])
                rec = product_nt(low, hh[way * width : (way + 1) * width])
                b_r = bias[way : way + 1, :units]
                b_z = bias[way : way + 1, units : 2 * units]
                b_n = bias[way : way + 1, 2 * units : 3 * units]
                b_c = bias[way : way + 1, 3 * units :]
                reset = sigmoid(gate[:, :units] + b_r + rec[:, :units])
                update = sigmoid(gate[:, units : 2 * units] + b_z + rec[:, units : 2 * units])
                carried = rec[:, 2 * units :] + b_c
                fresh = jnp.tanh(gate[:, 2 * units :] + b_n + reset * carried)
                rst[way, slot] = reset.astype(BF)
                upd[way, slot] = update.astype(BF)
                car[way, slot] = carried.astype(BF)
                fre[way, slot] = fresh.astype(BF)
                moved = (1.0 - update) * fresh + update * hidden
                state[way] = hidden + live_col * (moved - hidden)

        for way in range(2):
            final[:, way * units : (way + 1) * units] = state[way].astype(BF)

    return local_kernel(
        body,
        [shape((own_rows, 2 * units)), shape((2, MAXC, own_rows, embed))]
        + [saved_shape] * 5
        + [shape((2, count, 1), jnp.int32), shape((MAXC, own_rows, 1), F32)],
        (group, letters, counts, char_pack, hh_full, bias_full),
        [pltpu.VMEM((2, own_rows, units), F32)],
        limit=3,
        scalars=1,
    )


def encoder_backward(
    group, split, grad_parts, symbols, char_pack, hh_full, live, embeds, saved, table_lanes, bias_cols
):
    own_rows = live.shape[1]
    units = hh_full.shape[1]
    width = 3 * units
    lanes = table_lanes + 128
    embed, wide = char_pack.shape
    count = MAXC * own_rows
    pieces = len(grad_parts)

    def body(*refs):
        group_ref = refs[0]
        refs = refs[1:]
        parts = refs[:pieces]
        sym, pack, hh, alive, emb, prev, rst, upd, car, fre = refs[pieces : pieces + 10]
        results = refs[pieces + 10 : pieces + 12 + (not split)]
        grad, low, inner_low, sums, hh_grad, bias_grad = refs[pieces + 12 + (not split) :][:6]
        whole = parts[0][...].astype(F32)
        for part in parts[1:]:
            whole = whole + part[...].astype(F32)
        for way in range(2):
            grad[way] = whole[:, way * units : (way + 1) * units]
        sums[...] = jnp.zeros_like(sums)

        @pl.loop(0, MAXC)
        def _(step):
            slot = MAXC - 1 - step
            live_col = alive[slot]
            at = pl.ds(pl.multiple_of(slot * own_rows, 16), own_rows)
            for way in range(2):
                before = prev[way, slot].astype(F32)
                reset = rst[way, slot].astype(F32)
                update = upd[way, slot].astype(F32)
                carried = car[way, slot].astype(F32)
                fresh = fre[way, slot].astype(F32)
                g = grad[way]
                moved = live_col * g
                grad_fresh = moved * (1.0 - update)
                grad_update = moved * (before - fresh)
                grad_inner = grad_fresh * (1.0 - fresh * fresh)
                grad_carried = grad_inner * reset
                grad_reset = grad_carried * carried * (1.0 - reset)
                grad_z = grad_update * update * (1.0 - update)
                for part, what in enumerate((grad_reset, grad_z, grad_inner, grad_carried)):
                    sums[way, part] += jnp.sum(what.reshape(own_rows // 8, 8, units), 0)
                low[way, at, :units] = grad_reset.astype(BF)
                low[way, at, units : 2 * units] = grad_z.astype(BF)
                low[way, at, 2 * units :] = grad_carried.astype(BF)
                inner_low[way, at, :] = grad_inner.astype(BF)
                back = product(low[way, at, :], hh[way * width : (way + 1) * width])
                grad[way] = g - moved + moved * update + back

        if split:
            order8, order = Order("dp"), Order("mp")
            keep, send = results
            owners, depth = split
            strip = embed // owners
            steps = 2 * width // owners
            small = refs[-1]

        def pack_out(value, left):
            if not split:
                results[0][:, left : left + value.shape[1]] = value.astype(BF)
                return
            for b in range(owners):
                out = send if b % 2 else keep
                out[b // 2, :strip, left : left + value.shape[1]] = value[
                    b * strip : (b + 1) * strip
                ].astype(BF)

        table_total = jnp.zeros((embed, lanes), F32)
        for way in range(2):
            for part in range(4):
                bias_grad[way : way + 1, part * units : (part + 1) * units] = jnp.sum(
                    sums[way, part], 0, keepdims=True
                )
            rows = emb[way].reshape(count, embed)
            gates = low[way, :, : 2 * units]
            inner = inner_low[way]
            left = way * width
            pack_out(product_tn(rows, gates), left)
            pack_out(product_tn(rows, inner), left + 2 * units)
            embed_grad = product_nt(gates, pack[:, left : left + 2 * units]) + product_nt(
                inner, pack[:, left + 2 * units : left + width]
            )
            hits = one_hot(sym[way], group_ref[0], lanes, table_lanes)
            table_total = table_total + product_tn(embed_grad.astype(BF), hits)
            hh_grad[left : left + width] = product_tn(
                low[way], prev[way].reshape(count, units)
            ).astype(BF)
        if not split:
            pack_out(table_total, 2 * width)
            results[1][...] = hh_grad[...]
            results[2][...] = bias_grad[...]
            return
        pack_out(table_total[:, :table_lanes], 2 * width)
        small[...] = jnp.zeros_like(small)
        for k in range(owners * depth):
            small[k, :2, :bias_cols] = bias_grad[:, k * bias_cols : (k + 1) * bias_cols]
        lane = lax.broadcasted_iota(jnp.int32, (strip, 128), 1)
        for b in range(owners):
            out = send if b % 2 else keep
            mine = jnp.concatenate([small[order8[b] * depth + order[m]] for m in range(depth)], 0)
            last = table_total[b * strip : (b + 1) * strip, table_lanes:]
            out[b // 2, :strip, wide - 128 :] = jnp.where(lane < GROUP_LANE, mine, last).astype(BF)
            for g in range(steps // strip):
                at = pl.ds(pl.multiple_of(order8[b] * steps + g * strip, 16), strip)
                out[b // 2, strip:, g * units : (g + 1) * units] = hh_grad[at, :]

    outs = [shape(char_pack.shape), shape(hh_full.shape), shape((2, 4 * units), F32)]
    scratch = [
        pltpu.VMEM((2, own_rows, units), F32),
        pltpu.VMEM((2, count, width), BF),
        pltpu.VMEM((2, count, units), BF),
        pltpu.VMEM((2, 4, 8, units), F32),
        pltpu.VMEM(hh_full.shape, BF),
        pltpu.VMEM((2, 4 * units), F32),
    ]
    if split:
        owners, depth = split
        strip = embed // owners
        outs = [shape((owners // 2, 2 * strip, wide))] * 2
        scratch.append(pltpu.VMEM((owners * depth, strip // depth, 128), F32))
    return local_kernel(
        body,
        outs,
        (group, *grad_parts, symbols, char_pack, hh_full, live, embeds, *saved),
        scratch,
        limit=13.00,
        scalars=1,
    )


def char_split_kernel(number, blocks, units):
    high, wide = blocks[0].shape
    strip = high // 2
    rows = strip // number
    groups = wide // units
    pieces = len(blocks)

    def body(*refs):
        order = Order("mp")
        outs, steps = refs[pieces : pieces + number], refs[pieces + number]
        total = refs[0][...].astype(F32)
        for ref in refs[1:pieces]:
            total = total + ref[...].astype(F32)
        for g in range(groups):
            steps[g * strip : (g + 1) * strip, :] = total[strip:, g * units : (g + 1) * units]
        for m, out in enumerate(outs):
            low = jnp.concatenate(
                [
                    steps[pl.ds(pl.multiple_of((order[m] * groups + g) * rows, 8), rows), :]
                    for g in range(groups)
                ],
                1,
            )
            out[...] = jnp.concatenate([total[m * rows : (m + 1) * rows], low], 0).astype(BF)

    return local_kernel(
        body,
        [shape((2 * rows, wide))] * number,
        tuple(blocks),
        [pltpu.VMEM((strip * groups, units), F32)],
        limit=2,
    )


def per_device(
    tokens,
    char_ids,
    token_chars,
    groups,
    qkv_weight,
    out_weight,
    ffn_in,
    ffn_out,
    conv_weight,
    gains,
    ih_weight,
    hh_weight,
    gru_bias,
    char_table,
    group_table,
    token_cot,
    char_cot,
):
    dp_size, mp_size = lax.axis_size("dp"), lax.axis_size("mp")
    mp_index = lax.axis_index("mp")
    seq_len, model = tokens.shape
    local = out_weight.shape[0]
    heads = local // (model // HEADS)
    own_rows = seq_len // mp_size
    ih_rows, ih_cols = ih_weight.shape
    symbols_n, group_count = char_table.shape[0], group_table.shape[0]
    table_lanes = -(-symbols_n // 128) * 128
    misc_at = ih_cols + table_lanes
    units = hh_weight.shape[1]
    bias_cols, gain_cols = gru_bias.shape[1], gains.shape[1]
    both = ("dp", "mp")

    qkv_own = jnp.transpose(qkv_weight, (1, 0, 2))
    if quick():
        qkv_blocks = share_dp(qkv_own)
        pack, head = pack_kernel(
            ih_weight, hh_weight, gru_bias, char_table.T, group_table.T, out_weight.T, gains
        )
        out_blocks = share_dp(stack_kernel(share_mp(head)))
        out_full, gain_rows = unpack_out_kernel(out_blocks, gains.shape)
        feed_own = pack_feed_kernel(ffn_in, ffn_out.T, qkv_blocks[2:3])
        feed_blocks = share_dp(feed_own)
        in_full, down_full = unpack_feed_kernel(feed_blocks)
        char_blocks = share_dp(stack_kernel(share_mp(pack)))
        char_pack, hh_full, bias_full = unpack_char_kernel(
            char_blocks, units, gru_bias.shape, misc_at
        )
        conv_own = pack_conv_kernel(conv_weight.T, feed_blocks[2:3])
        conv_full = unpack_conv_kernel(share_dp(conv_own))
    else:
        qkv_blocks = [lax.all_gather(qkv_own, "dp", axis=1, tiled=True)]
        vocab = jnp.pad(char_table.T, ((0, 0), (0, table_lanes - symbols_n)))
        misc = jnp.pad(group_table.T, ((0, 0), (GROUP_LANE, 128 - GROUP_LANE - group_count)))
        char_pack = lax.all_gather(
            jnp.concatenate([ih_weight, vocab, misc], 1), both, axis=0, tiled=True
        )
        hh_full = lax.all_gather(hh_weight, both, axis=0, tiled=True)
        bias_full = lax.all_gather(gru_bias, both, axis=1, tiled=True).astype(F32)
        gain_rows = lax.all_gather(gains, "dp", axis=1, tiled=True).astype(F32)
        out_full = lax.all_gather(
            lax.all_gather(out_weight.T, "dp", axis=0, tiled=True), "mp", axis=0
        )
        order = jnp.stack([mp_index ^ m for m in range(mp_size)]).astype(jnp.int32)
        out_full = jnp.take(out_full, order, axis=0)
        ffn_full = lax.all_gather(jnp.stack([ffn_in, ffn_out.T]), "dp", axis=1, tiled=True)
        in_full, down_full = ffn_full[0], ffn_full[1]
        conv_full = lax.all_gather(conv_weight, "dp", axis=0, tiled=True)
    conv_full = conv_full.reshape(3, 2 * model, local)

    qkv_full, packed, probs, attn_low, sent = attention_kernel(tokens, qkv_blocks, heads)
    normed_low, hidden, hidden_slope, normal_one, scale_one, *down = middle_kernel(
        share_mp(sent), tokens, out_full, gain_rows, in_full, down_full
    )
    normal_two, scale_two, two_low = second_kernel(pass_on(down), normal_one, gain_rows)
    token_blocks = share_mp(two_low)

    final, embeds, *saved, symbols, live = encoder_forward(
        groups, char_ids, token_chars, char_pack, hh_full, bias_full, table_lanes, own_rows
    )
    char_rows = share_mp(final)

    mixed, joined_slope, sent = joining_kernel(token_blocks, char_rows, conv_full)
    token_out, char_out, own_token, own_char, pre3, gain_three, gain_four, *token_parts = (
        turn_kernel(
            share_mp(sent), mixed, token_cot, char_cot, gain_rows, joined_slope, conv_full
        )
    )
    mixed_token = pass_on(token_parts)
    mixed_char = pass_on(char_half_kernel(mp_size, pre3, conv_full))
    conv_grad = conv_grad_kernel(mixed, pre3)

    grad_second, second_low, gain_two = norm_back_kernel(
        mixed_token, own_token, normal_two, scale_two, gain_rows, 1
    )
    second_full, grad_hidden, *in_parts = feed_back_kernel(
        share_mp(second_low), hidden_slope, in_full, down_full
    )
    feed_args = (second_full, hidden, normed_low, grad_hidden)

    grad_first, first_low, _ = norm_back_kernel(
        pass_on(in_parts), grad_second, normal_one, scale_one, gain_rows, 0,
        (gain_two, gain_three, gain_four),
    )
    first_full, grad_packed, gain_grad, *token_parts = attention_back_kernel(
        share_mp(first_low), out_full, packed, probs, qkv_full
    )
    token_own = sum_kernel(grad_first, pass_on(token_parts))
    token_grad = widen_kernel(share_mp(token_own))

    backward = (
        [own_char] + mixed_char, symbols, char_pack, hh_full, live, embeds, saved,
        table_lanes, bias_cols,
    )
    group_at = misc_at + GROUP_LANE
    table_to = ih_cols + symbols_n
    gain_count = gains.shape[0]
    if quick():
        in_grad, down_grad, conv_grad = layer_final_kernel(
            sum_dp(*layer_split_kernel(*feed_args, conv_grad, dp_size)), local, model // dp_size
        )
        conv_grad = conv_grad.T
        qkv_grad, out_grad, gain_own = qkv_final_kernel(
            sum_dp(
                *qkv_split_kernel(
                    tokens, grad_packed, first_full, attn_low, gain_grad, gain_count, dp_size
                )
            ),
            gains.shape,
        )
        char_parts = sum_dp(*encoder_backward(groups, (dp_size, mp_size), *backward))
        ih_grad, table_grad, group_grad, bias_own, hh_own = char_final_kernel(
            pass_on(char_split_kernel(mp_size, char_parts, units)),
            (ih_cols, symbols_n, group_count, gru_bias.shape, hh_weight.shape),
        )
        table_grad, group_grad = table_grad.T, group_grad.T
    else:

        def spread(rows, axis):
            return lax.psum_scatter(rows.astype(F32), both, scatter_dimension=axis, tiled=True)

        attn_grads = qkv_grad_kernel(tokens, grad_packed, first_full, attn_low)
        attn_grads = lax.psum_scatter(
            attn_grads.astype(F32), "dp", scatter_dimension=1, tiled=True
        )
        qkv_grad, out_grad = attn_grads[:3], attn_grads[3].T
        feed_grad = feed_grad_kernel(*feed_args)
        feed_grad = lax.psum_scatter(
            feed_grad.astype(F32), "dp", scatter_dimension=1, tiled=True
        )
        in_grad, down_grad = feed_grad[0], feed_grad[1]
        conv_grad = conv_grad.reshape(-1, local).astype(F32)
        conv_grad = lax.psum_scatter(conv_grad, "dp", scatter_dimension=0, tiled=True)
        gain_own = lax.psum_scatter(
            gain_grad[:gain_count], "dp", scatter_dimension=1, tiled=True
        )
        pack_grad, hh_grad, bias_grad = encoder_backward(groups, None, *backward)
        ih_grad = spread(pack_grad[:, :ih_cols], 0)
        hh_own = spread(hh_grad, 0)
        table_grad = spread(pack_grad[:, ih_cols:table_to].T, 1)
        group_grad = spread(pack_grad[:, group_at : group_at + group_count].T, 1)
        bias_own = spread(bias_grad, 1)
    return (
        token_out,
        char_out,
        token_grad,
        jnp.transpose(qkv_grad, (1, 0, 2)),
        out_grad,
        in_grad,
        down_grad.T,
        conv_grad,
        gain_own,
        ih_grad,
        hh_own,
        bias_own,
        table_grad,
        group_grad,
    )


def solution(mesh):
    return jax.shard_map(
        per_device,
        mesh=mesh,
        in_specs=(
            P("dp", None),
            P("dp", None),
            P("dp", None),
            P("dp"),
            P("dp", None, "mp"),
            P("mp", "dp"),
            P("dp", "mp"),
            P("mp", "dp"),
            P("dp", "mp"),
            P(None, "dp"),
            P(("dp", "mp"), None),
            P(("dp", "mp"), None),
            P(None, ("dp", "mp")),
            P(None, ("dp", "mp")),
            P(None, ("dp", "mp")),
            P("dp", None),
            P("dp", None),
        ),
        out_specs=(
            P("dp", None),
            P("dp", None),
            P("dp", None),
            P("dp", None, "mp"),
            P("mp", "dp"),
            P("dp", "mp"),
            P("mp", "dp"),
            P("dp", "mp"),
            P(None, "dp"),
            P(("dp", "mp"), None),
            P(("dp", "mp"), None),
            P(None, ("dp", "mp")),
            P(None, ("dp", "mp")),
            P(None, ("dp", "mp")),
        ),
        check_vma=False,
    )
```

```python
import jax
import jax.numpy as jnp
from jax import lax
from jax.experimental import pallas as pl
from jax.experimental.pallas import tpu as pltpu
from jax.sharding import PartitionSpec as P

COST_SCALE = 4.0
COSTS = {"attention_kernel": 2.2, "middle_kernel": 3.6, "joining_kernel": 3.0, "turn_kernel": 2.6, "char_half_kernel": 0.8, "conv_split_kernel": 2.5, "feed_back_kernel": 1.5, "feed_split_kernel": 7.5, "encoder_forward": 11.0, "encoder_steps": 7.5, "encoder_backward": 5.5, "attention_back_kernel": 2.8, "qkv_split_kernel": 1.3}
HEADS = 12
MAXC = 8
NORM_EPS = 1e-05
BF = jnp.bfloat16
F32 = jnp.float32
GROUP_LANE = 96
HALO = 32
HOLDS = frozenset(["b1", "b16", "b21", "b22", "b25", "b26", "b4", "b6", "s2", "s5", "s6"])
MB = 1 << 20


def dot(left, right, dims):
    return lax.dot_general(left, right, (dims, ((), ())), preferred_element_type=F32)


def product(left, right):
    return dot(left, right, ((1,), (0,)))


def product_tn(left, right):
    return dot(left, right, ((0,), (0,)))


def product_nt(left, right):
    return dot(left, right, ((1,), (1,)))


def swap(rows, axis, mask):
    size = lax.axis_size(axis)
    return lax.ppermute(rows, axis, [(i, i ^ mask) for i in range(size)])


def quick():
    return lax.axis_size("dp") == 8


def held(**arrays):
    found = []
    for name, array in arrays.items():
        if name in HOLDS:
            found += list(array) if isinstance(array, (list, tuple)) else [array]
    return tuple(found)


def take(blocks, index, axis=0):
    return lax.dynamic_index_in_dim(blocks, index, axis, keepdims=False)


def share_mp(block):
    return [block] + [swap(block, "mp", m) for m in range(1, lax.axis_size("mp"))]


def pass_on(blocks):
    return [blocks[0]] + [swap(blocks[m], "mp", m) for m in range(1, len(blocks))]


def share_dp(block):
    even = [block] + [swap(block, "dp", a) for a in range(2, lax.axis_size("dp"), 2)]
    blocks = []
    for got in even:
        blocks += [got, swap(got, "dp", 1)]
    return blocks


def share_dp_two(first, second):
    lists = []
    for block, near, far in ((first, 2, 4), (second, 4, 2)):
        passed = swap(block, "dp", near)
        even = {0: block, near: passed, far: swap(block, "dp", far), 6: swap(passed, "dp", far)}
        blocks = []
        for a in range(0, 8, 2):
            blocks += [even[a], swap(even[a], "dp", 1)]
        lists.append(blocks)
    return lists


def merge_dp(keep, send, after=()):
    return merge_kernel(keep, swap(send, "dp", 1), after)


def spread_dp(blocks):
    return [blocks[0]] + [swap(block, "dp", 2 * i + 2) for i, block in enumerate(blocks[1:])]


def merge_two(keep, send, after=()):
    return merge_two_kernel(keep, swap(send, "dp", 1), after)


def spread_two(parts, after=()):
    first_keep, first_send, second_keep, second_send = parts
    first, first_next, second, second_next = relay_kernel(
        first_keep, swap(first_send, "dp", 4), second_keep, swap(second_send, "dp", 2), after
    )
    return [first, swap(first_next, "dp", 2), second, swap(second_next, "dp", 4)]


GELU_A = 0.7978845608028654
GELU_B = 0.044715


def gelu_both(v):
    t = jnp.tanh(GELU_A * (v + GELU_B * v * v * v))
    up = 0.5 * (1.0 + t)
    slope = up + 0.5 * v * (1.0 - t * t) * (GELU_A + 3.0 * GELU_A * GELU_B * v * v)
    return v * up, slope


def norm_parts(rows_in):
    row_mean = jnp.mean(rows_in, axis=-1, keepdims=True)
    centred = rows_in - row_mean
    spread = jnp.mean(centred * centred, axis=-1, keepdims=True)
    scale = lax.rsqrt(spread + NORM_EPS)
    return centred * scale, scale


def norm_back(normal, scale, gain_row, cotangent):
    lifted = cotangent * gain_row
    inner = jnp.mean(lifted * normal, axis=-1, keepdims=True)
    grad = scale * (lifted - jnp.mean(lifted, axis=-1, keepdims=True) - normal * inner)
    return grad, jnp.sum(cotangent * normal, axis=0, keepdims=True)


def shape(dims, dtype=BF):
    return jax.ShapeDtypeStruct(dims, dtype)


class Order:
    def __init__(self, axis):
        self.axis = axis

    def __getitem__(self, mask):
        return lax.axis_index(self.axis) ^ mask


class Spot:
    def __init__(self, seq):
        own = lax.axis_index("mp")
        top, pair = own >> 1, own & 1
        self.own, self.top, self.pair = own, top, pair
        self.window = top * (seq // 2 - HALO)
        self.half = top * HALO
        self.quarter = self.half + pair * (seq // 4)
        self.partner = self.half + (1 - pair) * (seq // 4)
        self.beside = (1 - top) * (seq // 2)
        self.in_half = pair * (seq // 4)
        self.partner_in_half = (1 - pair) * (seq // 4)
        self.beside_row = seq // 2 - HALO * top


def rows_at(ref, start, rows):
    return ref[pl.ds(pl.multiple_of(start, 16), rows), :]


def local_kernel(body, outs, args, scratch=(), limit=3.0, scalars=0, after=()):
    vmem = pl.BlockSpec(memory_space=pltpu.VMEM)
    smem = pl.BlockSpec(memory_space=pltpu.SMEM)
    idle = pl.BlockSpec(memory_space=pl.ANY)
    number, skip = len(args), len(after)

    def run(*refs):
        body(*refs[:number], *refs[number + skip :])

    return pl.pallas_call(
        run,
        out_shape=outs,
        in_specs=[smem] * scalars + [vmem] * (number - scalars) + [idle] * skip,
        out_specs=[vmem] * len(outs),
        scratch_shapes=list(scratch),
        compiler_params=pltpu.CompilerParams(vmem_limit_bytes=int((limit + 1.5) * MB)),
        name=body.__qualname__.split(".")[0],
        cost_estimate=pl.CostEstimate(
            flops=int(1e9 * COST_SCALE * COSTS.get(body.__qualname__.split(".")[0], 0.5)), bytes_accessed=0, transcendentals=0
        ),
    )(*args, *after)


def block_rows(ref, at, rows):
    return ref[pl.ds(pl.multiple_of(at * rows, 16), rows), :]


def spill(order, total, outs, rows):
    for m, out in enumerate(outs):
        out[...] = block_rows(total, order[m], rows).astype(BF)


def fill(order, blocks, full, rows):
    for m, block in enumerate(blocks):
        full[pl.ds(pl.multiple_of(order[m] * rows, 16), rows), :] = block[...]


def attention_kernel(tokens, blocks, heads):
    seq, model = tokens.shape
    number = len(blocks)
    _, rows, local = blocks[0].shape
    size = local // heads
    part = (seq // 2 + HALO) // 2

    def body(x, *refs):
        order = Order("dp")
        blk = refs[:number]
        w, packed, probs, attn, same, other = refs[number:]
        spot = Spot(seq)
        for i in range(3):
            for a in range(number):
                if number == 1:
                    w[i] = blk[a][i]
                else:
                    w[i, pl.ds(pl.multiple_of(order[a] * rows, 16), rows), :] = blk[a][i]
            packed[i] = product(x[...], w[i]).astype(BF)
        for h in range(heads):
            at = slice(h * size, (h + 1) * size)
            scores = product_nt(packed[0, :, at], packed[1, :, at]) * 0.125
            raised = jnp.exp(scores - jnp.max(scores, axis=-1, keepdims=True))
            total = jnp.sum(raised, axis=-1, keepdims=True)
            prob = (raised / total).astype(BF)
            probs[h] = prob
            attn[:, at] = product(prob, packed[2, :, at]).astype(BF)
        for out, start in ((same, spot.window), (other, seq // 2 - HALO - spot.window)):
            for top in range(2):
                at = pl.ds(pl.multiple_of(start + top * part, 16), part)
                out[:, top * local : (top + 1) * local] = attn[at, :]

    return local_kernel(
        body,
        [
            shape((3, model, local)),
            shape((3, seq, local)),
            shape((heads, seq, seq)),
            shape((seq, local)),
            shape((part, 2 * local)),
            shape((part, 2 * local)),
        ],
        (tokens, *blocks),
        limit=2,
    )


def middle_kernel(blocks, tokens, out_full, gain_rows, in_set, down_set, after=()):
    seq, model = tokens.shape
    number = len(blocks)
    local = out_full.shape[2]
    sets, _, hid = in_set.shape
    half, rows = seq // 2, seq // 4
    window, part = half + HALO, (half + HALO) // 2

    def body(*refs):
        spot = Spot(seq)
        blk = refs[:number]
        x, wo, g, wi, wd = refs[number : number + 5]
        low_half, hidden_half, slope_half, normal_own, scale_own, base, keep, send = refs[
            number + 5 : number + 13
        ]
        total, scales, low, hidden, slope = refs[number + 13 :]
        for top in range(2):
            at = slice(top * part, (top + 1) * part)
            lanes = slice(top * local, (top + 1) * local)
            acc = rows_at(x, spot.window + top * part, part).astype(F32)
            for m in range(number):
                acc = acc + product_nt(blk[m][:, lanes], wo[m])
            normal, scale = norm_parts(acc)
            total[at] = normal
            scales[at] = scale
            low[at] = (normal * g[0:1]).astype(BF)
        low_half[...] = rows_at(low, spot.half, half)
        normal_own[...] = rows_at(total, spot.quarter, rows)
        scale_own[...] = rows_at(scales, spot.quarter, rows)
        base[:rows] = normal_own[...] * g[0:1]
        base[rows:] = rows_at(total, spot.beside, HALO) * g[0:1]
        for s in range(sets):
            at = slice(s * hid, (s + 1) * hid)
            value, steep = gelu_both(product(low[...], wi[s]))
            hidden[:, at] = value.astype(BF)
            slope[:, at] = steep.astype(BF)
        hidden_half[...] = rows_at(hidden, spot.half, half)
        slope_half[...] = rows_at(slope, spot.half, half)
        whole = product_nt(hidden[:, :hid], wd[0])
        for s in range(1, sets):
            whole = whole + product_nt(hidden[:, s * hid : (s + 1) * hid], wd[s])
        total[...] = whole
        beside = rows_at(total, spot.beside, HALO).astype(BF)
        for out, start in ((keep, spot.quarter), (send, spot.partner)):
            out[:rows] = rows_at(total, start, rows).astype(BF)
            out[rows:] = beside

    return local_kernel(
        body,
        [
            shape((half, model)),
            shape((half, sets * hid)),
            shape((half, sets * hid)),
            shape((rows, model), F32),
            shape((rows, 1), F32),
            shape((rows + HALO, model), F32),
            shape((rows + HALO, model)),
            shape((rows + HALO, model)),
        ],
        (*blocks, tokens, out_full, gain_rows, in_set, down_set),
        [
            pltpu.VMEM((window, model), F32),
            pltpu.VMEM((window, 1), F32),
            pltpu.VMEM((window, model), BF),
            pltpu.VMEM((window, sets * hid), BF),
            pltpu.VMEM((window, sets * hid), BF),
        ],
        limit=6, after=after)


def second_kernel(keep, got, base, gain_rows):
    high, model = base.shape
    rows = high - HALO

    def body(keep, got, base, g, normal, scale, low, beside):
        xh, r = norm_parts(base[...] + keep[...].astype(F32) + got[...].astype(F32))
        normal[...] = xh[:rows]
        scale[...] = r[:rows]
        out = (xh * g[1:2]).astype(BF)
        low[...] = out[:rows]
        beside[...] = out[rows:]

    return local_kernel(
        body,
        [
            shape((rows, model), F32),
            shape((rows, 1), F32),
            shape((rows, model)),
            shape((HALO, model)),
        ],
        (keep, got, base, gain_rows),
    )


def joining_kernel(token_blocks, char_blocks, conv_set):
    rows, model = token_blocks[0].shape
    seq = 4 * rows
    half = seq // 2
    window = half + HALO
    local = conv_set.shape[2]

    def body(*refs):
        spot = Spot(seq)
        conv, mixed, slope, sent = refs[6:]
        places = ((spot.quarter, rows), (spot.partner, rows), (spot.beside, HALO))
        for i, (start, count) in enumerate(places):
            at = pl.ds(pl.multiple_of(start, 16), count)
            mixed[at, :model] = refs[i][...]
            mixed[at, model:] = refs[3 + i][...]
        line = lax.broadcasted_iota(jnp.int32, (window, 1), 0)
        before = pltpu.roll(product(mixed[...], conv[0]), 1, 0)
        after = pltpu.roll(product(mixed[...], conv[2]), window - 1, 0)
        pre = product(mixed[...], conv[1])
        pre = pre + jnp.where(line == 0, 0.0, before) + jnp.where(line == window - 1, 0.0, after)
        value, steep = gelu_both(pre)
        slope[...] = steep.astype(BF)
        sent[...] = value.astype(BF)

    return local_kernel(
        body,
        [shape((window, 2 * model)), shape((window, local)), shape((window, local))],
        (*token_blocks, *char_blocks, conv_set),
        limit=3,
    )


def turn_kernel(joined_own, joined_got, mixed, token_cot, char_cot, gain_rows, slope, conv_set):
    seq, model = token_cot.shape
    half, rows = seq // 2, seq // 4
    window, local = joined_own.shape
    one = local // 2

    def body(
        mine, got, mix, cot_t, cot_c, g, steep, conv,
        token_half, char_half, quarter, own_t, own_c, pre_half, pre_grad, gain_t, gain_c, keep, send,
        stack, joined, total, picked, outs, pre3, parts,
    ):
        spot = Spot(seq)
        order = Order("mp")
        for m, (ref, lane) in enumerate(((mine, 0), (got, 0), (mine, one), (got, one))):
            stack[order[m]] = ref[:, lane : lane + one]
        for j in range(4):
            joined[:, j * one : (j + 1) * one] = stack[j]
        both = joined[...].astype(F32)
        line = lax.broadcasted_iota(jnp.int32, (window, 1), 0)
        is_own = (line >= spot.quarter) & (line < spot.quarter + rows)
        grad_sum = None
        for lane, cot_ref, out, own, gain, row in (
            (0, cot_t, token_half, own_t, gain_t, 2),
            (model, cot_c, char_half, own_c, gain_c, 3),
        ):
            xh, r = norm_parts(mix[:, lane : lane + model].astype(F32) + both)
            outs[...] = (xh * g[row : row + 1]).astype(BF)
            out[...] = rows_at(outs, spot.half, half)
            quarter[row - 2] = rows_at(outs, spot.quarter, rows)
            cot = rows_at(cot_ref, spot.window, window).astype(F32)
            grad, _ = norm_back(xh, r, g[row : row + 1], cot)
            gain[...] = jnp.sum(jnp.where(is_own, cot * xh, 0.0), axis=0, keepdims=True)
            total[...] = grad
            own[...] = rows_at(total, spot.quarter, rows)
            grad_sum = grad if grad_sum is None else grad_sum + grad
        for j in range(4):

            @pl.when(spot.own == j)
            def _():
                picked[:, :one] = grad_sum[:, j * one : (j + 1) * one]
                picked[:, one:] = grad_sum[:, (j ^ 2) * one : ((j ^ 2) + 1) * one]

        grad = (picked[...] * steep[...].astype(F32)).astype(BF).astype(F32)

        def fan(rows_in, out):
            out[0] = jnp.where(line == window - 1, 0.0, pltpu.roll(rows_in, window - 1, 0)).astype(BF)
            out[1] = rows_in.astype(BF)
            out[2] = jnp.where(line == 0, 0.0, pltpu.roll(rows_in, 1, 0)).astype(BF)

        fan(grad, pre3)
        at = pl.ds(pl.multiple_of(spot.half, 16), half)
        for k in range(3):
            pre_half[k] = pre3[k, at, :]
        is_half = (line >= spot.half) & (line < spot.half + half)
        fan(jnp.where(is_half, grad, 0.0), pre_grad)
        parts[...] = (
            product_nt(pre_half[0], conv[0, :model])
            + product_nt(pre_half[1], conv[1, :model])
            + product_nt(pre_half[2], conv[2, :model])
        )
        keep[...] = rows_at(parts, spot.in_half, rows).astype(BF)
        send[...] = rows_at(parts, spot.partner_in_half, rows).astype(BF)

    return local_kernel(
        body,
        [shape((half, model))] * 2
        + [shape((2, rows, model))]
        + [shape((rows, model), F32)] * 2
        + [shape((3, half, local)), shape((3, window, local))]
        + [shape((1, model), F32)] * 2
        + [shape((rows, model))] * 2,
        (joined_own, joined_got, mixed, token_cot, char_cot, gain_rows, slope, conv_set),
        [
            pltpu.VMEM((4, window, one), BF),
            pltpu.VMEM((window, model), BF),
            pltpu.VMEM((window, model), F32),
            pltpu.VMEM((window, local), F32),
            pltpu.VMEM((window, model), BF),
            pltpu.VMEM((3, window, local), BF),
            pltpu.VMEM((half, model), F32),
        ],
        limit=8,
    )


def char_half_kernel(pre_half, conv_set, after=()):
    _, half, _ = pre_half.shape
    model = conv_set.shape[1] // 2
    rows = half // 2

    def body(pre, conv, keep, send, parts):
        spot = Spot(2 * half)
        parts[...] = (
            product_nt(pre[0], conv[0, model:])
            + product_nt(pre[1], conv[1, model:])
            + product_nt(pre[2], conv[2, model:])
        )
        keep[...] = rows_at(parts, spot.in_half, rows).astype(BF)
        send[...] = rows_at(parts, spot.partner_in_half, rows).astype(BF)

    return local_kernel(
        body,
        [shape((rows, model))] * 2,
        (pre_half, conv_set),
        [pltpu.VMEM((half, model), F32)], after=after)


def conv_grad_kernel(mixed, pre_grad):
    local = pre_grad.shape[2]
    wide = mixed.shape[1]

    def body(mix, pre, grad):
        for k in range(3):
            grad[k] = product_tn(mix[...], pre[k]).astype(BF)

    return local_kernel(body, [shape((3, wide, local))], (mixed, pre_grad), limit=3)[0]


def conv_split_kernel(mixed, pre_grad, owners, sets, after=()):
    taps, _, both = pre_grad.shape
    wide = mixed.shape[1]
    local = both // sets
    rows = taps * wide // owners
    part = rows // 2

    def body(mix, pre, keep, send, whole):
        order = Order("dp")
        for k in range(taps):
            whole[k * wide : (k + 1) * wide] = product_tn(mix[...], pre[k]).astype(BF)
        for b in range(owners):
            out = send if b % 2 else keep
            for h in range(2):
                at = pl.ds(pl.multiple_of(order[b] * rows + h * part, 16), part)
                for s in range(sets):
                    out[b // 2, s, :, h * local : (h + 1) * local] = whole[
                        at, s * local : (s + 1) * local
                    ]

    return local_kernel(
        body,
        [shape((owners // 2, sets, part, 2 * local))] * 2,
        (mixed, pre_grad),
        [pltpu.VMEM((taps * wide, both), BF)],
        limit=7, after=after)


def outputs_kernel(token_half, char_half, got, passed, after=()):
    half, model = token_half.shape
    rows = half // 2

    def body(token_half, char_half, got, passed, token_out, char_out):
        spot = Spot(2 * half)
        mine = pl.ds(pl.multiple_of(spot.top * half, 16), half)
        other = (1 - spot.top) * half
        for i, (own, out) in enumerate(((token_half, token_out), (char_half, char_out))):
            out[mine, :] = own[...]
            for ref, start in ((got, spot.in_half), (passed, spot.partner_in_half)):
                out[pl.ds(pl.multiple_of(other + start, 16), rows), :] = ref[i]

    return local_kernel(
        body, [shape((2 * half, model))] * 2, (token_half, char_half, got, passed), after=after)


def norm_back_kernel(parts, residual, normal, scale, gain_rows, row, gain_parts=(), after=()):
    rows, model = residual.shape
    number = len(parts)
    extra = len(gain_parts)

    def body(*refs):
        res, xh, r, g = refs[number : number + 4]
        others = refs[number + 4 : number + 4 + extra]
        grad, low, gain = refs[number + 4 + extra :]
        total = res[...]
        for part in refs[:number]:
            total = total + part[...].astype(F32)
        out, own = norm_back(xh[...], r[...], g[row : row + 1], total)
        gain[...] = own
        grad[...] = out
        low[:rows] = out.astype(BF)
        if extra:
            line = lax.broadcasted_iota(jnp.int32, (16, model), 0)
            tail = jnp.where(line == 0, own, 0.0)
            for i, other in enumerate(others):
                tail = jnp.where(line == i + 1, other[...], tail)
            low[rows:] = tail.astype(BF)

    return local_kernel(
        body,
        [
            shape((rows, model), F32),
            shape((rows + (16 if extra else 0), model)),
            shape((1, model), F32),
        ],
        (*parts, residual, normal, scale, gain_rows, *gain_parts),
        limit=1, after=after)


def feed_back_kernel(second_own, second_got, slope, in_set, down_set, after=()):
    rows, model = second_own.shape
    half = 2 * rows
    sets, _, hid = in_set.shape

    def body(mine, got, steep, wi, wd, full, grad, keep, send, parts):
        spot = Spot(2 * half)
        full[pl.ds(pl.multiple_of(spot.in_half, 16), rows), :] = mine[...]
        full[pl.ds(pl.multiple_of(spot.partner_in_half, 16), rows), :] = got[...]
        total = None
        for s in range(sets):
            at = slice(s * hid, (s + 1) * hid)
            grad[:, at] = (product(full[...], wd[s]) * steep[:, at].astype(F32)).astype(BF)
            part = product_nt(grad[:, at], wi[s])
            total = part if total is None else total + part
        parts[...] = total
        keep[...] = rows_at(parts, spot.in_half, rows).astype(BF)
        send[...] = rows_at(parts, spot.partner_in_half, rows).astype(BF)

    return local_kernel(
        body,
        [shape((half, model)), shape((half, sets * hid))] + [shape((rows, model))] * 2,
        (second_own, second_got, slope, in_set, down_set),
        [pltpu.VMEM((half, model), F32)],
        limit=3, after=after)


def feed_grad_kernel(second_half, hidden, low_half, grad_hidden, sets):
    model = second_half.shape[1]
    hid = hidden.shape[1] // sets

    def body(second, hide, low, grad, out):
        for s in range(sets):
            at = slice(s * hid, (s + 1) * hid)
            out[s, 0] = product_tn(low[...], grad[:, at]).astype(BF)
            out[s, 1] = product_tn(second[...], hide[:, at]).astype(BF)

    return local_kernel(
        body,
        [shape((sets, 2, model, hid))],
        (second_half, hidden, low_half, grad_hidden),
        limit=3,
    )[0]


def feed_split_kernel(second_half, hidden, low_half, grad_hidden, owners, sets, after=()):
    model = second_half.shape[1]
    hid = hidden.shape[1] // sets
    rows = model // owners
    half = hid // 2

    def body(second, hide, low, grad, keep, send, whole):
        order = Order("dp")
        for s in range(sets):
            lanes = slice(s * hid, (s + 1) * hid)
            whole[:model] = product_tn(low[...], grad[:, lanes]).astype(BF)
            whole[model:] = product_tn(second[...], hide[:, lanes]).astype(BF)
            for b in range(owners):
                out = send if b % 2 else keep
                for i in range(2):
                    at = pl.ds(pl.multiple_of(i * model + order[b] * rows, 16), rows)
                    for h in range(2):
                        to = (2 * i + h) * rows
                        out[b // 2, s, to : to + rows, :] = whole[at, h * half : (h + 1) * half]

    return local_kernel(
        body,
        [shape((owners // 2, sets, 4 * rows, half))] * 2,
        (second_half, hidden, low_half, grad_hidden),
        [pltpu.VMEM((2 * model, hid), BF)],
        limit=6, after=after)


def layer_sum_kernel(parts, after=()):
    dims = parts[0].shape

    def body(*refs):
        keep, send = refs[4:]
        keep[...] = refs[0][...].astype(F32) + refs[1][...].astype(F32)
        send[...] = (refs[2][...].astype(F32) + refs[3][...].astype(F32)).astype(BF)

    return local_kernel(body, [shape(dims, F32), shape(dims)], tuple(parts), after=after)


def feed_final_kernel(keep, got):
    high, half = keep.shape
    rows = high // 4

    def body(keep, got, grad_in, grad_down):
        total = keep[...] + got[...].astype(F32)
        for i, out in enumerate((grad_in, grad_down)):
            for h in range(2):
                at = (2 * i + h) * rows
                out[:, h * half : (h + 1) * half] = total[at : at + rows]

    return local_kernel(body, [shape((rows, 2 * half), F32)] * 2, (keep, got), limit=3)


def conv_final_kernel(keep, got, after=()):
    part, wide = keep.shape
    local = wide // 2

    def body(keep, got, grad):
        total = keep[...] + got[...].astype(F32)
        for h in range(2):
            grad[:, h * part : (h + 1) * part] = total[:, h * local : (h + 1) * local].T

    return local_kernel(body, [shape((local, 2 * part), F32)], (keep, got), limit=3, after=after)[0]


def attention_back_kernel(blocks, out_own, packed, probs, weights, after=()):
    number = len(blocks)
    high, model = blocks[0].shape
    rows = high - 16
    seq = number * rows
    heads = probs.shape[0]
    local = packed.shape[2]
    size = local // heads

    def body(*refs):
        order = Order("mp")
        blk = refs[:number]
        wo, pack, prob, w, full, grads, gains = refs[number : number + 7]
        outs = refs[number + 7 : 2 * number + 7]
        total, grad_attn = refs[2 * number + 7 :]
        sums = jnp.zeros((16, model), F32)
        for m in range(number):
            full[pl.ds(pl.multiple_of(order[m] * rows, 16), rows), :] = blk[m][:rows]
            sums = sums + blk[m][rows:].astype(F32)
        gains[...] = sums
        grad_attn[...] = product(full[...], wo[0]).astype(BF)
        for h in range(heads):
            at = slice(h * size, (h + 1) * size)
            p = prob[h].astype(F32)
            grad_probs = product_nt(grad_attn[:, at], pack[2, :, at])
            inner = jnp.sum(grad_probs * p, axis=-1, keepdims=True)
            scores = (p * (grad_probs - inner)).astype(BF)
            grads[0, :, at] = (product(scores, pack[1, :, at]) * 0.125).astype(BF)
            grads[1, :, at] = (product_tn(scores, pack[0, :, at]) * 0.125).astype(BF)
            grads[2, :, at] = product_tn(prob[h], grad_attn[:, at]).astype(BF)
        total[...] = (
            product_nt(grads[0], w[0]) + product_nt(grads[1], w[1]) + product_nt(grads[2], w[2])
        )
        spill(order, total, outs, rows)

    return local_kernel(
        body,
        [shape((seq, model)), shape((3, seq, local)), shape((16, model), F32)]
        + [shape((rows, model))] * number,
        (*blocks, out_own, packed, probs, weights),
        [pltpu.VMEM((seq, model), F32), pltpu.VMEM((seq, local), BF)],
        limit=3, after=after)


def qkv_grad_kernel(tokens, grads, first_low, attn):
    model = tokens.shape[1]
    local = attn.shape[1]

    def body(x, g, first, a, out):
        for i in range(3):
            out[i] = product_tn(x[...], g[i]).astype(BF)
        out[3] = product_tn(first[...], a[...]).astype(BF)

    return local_kernel(
        body,
        [shape((4, model, local))],
        (tokens, grads, first_low, attn),
        limit=2,
        scalars=0,
    )[0]


def qkv_split_kernel(tokens, grads, first_low, attn, gains, gain_count, owners, after=()):
    model = tokens.shape[1]
    local = attn.shape[1]
    rows = model // owners

    def body(x, g, first, a, gain, keep, send, whole, small):
        order = Order("dp")
        for i in range(3):
            whole[i] = product_tn(x[...], g[i]).astype(BF)
        whole[3] = product_tn(first[...], a[...]).astype(BF)
        small[...] = jnp.zeros_like(small)
        for d in range(owners):
            small[d, :gain_count, :rows] = gain[:gain_count, d * rows : (d + 1) * rows]
        for b in range(owners):
            out = send if b % 2 else keep
            at = pl.ds(pl.multiple_of(order[b] * rows, 16), rows)
            for i in range(4):
                to, lane = i // 2 * rows, i % 2 * local
                out[b // 2, to : to + rows, lane : lane + local] = whole[i, at, :]
            out[b // 2, 2 * rows :, :] = small[order[b]].astype(BF)

    return local_kernel(
        body,
        [shape((owners // 2, 2 * rows + 16, 2 * local))] * 2,
        (tokens, grads, first_low, attn, gains),
        [pltpu.VMEM((4, model, local), BF), pltpu.VMEM((owners, 16, 2 * local), F32)],
        limit=4, after=after)


def qkv_final_kernel(blocks, gain_shape):
    high, wide = blocks[0].shape
    rows, local = (high - 16) // 2, wide // 2
    number = len(blocks)
    gain_count, gain_cols = gain_shape

    def body(*refs):
        qkv, out, gain = refs[number:]
        total = refs[0][...].astype(F32)
        for ref in refs[1:number]:
            total = total + ref[...].astype(F32)
        qkv[0] = total[:rows, :local]
        qkv[1] = total[:rows, local:]
        qkv[2] = total[rows : 2 * rows, :local]
        out[...] = total[rows : 2 * rows, local:].T
        gain[...] = total[2 * rows : 2 * rows + gain_count, :gain_cols]

    return local_kernel(
        body,
        [shape((3, rows, local), F32), shape((local, rows), F32), shape(gain_shape, F32)],
        tuple(blocks),
        limit=3,
    )


def char_final_kernel(blocks, shapes):
    high, wide = blocks[0].shape
    rows = high // 2
    number = len(blocks)
    ih_cols, symbols, groups, bias_shape, hh_shape = shapes
    misc = wide - 128
    units = hh_shape[1]

    def body(*refs):
        ih, table, group, bias, hh = refs[number:]
        total = refs[0][...].astype(F32)
        for ref in refs[1:number]:
            total = total + ref[...].astype(F32)
        ih[...] = total[:rows, :ih_cols]
        table[...] = total[:rows, ih_cols : ih_cols + symbols]
        last = total[:rows, misc:]
        group[...] = last[:, GROUP_LANE : GROUP_LANE + groups]
        bias[...] = last[: bias_shape[0], : bias_shape[1]]
        for g in range(hh_shape[0] // rows):
            hh[g * rows : (g + 1) * rows, :] = total[rows:, g * units : (g + 1) * units]

    return local_kernel(
        body,
        [
            shape((rows, ih_cols), F32),
            shape((rows, symbols), F32),
            shape((rows, groups), F32),
            shape(bias_shape, F32),
            shape(hh_shape, F32),
        ],
        tuple(blocks),
    )


def sum_kernel(residual, parts, after=()):
    number = len(parts)

    def body(*refs):
        total = refs[0][...]
        for ref in refs[1 : number + 1]:
            total = total + ref[...].astype(F32)
        refs[number + 1][...] = total.astype(BF)

    return local_kernel(body, [shape(residual.shape)], (residual, *parts), after=after)[0]


def stack_kernel(blocks, after=()):
    number = len(blocks)

    def body(*refs):
        for i in range(number):
            refs[number][i] = refs[i][...]

    return local_kernel(body, [shape((number,) + blocks[0].shape)], tuple(blocks), after=after)[0]


def merge_kernel(keep, got, after=()):
    number = keep.shape[0]
    dims = keep.shape[1:]

    def body(keep, got, *outs):
        for i, out in enumerate(outs):
            out[...] = (keep[i].astype(F32) + got[i].astype(F32)).astype(BF)

    return local_kernel(body, [shape(dims)] * number, (keep, got), limit=4, after=after)


def merge_two_kernel(keep, got, after=()):
    dims = keep.shape[2:]

    def body(keep, got, *outs):
        for out, half, picks in zip(outs, (0, 0, 1, 1), ((0, 1), (2, 3), (0, 2), (1, 3))):
            for at, i in enumerate(picks):
                out[at] = (keep[i, half].astype(F32) + got[i, half].astype(F32)).astype(BF)

    return local_kernel(
        body, [shape((2,) + dims)] * 4, (keep, got), limit=4, after=after
    )


def relay_kernel(first_keep, first_got, second_keep, second_got, after=()):
    dims = first_keep.shape[1:]

    def body(first_keep, first_got, second_keep, second_got, *outs):
        for i, (keep, got) in enumerate(((first_keep, first_got), (second_keep, second_got))):
            for at in range(2):
                total = keep[at].astype(F32) + got[at].astype(F32)
                outs[2 * i + at][...] = total.astype(BF)

    return local_kernel(
        body,
        [shape(dims)] * 4,
        (first_keep, first_got, second_keep, second_got),
        after=after,
    )


def pack_kernel(ih, hh, bias, table, group, out, gains):
    rows, ih_cols = ih.shape
    hh_rows, units = hh.shape
    symbols, groups = table.shape[1], group.shape[1]
    lanes = -(-symbols // 128) * 128
    misc = ih_cols + lanes
    wide = misc + 128
    half, local = out.shape[0] // 2, out.shape[1]

    args = (ih, hh, bias, table, group, out, gains)

    def body(*refs):
        copies = [
            pltpu.make_async_copy(refs[i], refs[10 + i], refs[17].at[i]) for i in range(7)
        ]
        for copy in copies:
            copy.start()
        pack, top, low = refs[7:10]
        ih, hh, bias, table, group, out, gains = refs[10:17]
        top[...] = jnp.zeros_like(top)
        low[...] = jnp.zeros_like(low)
        for copy in copies:
            copy.wait()
        top[:rows, :ih_cols] = ih[...].astype(F32)
        top[:rows, ih_cols : ih_cols + symbols] = table[...].astype(F32)
        top[: bias.shape[0], misc : misc + bias.shape[1]] = bias[...].astype(F32)
        top[:rows, misc + GROUP_LANE : misc + GROUP_LANE + groups] = group[...].astype(F32)
        steps = hh[...].astype(F32)
        for g in range(hh_rows // rows):
            top[rows:, g * units : (g + 1) * units] = steps[g * rows : (g + 1) * rows]
        pack[:, :wide] = top[...].astype(BF)
        low[:half, :local] = out[:half].astype(F32)
        low[:half, local:] = out[half:].astype(F32)
        low[half : half + gains.shape[0], : gains.shape[1]] = gains[...].astype(F32)
        for g in range((half + 16) // 16):
            at = wide + g * 2 * local
            pack[:, at : at + 2 * local] = low[g * 16 : (g + 1) * 16].astype(BF)

    vmem = pl.BlockSpec(memory_space=pltpu.VMEM)
    return pl.pallas_call(
        body,
        out_shape=shape((2 * rows, wide + (half + 16) // 16 * 2 * local)),
        in_specs=[pl.BlockSpec(memory_space=pltpu.HBM)] * 7,
        out_specs=vmem,
        scratch_shapes=[pltpu.VMEM((2 * rows, wide), F32), pltpu.VMEM((half + 16, 2 * local), F32)]
        + [pltpu.VMEM(arg.shape, BF) for arg in args]
        + [pltpu.SemaphoreType.DMA((7,))],
        compiler_params=pltpu.CompilerParams(vmem_limit_bytes=5 * MB),
        name="pack_kernel",
    )(*args)


def pack_layer_kernel(ffn_in, ffn_down, conv, after):
    rows, hid = ffn_in.shape
    local, taps = conv.shape
    half, part = hid // 2, taps // 2

    def body(wi, wd, conv, out):
        for i, ref in enumerate((wi, wd)):
            for h in range(2):
                at = (2 * i + h) * rows
                out[at : at + rows, :] = ref[:, h * half : (h + 1) * half]
        both = conv[...].astype(F32).T.astype(BF)
        for h in range(2):
            out[4 * rows :, h * local : (h + 1) * local] = both[h * part : (h + 1) * part]

    return local_kernel(
        body,
        [shape((4 * rows + part, half))],
        (ffn_in, ffn_down, conv),
        limit=3,
        after=after,
    )[0]


def unpack_layer_kernel(lists, rows, after=()):
    sets, number = len(lists), len(lists[0])
    high, half = lists[0][0].shape
    part = high - 4 * rows
    local = half // 2

    def body(*refs):
        order = Order("dp")
        outs, conv = refs[sets * number : sets * number + 2], refs[sets * number + 2]
        for a in range(number):
            at = pl.ds(pl.multiple_of(order[a] * rows, 16), rows)
            for s in range(sets):
                ref = refs[s * number + a]
                for i in range(2):
                    for h in range(2):
                        to = (2 * i + h) * rows
                        outs[i][s, at, h * half : (h + 1) * half] = ref[to : to + rows, :]
                for h in range(2):
                    to = pl.ds(pl.multiple_of((order[a] * 2 + h) * part, 16), part)
                    conv[to, s * local : (s + 1) * local] = ref[
                        4 * rows :, h * local : (h + 1) * local
                    ]

    return local_kernel(
        body,
        [shape((sets, number * rows, 2 * half))] * 2
        + [shape((number * 2 * part, sets * local))],
        tuple(lists[0]) + tuple(lists[1]), after=after)


def unpack_out_kernel(lists, start, local, gain_shape):
    number = len(lists[0])
    each, high, _ = lists[0][0].shape
    depth = 2 * each
    gain_count, gain_cols = gain_shape
    rows = gain_cols
    half = rows // 2

    def body(*refs):
        order = Order("dp")
        out, gain, stack = refs[2 * number :]
        for a in range(number):
            for m in range(depth):
                ref = refs[m // each * number + a]
                for g in range(half // 16):
                    for h in range(2):
                        at = pl.ds(
                            pl.multiple_of(order[a] * rows + h * half + g * 16, 16), 16
                        )
                        lane = start + (2 * g + h) * local
                        out[m, at, :] = ref[m % each, :, lane : lane + local]
            stack[order[a]] = refs[a][0, :, start + half // 16 * 2 * local :].astype(F32)
        for d in range(number):
            gain[:, d * gain_cols : (d + 1) * gain_cols] = stack[d, :gain_count, :gain_cols]

    return local_kernel(
        body,
        [shape((depth, number * rows, local)), shape((gain_count, number * gain_cols), F32)],
        tuple(lists[0]) + tuple(lists[1]),
        [pltpu.VMEM((number, 16, 2 * local), F32)],
    )


def unpack_char_kernel(lists, units, bias_shape, misc):
    number = len(lists[0])
    each, high, _ = lists[0][0].shape
    wide = misc + 128
    depth = 2 * each
    rows = high // 2
    groups = wide // units
    ways, bias_cols = bias_shape
    total = number * depth

    def body(*refs):
        order8, order = Order("dp"), Order("mp")
        pack, hh, bias, steps, small = refs[2 * number :]
        for a in range(number):
            for m in range(depth):
                whole = refs[m // each * number + a][m % each, :, :wide].astype(F32)
                at = (a * depth + m) * rows
                if m % 2 == 0:
                    before = whole[:rows]
                else:
                    pack[at - rows : at + rows, :] = jnp.concatenate(
                        [before, whole[:rows]], 0
                    ).astype(BF)
                place = order8[a] * depth + order[m]
                small[place] = whole[:rows, misc:]
                steps[place] = jnp.concatenate(
                    [whole[rows:, g * units : (g + 1) * units] for g in range(groups)], 0
                )
        hh[...] = steps[...].reshape(total * groups * rows, units).astype(BF)
        for k in range(total):
            bias[:, k * bias_cols : (k + 1) * bias_cols] = small[k, :ways, :bias_cols]

    return local_kernel(
        body,
        [
            shape((total * rows, wide)),
            shape((total * groups * rows, units)),
            shape((ways, total * bias_cols), F32),
        ],
        tuple(lists[0]) + tuple(lists[1]),
        [
            pltpu.VMEM((total, groups * rows, units), F32),
            pltpu.VMEM((total, rows, wide - misc), F32),
        ],
        limit=6,
    )


def widen_kernel(blocks, after=()):
    number = len(blocks)
    rows, model = blocks[0].shape

    def body(*refs):
        order = Order("mp")
        out = refs[number]
        for m in range(number):
            at = pl.ds(pl.multiple_of(order[m] * rows, 16), rows)
            out[at, :] = refs[m][...].astype(F32)

    return local_kernel(
        body, [shape((number * rows, model), F32)], tuple(blocks), limit=2, after=after)[0]


def sigmoid(v):
    return 0.5 * jnp.tanh(0.5 * v) + 0.5


def one_hot(symbols, group, lanes, table_lanes):
    lane = lax.broadcasted_iota(jnp.int32, (symbols.shape[0], lanes), 1)
    hit = (lane == symbols) | (lane == table_lanes + GROUP_LANE + group)
    return hit.astype(F32).astype(BF)


def symbols_kernel(letters, counts, own_rows):
    seq = counts.shape[1]
    chars = letters.shape[1]
    every = own_rows + HALO

    def body(let, cnt, sym_all, alive_all, sym, alive):
        spot = Spot(seq)
        row = lax.broadcasted_iota(jnp.int32, (every, seq), 0)
        mine = jnp.where(
            row < own_rows, spot.own * own_rows + row, spot.beside_row - own_rows + row
        )
        line = lax.broadcasted_iota(jnp.int32, (every, seq), 1)
        sizes = cnt[...].astype(F32)
        start = jnp.sum(jnp.where(line < mine, sizes, 0.0), axis=1, keepdims=True)
        size = jnp.sum(jnp.where(line == mine, sizes, 0.0), axis=1, keepdims=True)
        letter = lax.broadcasted_iota(jnp.int32, (every, chars), 1).astype(F32)
        values = let[...].astype(F32)
        for slot in range(MAXC):
            alive_all[slot] = jnp.where(size > slot, 1.0, 0.0)
            alive[slot] = alive_all[slot, :own_rows]
            for way in range(2):
                if way == 0:
                    at = start + jnp.minimum(float(slot), size - 1.0)
                else:
                    at = start + jnp.maximum(size - 1.0 - slot, 0.0)
                found = jnp.sum(jnp.where(letter == at, values, 0.0), axis=1, keepdims=True)
                found = found.astype(jnp.int32)
                sym_all[way, slot * every : (slot + 1) * every, :] = found
                sym[way, slot * own_rows : (slot + 1) * own_rows, :] = found[:own_rows]

    return local_kernel(
        body,
        [
            shape((2, MAXC * every, 1), jnp.int32),
            shape((MAXC, every, 1), F32),
            shape((2, MAXC * own_rows, 1), jnp.int32),
            shape((MAXC, own_rows, 1), F32),
        ],
        (letters, counts),
    )


def encoder_forward(group, sym_all, alive_all, char_pack, hh_full, bias_full, table_lanes, own_rows, after=()):
    units = hh_full.shape[1]
    width = 3 * units
    lanes = table_lanes + 128
    embed = char_pack.shape[0]
    every = own_rows + HALO
    saved_shape = shape((2, MAXC, own_rows, units))

    def body(
        group_ref, sym_all, alive_all, pack, hh, bias,
        final, beside, emb, prev, rst, upd, car, fre,
        state, emb_all,
    ):
        for way in range(2):
            hits = one_hot(sym_all[way], group_ref[0], lanes, table_lanes)
            rows = product_nt(hits, pack[:, 2 * width :]).astype(BF)
            emb_all[way] = rows.reshape(MAXC, every, embed)
        emb[...] = emb_all[:, :, :own_rows]
        state[...] = jnp.zeros_like(state)

        @pl.loop(0, MAXC)
        def _(slot):
            live_col = alive_all[slot]
            for way in range(2):
                hidden = state[way]
                low = hidden.astype(BF)
                prev[way, slot] = low[:own_rows]
                gate = product(emb_all[way, slot], pack[:, way * width : (way + 1) * width])
                rec = product_nt(low, hh[way * width : (way + 1) * width])
                b_r = bias[way : way + 1, :units]
                b_z = bias[way : way + 1, units : 2 * units]
                b_n = bias[way : way + 1, 2 * units : 3 * units]
                b_c = bias[way : way + 1, 3 * units :]
                reset = sigmoid(gate[:, :units] + b_r + rec[:, :units])
                update = sigmoid(gate[:, units : 2 * units] + b_z + rec[:, units : 2 * units])
                carried = rec[:, 2 * units :] + b_c
                fresh = jnp.tanh(gate[:, 2 * units :] + b_n + reset * carried)
                rst[way, slot] = reset[:own_rows].astype(BF)
                upd[way, slot] = update[:own_rows].astype(BF)
                car[way, slot] = carried[:own_rows].astype(BF)
                fre[way, slot] = fresh[:own_rows].astype(BF)
                moved = (1.0 - update) * fresh + update * hidden
                state[way] = hidden + live_col * (moved - hidden)

        for way in range(2):
            low = state[way].astype(BF)
            final[:, way * units : (way + 1) * units] = low[:own_rows]
            beside[:, way * units : (way + 1) * units] = low[own_rows:]

    return local_kernel(
        body,
        [
            shape((own_rows, 2 * units)),
            shape((HALO, 2 * units)),
            shape((2, MAXC, own_rows, embed)),
        ]
        + [saved_shape] * 5,
        (group, sym_all, alive_all, char_pack, hh_full, bias_full),
        [
            pltpu.VMEM((2, every, units), F32),
            pltpu.VMEM((2, MAXC, every, embed), BF),
        ],
        limit=6,
        scalars=1, after=after)


def encoder_steps(grad_parts, hh_full, live, saved, after=()):
    own_rows = live.shape[1]
    units = hh_full.shape[1]
    width = 3 * units
    count = MAXC * own_rows
    pieces = len(grad_parts)

    def body(*refs):
        parts = refs[:pieces]
        hh, alive, prev, rst, upd, car, fre, low, inner_low, bias_grad, grad, sums = refs[pieces:]
        whole = parts[0][...].astype(F32)
        for part in parts[1:]:
            whole = whole + part[...].astype(F32)
        for way in range(2):
            grad[way] = whole[:, way * units : (way + 1) * units]
        sums[...] = jnp.zeros_like(sums)

        @pl.loop(0, MAXC)
        def _(step):
            slot = MAXC - 1 - step
            live_col = alive[slot]
            at = pl.ds(pl.multiple_of(slot * own_rows, 16), own_rows)
            for way in range(2):
                before = prev[way, slot].astype(F32)
                reset = rst[way, slot].astype(F32)
                update = upd[way, slot].astype(F32)
                carried = car[way, slot].astype(F32)
                fresh = fre[way, slot].astype(F32)
                g = grad[way]
                moved = live_col * g
                grad_fresh = moved * (1.0 - update)
                grad_update = moved * (before - fresh)
                grad_inner = grad_fresh * (1.0 - fresh * fresh)
                grad_carried = grad_inner * reset
                grad_reset = grad_carried * carried * (1.0 - reset)
                grad_z = grad_update * update * (1.0 - update)
                for part, what in enumerate((grad_reset, grad_z, grad_inner, grad_carried)):
                    sums[way, part] += jnp.sum(what.reshape(own_rows // 8, 8, units), 0)
                low[way, at, :units] = grad_reset.astype(BF)
                low[way, at, units : 2 * units] = grad_z.astype(BF)
                low[way, at, 2 * units :] = grad_carried.astype(BF)
                inner_low[way, at, :] = grad_inner.astype(BF)
                back = product(low[way, at, :], hh[way * width : (way + 1) * width])
                grad[way] = g - moved + moved * update + back

        for way in range(2):
            for part in range(4):
                bias_grad[way : way + 1, part * units : (part + 1) * units] = jnp.sum(
                    sums[way, part], 0, keepdims=True
                )

    return local_kernel(
        body,
        [
            shape((2, count, width)),
            shape((2, count, units)),
            shape((2, 4 * units), F32),
        ],
        (*grad_parts, hh_full, live, *saved),
        [pltpu.VMEM((2, own_rows, units), F32), pltpu.VMEM((2, 4, 8, units), F32)],
        limit=3, after=after)


def encoder_backward(
    group, split, steps_out, symbols, char_pack, embeds, previous, table_lanes, bias_cols, after=()
):
    low_all, inner_all, bias_all = steps_out
    units = inner_all.shape[2]
    width = 3 * units
    lanes = table_lanes + 128
    embed, wide = char_pack.shape
    count = low_all.shape[1]

    def body(*refs):
        group_ref = refs[0]
        sym, pack, low, inner_low, bias_grad, emb, prev = refs[1:8]
        results = refs[8 : 10 + (not split)]
        hh_grad = refs[10 + (not split)]
        if split:
            order8, order = Order("dp"), Order("mp")
            keep, send = results
            owners, depth = split
            strip = embed // owners
            steps = 2 * width // owners
            small = refs[-1]

        def pack_out(value, left):
            if not split:
                results[0][:, left : left + value.shape[1]] = value.astype(BF)
                return
            for b in range(owners):
                out = send if b % 2 else keep
                out[b // 2, 0, :, left : left + value.shape[1]] = value[
                    b * strip : (b + 1) * strip
                ].astype(BF)

        table_total = jnp.zeros((embed, lanes), F32)
        for way in range(2):
            rows = emb[way].reshape(count, embed)
            gates = low[way, :, : 2 * units]
            inner = inner_low[way]
            left = way * width
            pack_out(product_tn(rows, gates), left)
            pack_out(product_tn(rows, inner), left + 2 * units)
            embed_grad = product_nt(gates, pack[:, left : left + 2 * units]) + product_nt(
                inner, pack[:, left + 2 * units : left + width]
            )
            hits = one_hot(sym[way], group_ref[0], lanes, table_lanes)
            table_total = table_total + product_tn(embed_grad.astype(BF), hits)
            hh_grad[left : left + width] = product_tn(
                low[way], prev[way].reshape(count, units)
            ).astype(BF)
        if not split:
            pack_out(table_total, 2 * width)
            results[1][...] = hh_grad[...]
            results[2][...] = bias_grad[...]
            return
        pack_out(table_total[:, :table_lanes], 2 * width)
        small[...] = jnp.zeros_like(small)
        for k in range(owners * depth):
            small[k, :2, :bias_cols] = bias_grad[:, k * bias_cols : (k + 1) * bias_cols]
        lane = lax.broadcasted_iota(jnp.int32, (strip, 128), 1)
        for b in range(owners):
            out = send if b % 2 else keep
            mine = jnp.concatenate([small[order8[b] * depth + order[m]] for m in range(depth)], 0)
            last = table_total[b * strip : (b + 1) * strip, table_lanes:]
            out[b // 2, 0, :, wide - 128 :] = jnp.where(lane < GROUP_LANE, mine, last).astype(BF)
            for g in range(steps // strip):
                at = pl.ds(pl.multiple_of(order8[b] * steps + g * strip, 16), strip)
                out[b // 2, 1, :, g * units : (g + 1) * units] = hh_grad[at, :]

    outs = [shape(char_pack.shape), shape((2 * width, units)), shape((2, 4 * units), F32)]
    scratch = [pltpu.VMEM((2 * width, units), BF)]
    if split:
        owners, depth = split
        strip = embed // owners
        outs = [shape((owners // 2, 2, strip, wide))] * 2
        scratch.append(pltpu.VMEM((owners * depth, strip // depth, 128), F32))
    return local_kernel(
        body,
        outs,
        (group, symbols, char_pack, *steps_out, embeds, previous),
        scratch,
        limit=13.00,
        scalars=1, after=after)


def char_split_kernel(number, blocks, units, after=()):
    strip, wide = blocks[0].shape
    rows = strip // number
    groups = wide // units
    pieces = len(blocks)

    def body(*refs):
        order = Order("mp")
        outs, steps = refs[pieces : pieces + number], refs[pieces + number]
        total = refs[0][...].astype(F32) + refs[1][...].astype(F32)
        below = refs[2][...].astype(F32) + refs[3][...].astype(F32)
        for g in range(groups):
            steps[g * strip : (g + 1) * strip, :] = below[:, g * units : (g + 1) * units]
        for m, out in enumerate(outs):
            low = jnp.concatenate(
                [
                    steps[pl.ds(pl.multiple_of((order[m] * groups + g) * rows, 8), rows), :]
                    for g in range(groups)
                ],
                1,
            )
            out[...] = jnp.concatenate([total[m * rows : (m + 1) * rows], low], 0).astype(BF)

    return local_kernel(
        body,
        [shape((2 * rows, wide))] * number,
        tuple(blocks),
        [pltpu.VMEM((strip * groups, units), F32)],
        limit=2, after=after)


def per_device(
    tokens,
    char_ids,
    token_chars,
    groups,
    qkv_weight,
    out_weight,
    ffn_in,
    ffn_out,
    conv_weight,
    gains,
    ih_weight,
    hh_weight,
    gru_bias,
    char_table,
    group_table,
    token_cot,
    char_cot,
):
    dp_size, mp_size = lax.axis_size("dp"), lax.axis_size("mp")
    mp_index = lax.axis_index("mp")
    seq_len, model = tokens.shape
    local = out_weight.shape[0]
    heads = local // (model // HEADS)
    own_rows = seq_len // mp_size
    ih_rows, ih_cols = ih_weight.shape
    symbols_n, group_count = char_table.shape[0], group_table.shape[0]
    table_lanes = -(-symbols_n // 128) * 128
    misc_at = ih_cols + table_lanes
    units = hh_weight.shape[1]
    bias_cols, gain_cols = gru_bias.shape[1], gains.shape[1]
    both = ("dp", "mp")

    qkv_own = jnp.transpose(qkv_weight, (1, 0, 2))
    if quick():
        qkv_blocks = share_dp(qkv_own)
        qkv_full, packed, probs, attn_low, same, other = attention_kernel(
            tokens, qkv_blocks, heads
        )
        attn_blocks = pass_on([same, same, other, other])
        packs = share_mp(
            pack_kernel(
                ih_weight, hh_weight, gru_bias, char_table.T, group_table.T, out_weight.T, gains
            )
        )
        layer_own = pack_layer_kernel(
            ffn_in, ffn_out.T, conv_weight.T, held(s5=qkv_blocks[2:3])
        )
        layer_send = layer_own
        if "s4" in HOLDS:
            layer_send = stack_kernel([layer_own], packs[1:2])[0]
        layer_lists = share_dp_two(layer_own, swap(layer_send, "mp", 2))
        char_lists = share_dp_two(
            stack_kernel(packs[:2], held(s6=same, s7=attn_blocks[1:])),
            stack_kernel(packs[2:], held(s6=same, s1=attn_blocks[1:])),
        )
        out_full, gain_rows = unpack_out_kernel(
            char_lists, misc_at + 128, local, gains.shape
        )
        char_pack, hh_full, bias_full = unpack_char_kernel(
            char_lists, units, gru_bias.shape, misc_at
        )
        in_set, down_set, conv_set = unpack_layer_kernel(
            layer_lists, ffn_in.shape[0], held(s2=attn_blocks[1:])
        )
    else:
        qkv_blocks = [lax.all_gather(qkv_own, "dp", axis=1, tiled=True)]
        qkv_full, packed, probs, attn_low, same, other = attention_kernel(
            tokens, qkv_blocks, heads
        )
        attn_blocks = pass_on([same, same, other, other])
        vocab = jnp.pad(char_table.T, ((0, 0), (0, table_lanes - symbols_n)))
        misc = jnp.pad(group_table.T, ((0, 0), (GROUP_LANE, 128 - GROUP_LANE - group_count)))
        char_pack = lax.all_gather(
            jnp.concatenate([ih_weight, vocab, misc], 1), both, axis=0, tiled=True
        )
        hh_full = lax.all_gather(hh_weight, both, axis=0, tiled=True)
        bias_full = lax.all_gather(gru_bias, both, axis=1, tiled=True).astype(F32)
        gain_rows = lax.all_gather(gains, "dp", axis=1, tiled=True).astype(F32)
        out_full = lax.all_gather(
            lax.all_gather(out_weight.T, "dp", axis=0, tiled=True), "mp", axis=0
        )
        order = jnp.stack([mp_index ^ m for m in range(mp_size)]).astype(jnp.int32)
        out_full = jnp.take(out_full, order, axis=0)
        ffn_full = lax.all_gather(jnp.stack([ffn_in, ffn_out.T]), "dp", axis=1, tiled=True)
        ffn_full = jnp.stack([ffn_full, swap(ffn_full, "mp", 2)])
        in_set, down_set = ffn_full[:, 0], ffn_full[:, 1]
        conv_set = lax.all_gather(conv_weight, "dp", axis=0, tiled=True)
        conv_set = jnp.concatenate([conv_set, swap(conv_set, "mp", 2)], 1)
    conv_set = conv_set.reshape(3, 2 * model, 2 * local)

    sym_all, alive_all, symbols, live = symbols_kernel(char_ids, token_chars, own_rows)
    final, final_beside, embeds, *saved = encoder_forward(
        groups, sym_all, alive_all, char_pack, hh_full, bias_full, table_lanes, own_rows
    )
    char_blocks = [final, swap(final, "mp", 1), final_beside]

    low_half, hidden, hidden_slope, normal_one, scale_one, base, keep, send = middle_kernel(
        attn_blocks, tokens, out_full, gain_rows, in_set, down_set, held(s3=final)
    )
    normal_two, scale_two, two_low, two_beside = second_kernel(
        keep, swap(send, "mp", 1), base, gain_rows
    )
    token_blocks = [two_low, swap(two_low, "mp", 1), two_beside]

    mixed, joined_slope, sent = joining_kernel(token_blocks, char_blocks, conv_set)
    (
        token_half, char_half, quarter, own_token, own_char, pre_half, pre_grad, gain_three, gain_four,
        keep, send,
    ) = turn_kernel(
        sent, swap(sent, "mp", 1), mixed, token_cot, char_cot, gain_rows, joined_slope, conv_set
    )
    mixed_token = [keep, swap(send, "mp", 1)]
    keep, send = char_half_kernel(pre_half, conv_set)
    mixed_char = [keep, swap(send, "mp", 1)]
    quarter = swap(quarter, "mp", 2)
    if quick():
        conv_keep, conv_send = conv_split_kernel(mixed, pre_grad, dp_size, 2)
    else:
        conv_send = conv_grad_kernel(mixed, pre_grad)
    grad_second, second_low, gain_two = norm_back_kernel(
        mixed_token, own_token, normal_two, scale_two, gain_rows, 1, (), held(b1=conv_send)
    )
    steps_out = encoder_steps(
        [own_char] + mixed_char, hh_full, live, saved, held(b2=second_low)
    )
    backward = (steps_out, symbols, char_pack, embeds, saved[0], table_lanes, bias_cols)
    hold = held(b3=steps_out[2])
    if quick():
        conv_blocks = merge_two(conv_keep, conv_send)
        hold += held(b4=conv_blocks[0])
    second_half, grad_hidden, keep, send = feed_back_kernel(
        second_low, swap(second_low, "mp", 1), hidden_slope, in_set, down_set, hold
    )
    feed_args = (second_half, hidden, low_half, grad_hidden)
    hold = ()
    if quick():
        char_keep, char_send = encoder_backward(
            groups, (dp_size, mp_size), *backward, held(b5=second_half)
        )
        hold = held(b6=char_send)
        if "b7" not in HOLDS:
            feed_keep, feed_send = feed_split_kernel(*feed_args, dp_size, 2)
            hold += held(b26=feed_send)
    grad_first, first_low, _ = norm_back_kernel(
        [keep, swap(send, "mp", 1)], grad_second, normal_one, scale_one, gain_rows, 0,
        (gain_two, gain_three, gain_four), hold,
    )
    hold = held(b25=steps_out[2])
    if quick():
        if "b7" in HOLDS:
            feed_keep, feed_send = feed_split_kernel(*feed_args, dp_size, 2, (first_low,))
        char_parts = merge_two(char_keep, char_send, held(b8=first_low))
        conv_keep, conv_send = layer_sum_kernel(spread_two(conv_blocks), held(b9=first_low))
        hold += held(b10=feed_send, b11=char_parts[0], b12=conv_keep)
        if "b13" in HOLDS:
            feed_blocks = merge_two(feed_keep, feed_send)
            hold += (feed_blocks[0],)
    first_full, grad_packed, gain_grad, *token_parts = attention_back_kernel(
        share_mp(first_low), out_full, packed, probs, qkv_full, hold
    )
    token_out, char_out = outputs_kernel(
        token_half, char_half, quarter, swap(quarter, "mp", 1), held(b14=first_full)
    )
    token_parts = pass_on(token_parts)
    hold = ()
    if quick():
        if "b13" not in HOLDS:
            feed_blocks = merge_two(feed_keep, feed_send, held(b15=token_parts[1]))
        attn_keep, attn_send = qkv_split_kernel(
            tokens, grad_packed, first_full, attn_low, gain_grad, gains.shape[0], dp_size,
            held(b16=token_parts[1]),
        )
        hold = held(b17=feed_blocks[0], b18=attn_send)
        char_parts = spread_two(char_parts)
        if "b23" in HOLDS:
            char_parts = char_split_kernel(mp_size, char_parts, units)
            hold += (char_parts[0],)
        if "b27" in HOLDS:
            conv_grad = conv_final_kernel(conv_keep, swap(conv_send, "mp", 2))
            hold += (conv_grad,)
    token_own = sum_kernel(grad_first, token_parts, hold)
    token_blocks = share_mp(token_own)
    hold = ()
    if quick():
        attn_parts = merge_dp(attn_keep, attn_send, held(b19=token_own))
        if "b23" not in HOLDS:
            char_parts = char_split_kernel(mp_size, char_parts, units, held(b20=token_blocks[1]))
        if "b27" not in HOLDS:
            conv_grad = conv_final_kernel(conv_keep, swap(conv_send, "mp", 2))
        feed_keep, feed_send = layer_sum_kernel(spread_two(feed_blocks))
        hold = held(b21=char_parts[0], b22=attn_parts[0], b24=feed_keep)
    token_grad = widen_kernel(token_blocks, hold)

    group_at = misc_at + GROUP_LANE
    table_to = ih_cols + symbols_n
    gain_count = gains.shape[0]
    if quick():
        in_grad, down_grad = feed_final_kernel(feed_keep, swap(feed_send, "mp", 2))
        conv_grad = conv_grad.T
        qkv_grad, out_grad, gain_own = qkv_final_kernel(
            spread_dp(attn_parts),
            gains.shape,
        )
        ih_grad, table_grad, group_grad, bias_own, hh_own = char_final_kernel(
            pass_on(char_parts),
            (ih_cols, symbols_n, group_count, gru_bias.shape, hh_weight.shape),
        )
        table_grad, group_grad = table_grad.T, group_grad.T
    else:

        def spread(rows, axis):
            return lax.psum_scatter(rows.astype(F32), both, scatter_dimension=axis, tiled=True)

        attn_grads = qkv_grad_kernel(tokens, grad_packed, first_full, attn_low)
        attn_grads = lax.psum_scatter(
            attn_grads.astype(F32), "dp", scatter_dimension=1, tiled=True
        )
        qkv_grad, out_grad = attn_grads[:3], attn_grads[3].T
        feed_grad = feed_grad_kernel(*feed_args, 2).astype(F32)
        feed_grad = lax.psum_scatter(
            feed_grad[0] + swap(feed_grad[1], "mp", 2), "dp", scatter_dimension=1, tiled=True
        )
        in_grad, down_grad = feed_grad[0], feed_grad[1]
        conv_grad = conv_send.reshape(-1, 2 * local).astype(F32)
        conv_grad = conv_grad[:, :local] + swap(conv_grad[:, local:], "mp", 2)
        conv_grad = lax.psum_scatter(conv_grad, "dp", scatter_dimension=0, tiled=True)
        gain_own = lax.psum_scatter(
            gain_grad[:gain_count], "dp", scatter_dimension=1, tiled=True
        )
        pack_grad, hh_grad, bias_grad = encoder_backward(groups, None, *backward)
        ih_grad = spread(pack_grad[:, :ih_cols], 0)
        hh_own = spread(hh_grad, 0)
        table_grad = spread(pack_grad[:, ih_cols:table_to].T, 1)
        group_grad = spread(pack_grad[:, group_at : group_at + group_count].T, 1)
        bias_own = spread(bias_grad, 1)
    return (
        token_out,
        char_out,
        token_grad,
        jnp.transpose(qkv_grad, (1, 0, 2)),
        out_grad,
        in_grad,
        down_grad.T,
        conv_grad,
        gain_own,
        ih_grad,
        hh_own,
        bias_own,
        table_grad,
        group_grad,
    )


def solution(mesh):
    return jax.shard_map(
        per_device,
        mesh=mesh,
        in_specs=(
            P("dp", None),
            P("dp", None),
            P("dp", None),
            P("dp"),
            P("dp", None, "mp"),
            P("mp", "dp"),
            P("dp", "mp"),
            P("mp", "dp"),
            P("dp", "mp"),
            P(None, "dp"),
            P(("dp", "mp"), None),
            P(("dp", "mp"), None),
            P(None, ("dp", "mp")),
            P(None, ("dp", "mp")),
            P(None, ("dp", "mp")),
            P("dp", None),
            P("dp", None),
        ),
        out_specs=(
            P("dp", None),
            P("dp", None),
            P("dp", None),
            P("dp", None, "mp"),
            P("mp", "dp"),
            P("dp", "mp"),
            P("mp", "dp"),
            P("dp", "mp"),
            P(None, "dp"),
            P(("dp", "mp"), None),
            P(("dp", "mp"), None),
            P(None, ("dp", "mp")),
            P(None, ("dp", "mp")),
            P(None, ("dp", "mp")),
        ),
        check_vma=False,
    )
```

```python
import jax
import jax.numpy as jnp
from jax import lax
from jax.experimental import pallas as pl
from jax.experimental.pallas import tpu as pltpu
from jax.sharding import PartitionSpec as P

COST_SCALE = 4.0
COSTS = {"attention_kernel": 2.2, "middle_kernel": 3.6, "joining_kernel": 3.0, "turn_kernel": 2.6, "char_half_kernel": 0.8, "conv_split_kernel": 2.5, "feed_back_kernel": 1.5, "feed_split_kernel": 7.5, "encoder_forward": 11.0, "encoder_steps": 7.5, "encoder_backward": 5.5, "attention_back_kernel": 2.8, "qkv_split_kernel": 6.5}
HEADS = 12
MAXC = 8
NORM_EPS = 1e-05
BF = jnp.bfloat16
F32 = jnp.float32
GROUP_LANE = 96
HALO = 32
HOLDS = frozenset(["b1", "b16", "b21", "b22", "b26", "b4", "b6", "p1", "s2", "s5", "s6"])
ROUTES = "xyxy"
MB = 1 << 20


def dot(left, right, dims):
    return lax.dot_general(left, right, (dims, ((), ())), preferred_element_type=F32)


def product(left, right):
    return dot(left, right, ((1,), (0,)))


def product_tn(left, right):
    return dot(left, right, ((0,), (0,)))


def product_nt(left, right):
    return dot(left, right, ((1,), (1,)))


def swap(rows, axis, mask):
    size = lax.axis_size(axis)
    return lax.ppermute(rows, axis, [(i, i ^ mask) for i in range(size)])


def quick():
    return lax.axis_size("dp") == 8


def held(**arrays):
    found = []
    for name, array in arrays.items():
        if name in HOLDS:
            found += list(array) if isinstance(array, (list, tuple)) else [array]
    return tuple(found)


def take(blocks, index, axis=0):
    return lax.dynamic_index_in_dim(blocks, index, axis, keepdims=False)


def share_mp(block):
    return [block] + [swap(block, "mp", m) for m in range(1, lax.axis_size("mp"))]


def pass_on(blocks):
    return [blocks[0]] + [swap(blocks[m], "mp", m) for m in range(1, len(blocks))]


def share_dp(block, after=()):
    even = [block] + [swap(block, "dp", a) for a in range(2, lax.axis_size("dp"), 2)]
    if after:
        even[-1] = stack_kernel(even[-1:], after)[0]
    blocks = []
    for got in even:
        blocks += [got, swap(got, "dp", 1)]
    return blocks


def share_dp_by(block, route):
    if route == "d":
        return share_dp(block)
    near = 2 if route == "x" else 4
    far = 6 - near
    passed = swap(block, "dp", near)
    even = {0: block, near: passed, far: swap(block, "dp", far), 6: swap(passed, "dp", far)}
    blocks = []
    for a in range(0, 8, 2):
        blocks += [even[a], swap(even[a], "dp", 1)]
    return blocks


def merge_dp(keep, send, after=()):
    return merge_kernel(keep, swap(send, "dp", 1), after)


def spread_dp(blocks):
    return [blocks[0]] + [swap(block, "dp", 2 * i + 2) for i, block in enumerate(blocks[1:])]


def merge_two(keep, send, after=()):
    return merge_two_kernel(keep, swap(send, "dp", 1), after)


def spread_two(parts, after=()):
    first_keep, first_send, second_keep, second_send = parts
    first, first_next, second, second_next = relay_kernel(
        first_keep, swap(first_send, "dp", 4), second_keep, swap(second_send, "dp", 2), after
    )
    return [first, swap(first_next, "dp", 2), second, swap(second_next, "dp", 4)]


GELU_A = 0.7978845608028654
GELU_B = 0.044715


def gelu_both(v):
    t = jnp.tanh(GELU_A * (v + GELU_B * v * v * v))
    up = 0.5 * (1.0 + t)
    slope = up + 0.5 * v * (1.0 - t * t) * (GELU_A + 3.0 * GELU_A * GELU_B * v * v)
    return v * up, slope


def norm_parts(rows_in):
    row_mean = jnp.mean(rows_in, axis=-1, keepdims=True)
    centred = rows_in - row_mean
    spread = jnp.mean(centred * centred, axis=-1, keepdims=True)
    scale = lax.rsqrt(spread + NORM_EPS)
    return centred * scale, scale


def norm_back(normal, scale, gain_row, cotangent):
    lifted = cotangent * gain_row
    inner = jnp.mean(lifted * normal, axis=-1, keepdims=True)
    grad = scale * (lifted - jnp.mean(lifted, axis=-1, keepdims=True) - normal * inner)
    return grad, jnp.sum(cotangent * normal, axis=0, keepdims=True)


def shape(dims, dtype=BF):
    return jax.ShapeDtypeStruct(dims, dtype)


class Order:
    def __init__(self, axis):
        self.axis = axis

    def __getitem__(self, mask):
        return lax.axis_index(self.axis) ^ mask


class Spot:
    def __init__(self, seq):
        own = lax.axis_index("mp")
        top, pair = own >> 1, own & 1
        self.own, self.top, self.pair = own, top, pair
        self.window = top * (seq // 2 - HALO)
        self.half = top * HALO
        self.quarter = self.half + pair * (seq // 4)
        self.partner = self.half + (1 - pair) * (seq // 4)
        self.beside = (1 - top) * (seq // 2)
        self.in_half = pair * (seq // 4)
        self.partner_in_half = (1 - pair) * (seq // 4)
        self.beside_row = seq // 2 - HALO * top


def rows_at(ref, start, rows):
    return ref[pl.ds(pl.multiple_of(start, 16), rows), :]


def local_kernel(body, outs, args, scratch=(), limit=3.0, scalars=0, after=()):
    vmem = pl.BlockSpec(memory_space=pltpu.VMEM)
    smem = pl.BlockSpec(memory_space=pltpu.SMEM)
    idle = pl.BlockSpec(memory_space=pl.ANY)
    number, skip = len(args), len(after)

    def run(*refs):
        body(*refs[:number], *refs[number + skip :])

    return pl.pallas_call(
        run,
        out_shape=outs,
        in_specs=[smem] * scalars + [vmem] * (number - scalars) + [idle] * skip,
        out_specs=[vmem] * len(outs),
        scratch_shapes=list(scratch),
        compiler_params=pltpu.CompilerParams(vmem_limit_bytes=int((limit + 1.5) * MB)),
        name=body.__qualname__.split(".")[0],
        cost_estimate=pl.CostEstimate(
            flops=int(1e9 * COST_SCALE * COSTS.get(body.__qualname__.split(".")[0], 0.5)), bytes_accessed=0, transcendentals=0
        ),
    )(*args, *after)


def block_rows(ref, at, rows):
    return ref[pl.ds(pl.multiple_of(at * rows, 16), rows), :]


def spill(order, total, outs, rows):
    for m, out in enumerate(outs):
        out[...] = block_rows(total, order[m], rows).astype(BF)


def fill(order, blocks, full, rows):
    for m, block in enumerate(blocks):
        full[pl.ds(pl.multiple_of(order[m] * rows, 16), rows), :] = block[...]


def attention_kernel(tokens, blocks, heads):
    seq, model = tokens.shape
    number = len(blocks)
    _, rows, local = blocks[0].shape
    size = local // heads
    part = (seq // 2 + HALO) // 2

    def body(x, *refs):
        order = Order("dp")
        blk = refs[:number]
        w, packed, probs, attn, same, other = refs[number:]
        spot = Spot(seq)
        for i in range(3):
            for a in range(number):
                if number == 1:
                    w[i] = blk[a][i]
                else:
                    w[i, pl.ds(pl.multiple_of(order[a] * rows, 16), rows), :] = blk[a][i]
            packed[i] = product(x[...], w[i]).astype(BF)
        for h in range(heads):
            at = slice(h * size, (h + 1) * size)
            scores = product_nt(packed[0, :, at], packed[1, :, at]) * 0.125
            raised = jnp.exp(scores - jnp.max(scores, axis=-1, keepdims=True))
            total = jnp.sum(raised, axis=-1, keepdims=True)
            prob = (raised / total).astype(BF)
            probs[h] = prob
            attn[:, at] = product(prob, packed[2, :, at]).astype(BF)
        for out, start in ((same, spot.window), (other, seq // 2 - HALO - spot.window)):
            for top in range(2):
                at = pl.ds(pl.multiple_of(start + top * part, 16), part)
                out[:, top * local : (top + 1) * local] = attn[at, :]

    return local_kernel(
        body,
        [
            shape((3, model, local)),
            shape((3, seq, local)),
            shape((heads, seq, seq)),
            shape((seq, local)),
            shape((part, 2 * local)),
            shape((part, 2 * local)),
        ],
        (tokens, *blocks),
        limit=2,
    )


def middle_kernel(blocks, tokens, out_full, gain_rows, in_set, down_set, after=()):
    seq, model = tokens.shape
    number = len(blocks)
    local = out_full.shape[2]
    sets, _, hid = in_set.shape
    half, rows = seq // 2, seq // 4
    window, part = half + HALO, (half + HALO) // 2

    def body(*refs):
        spot = Spot(seq)
        blk = refs[:number]
        x, wo, g, wi, wd = refs[number : number + 5]
        low_half, hidden_half, slope_half, normal_own, scale_own, base, keep, send = refs[
            number + 5 : number + 13
        ]
        total, scales, low, hidden, slope = refs[number + 13 :]
        for top in range(2):
            at = slice(top * part, (top + 1) * part)
            lanes = slice(top * local, (top + 1) * local)
            acc = rows_at(x, spot.window + top * part, part).astype(F32)
            for m in range(number):
                acc = acc + product_nt(blk[m][:, lanes], wo[m])
            normal, scale = norm_parts(acc)
            total[at] = normal
            scales[at] = scale
            low[at] = (normal * g[0:1]).astype(BF)
        low_half[...] = rows_at(low, spot.half, half)
        normal_own[...] = rows_at(total, spot.quarter, rows)
        scale_own[...] = rows_at(scales, spot.quarter, rows)
        base[:rows] = normal_own[...] * g[0:1]
        base[rows:] = rows_at(total, spot.beside, HALO) * g[0:1]
        for s in range(sets):
            at = slice(s * hid, (s + 1) * hid)
            value, steep = gelu_both(product(low[...], wi[s]))
            hidden[:, at] = value.astype(BF)
            slope[:, at] = steep.astype(BF)
        hidden_half[...] = rows_at(hidden, spot.half, half)
        slope_half[...] = rows_at(slope, spot.half, half)
        whole = product_nt(hidden[:, :hid], wd[0])
        for s in range(1, sets):
            whole = whole + product_nt(hidden[:, s * hid : (s + 1) * hid], wd[s])
        total[...] = whole
        beside = rows_at(total, spot.beside, HALO).astype(BF)
        for out, start in ((keep, spot.quarter), (send, spot.partner)):
            out[:rows] = rows_at(total, start, rows).astype(BF)
            out[rows:] = beside

    return local_kernel(
        body,
        [
            shape((half, model)),
            shape((half, sets * hid)),
            shape((half, sets * hid)),
            shape((rows, model), F32),
            shape((rows, 1), F32),
            shape((rows + HALO, model), F32),
            shape((rows + HALO, model)),
            shape((rows + HALO, model)),
        ],
        (*blocks, tokens, out_full, gain_rows, in_set, down_set),
        [
            pltpu.VMEM((window, model), F32),
            pltpu.VMEM((window, 1), F32),
            pltpu.VMEM((window, model), BF),
            pltpu.VMEM((window, sets * hid), BF),
            pltpu.VMEM((window, sets * hid), BF),
        ],
        limit=6, after=after)


def second_kernel(keep, got, base, gain_rows):
    high, model = base.shape
    rows = high - HALO

    def body(keep, got, base, g, normal, scale, low, beside):
        xh, r = norm_parts(base[...] + keep[...].astype(F32) + got[...].astype(F32))
        normal[...] = xh[:rows]
        scale[...] = r[:rows]
        out = (xh * g[1:2]).astype(BF)
        low[...] = out[:rows]
        beside[...] = out[rows:]

    return local_kernel(
        body,
        [
            shape((rows, model), F32),
            shape((rows, 1), F32),
            shape((rows, model)),
            shape((HALO, model)),
        ],
        (keep, got, base, gain_rows),
    )


def joining_kernel(token_blocks, char_blocks, conv_set):
    rows, model = token_blocks[0].shape
    seq = 4 * rows
    half = seq // 2
    window = half + HALO
    local = conv_set.shape[2]

    def body(*refs):
        spot = Spot(seq)
        conv, mixed, slope, sent = refs[6:]
        places = ((spot.quarter, rows), (spot.partner, rows), (spot.beside, HALO))
        for i, (start, count) in enumerate(places):
            at = pl.ds(pl.multiple_of(start, 16), count)
            mixed[at, :model] = refs[i][...]
            mixed[at, model:] = refs[3 + i][...]
        line = lax.broadcasted_iota(jnp.int32, (window, 1), 0)
        before = pltpu.roll(product(mixed[...], conv[0]), 1, 0)
        after = pltpu.roll(product(mixed[...], conv[2]), window - 1, 0)
        pre = product(mixed[...], conv[1])
        pre = pre + jnp.where(line == 0, 0.0, before) + jnp.where(line == window - 1, 0.0, after)
        value, steep = gelu_both(pre)
        slope[...] = steep.astype(BF)
        sent[...] = value.astype(BF)

    return local_kernel(
        body,
        [shape((window, 2 * model)), shape((window, local)), shape((window, local))],
        (*token_blocks, *char_blocks, conv_set),
        limit=3,
    )


def turn_kernel(joined_own, joined_got, mixed, token_cot, char_cot, gain_rows, slope, conv_set):
    seq, model = token_cot.shape
    half, rows = seq // 2, seq // 4
    window, local = joined_own.shape
    one = local // 2

    def body(
        mine, got, mix, cot_t, cot_c, g, steep, conv,
        token_half, char_half, quarter, own_t, own_c, pre_half, pre_grad, gain_t, gain_c, keep, send,
        stack, joined, total, picked, outs, pre3, parts,
    ):
        spot = Spot(seq)
        order = Order("mp")
        for m, (ref, lane) in enumerate(((mine, 0), (got, 0), (mine, one), (got, one))):
            stack[order[m]] = ref[:, lane : lane + one]
        for j in range(4):
            joined[:, j * one : (j + 1) * one] = stack[j]
        both = joined[...].astype(F32)
        line = lax.broadcasted_iota(jnp.int32, (window, 1), 0)
        is_own = (line >= spot.quarter) & (line < spot.quarter + rows)
        grad_sum = None
        for lane, cot_ref, out, own, gain, row in (
            (0, cot_t, token_half, own_t, gain_t, 2),
            (model, cot_c, char_half, own_c, gain_c, 3),
        ):
            xh, r = norm_parts(mix[:, lane : lane + model].astype(F32) + both)
            outs[...] = (xh * g[row : row + 1]).astype(BF)
            out[...] = rows_at(outs, spot.half, half)
            quarter[row - 2] = rows_at(outs, spot.quarter, rows)
            cot = rows_at(cot_ref, spot.window, window).astype(F32)
            grad, _ = norm_back(xh, r, g[row : row + 1], cot)
            gain[...] = jnp.sum(jnp.where(is_own, cot * xh, 0.0), axis=0, keepdims=True)
            total[...] = grad
            own[...] = rows_at(total, spot.quarter, rows)
            grad_sum = grad if grad_sum is None else grad_sum + grad
        for j in range(4):

            @pl.when(spot.own == j)
            def _():
                picked[:, :one] = grad_sum[:, j * one : (j + 1) * one]
                picked[:, one:] = grad_sum[:, (j ^ 2) * one : ((j ^ 2) + 1) * one]

        grad = (picked[...] * steep[...].astype(F32)).astype(BF).astype(F32)

        def fan(rows_in, out):
            out[0] = jnp.where(line == window - 1, 0.0, pltpu.roll(rows_in, window - 1, 0)).astype(BF)
            out[1] = rows_in.astype(BF)
            out[2] = jnp.where(line == 0, 0.0, pltpu.roll(rows_in, 1, 0)).astype(BF)

        fan(grad, pre3)
        at = pl.ds(pl.multiple_of(spot.half, 16), half)
        for k in range(3):
            pre_half[k] = pre3[k, at, :]
        is_half = (line >= spot.half) & (line < spot.half + half)
        fan(jnp.where(is_half, grad, 0.0), pre_grad)
        parts[...] = (
            product_nt(pre_half[0], conv[0, :model])
            + product_nt(pre_half[1], conv[1, :model])
            + product_nt(pre_half[2], conv[2, :model])
        )
        keep[...] = rows_at(parts, spot.in_half, rows).astype(BF)
        send[...] = rows_at(parts, spot.partner_in_half, rows).astype(BF)

    return local_kernel(
        body,
        [shape((half, model))] * 2
        + [shape((2, rows, model))]
        + [shape((rows, model), F32)] * 2
        + [shape((3, half, local)), shape((3, window, local))]
        + [shape((1, model), F32)] * 2
        + [shape((rows, model))] * 2,
        (joined_own, joined_got, mixed, token_cot, char_cot, gain_rows, slope, conv_set),
        [
            pltpu.VMEM((4, window, one), BF),
            pltpu.VMEM((window, model), BF),
            pltpu.VMEM((window, model), F32),
            pltpu.VMEM((window, local), F32),
            pltpu.VMEM((window, model), BF),
            pltpu.VMEM((3, window, local), BF),
            pltpu.VMEM((half, model), F32),
        ],
        limit=8,
    )


def char_half_kernel(pre_half, conv_set, after=()):
    _, half, _ = pre_half.shape
    model = conv_set.shape[1] // 2
    rows = half // 2

    def body(pre, conv, keep, send, parts):
        spot = Spot(2 * half)
        parts[...] = (
            product_nt(pre[0], conv[0, model:])
            + product_nt(pre[1], conv[1, model:])
            + product_nt(pre[2], conv[2, model:])
        )
        keep[...] = rows_at(parts, spot.in_half, rows).astype(BF)
        send[...] = rows_at(parts, spot.partner_in_half, rows).astype(BF)

    return local_kernel(
        body,
        [shape((rows, model))] * 2,
        (pre_half, conv_set),
        [pltpu.VMEM((half, model), F32)], after=after)


def conv_grad_kernel(mixed, pre_grad):
    local = pre_grad.shape[2]
    wide = mixed.shape[1]

    def body(mix, pre, grad):
        for k in range(3):
            grad[k] = product_tn(mix[...], pre[k]).astype(BF)

    return local_kernel(body, [shape((3, wide, local))], (mixed, pre_grad), limit=3)[0]


def conv_split_kernel(mixed, pre_grad, owners, sets, after=()):
    taps, _, both = pre_grad.shape
    wide = mixed.shape[1]
    local = both // sets
    rows = taps * wide // owners
    part = rows // 2

    def body(mix, pre, keep, send, whole):
        order = Order("dp")
        for k in range(taps):
            whole[k * wide : (k + 1) * wide] = product_tn(mix[...], pre[k]).astype(BF)
        for b in range(owners):
            out = send if b % 2 else keep
            for h in range(2):
                at = pl.ds(pl.multiple_of(order[b] * rows + h * part, 16), part)
                for s in range(sets):
                    out[b // 2, s, :, h * local : (h + 1) * local] = whole[
                        at, s * local : (s + 1) * local
                    ]

    return local_kernel(
        body,
        [shape((owners // 2, sets, part, 2 * local))] * 2,
        (mixed, pre_grad),
        [pltpu.VMEM((taps * wide, both), BF)],
        limit=7, after=after)


def outputs_kernel(token_half, char_half, got, passed, after=()):
    half, model = token_half.shape
    rows = half // 2

    def body(token_half, char_half, got, passed, token_out, char_out):
        spot = Spot(2 * half)
        mine = pl.ds(pl.multiple_of(spot.top * half, 16), half)
        other = (1 - spot.top) * half
        for i, (own, out) in enumerate(((token_half, token_out), (char_half, char_out))):
            out[mine, :] = own[...]
            for ref, start in ((got, spot.in_half), (passed, spot.partner_in_half)):
                out[pl.ds(pl.multiple_of(other + start, 16), rows), :] = ref[i]

    return local_kernel(
        body, [shape((2 * half, model))] * 2, (token_half, char_half, got, passed), after=after)


def norm_back_kernel(parts, residual, normal, scale, gain_rows, row, gain_parts=(), after=()):
    rows, model = residual.shape
    number = len(parts)
    extra = len(gain_parts)

    def body(*refs):
        res, xh, r, g = refs[number : number + 4]
        others = refs[number + 4 : number + 4 + extra]
        grad, low, gain = refs[number + 4 + extra :]
        total = res[...]
        for part in refs[:number]:
            total = total + part[...].astype(F32)
        out, own = norm_back(xh[...], r[...], g[row : row + 1], total)
        gain[...] = own
        grad[...] = out
        low[:rows] = out.astype(BF)
        if extra:
            line = lax.broadcasted_iota(jnp.int32, (16, model), 0)
            tail = jnp.where(line == 0, own, 0.0)
            for i, other in enumerate(others):
                tail = jnp.where(line == i + 1, other[...], tail)
            low[rows:] = tail.astype(BF)

    return local_kernel(
        body,
        [
            shape((rows, model), F32),
            shape((rows + (16 if extra else 0), model)),
            shape((1, model), F32),
        ],
        (*parts, residual, normal, scale, gain_rows, *gain_parts),
        limit=1, after=after)


def feed_back_kernel(second_own, second_got, slope, in_set, down_set, after=()):
    rows, model = second_own.shape
    half = 2 * rows
    sets, _, hid = in_set.shape

    def body(mine, got, steep, wi, wd, full, grad, keep, send, parts):
        spot = Spot(2 * half)
        full[pl.ds(pl.multiple_of(spot.in_half, 16), rows), :] = mine[...]
        full[pl.ds(pl.multiple_of(spot.partner_in_half, 16), rows), :] = got[...]
        total = None
        for s in range(sets):
            at = slice(s * hid, (s + 1) * hid)
            grad[:, at] = (product(full[...], wd[s]) * steep[:, at].astype(F32)).astype(BF)
            part = product_nt(grad[:, at], wi[s])
            total = part if total is None else total + part
        parts[...] = total
        keep[...] = rows_at(parts, spot.in_half, rows).astype(BF)
        send[...] = rows_at(parts, spot.partner_in_half, rows).astype(BF)

    return local_kernel(
        body,
        [shape((half, model)), shape((half, sets * hid))] + [shape((rows, model))] * 2,
        (second_own, second_got, slope, in_set, down_set),
        [pltpu.VMEM((half, model), F32)],
        limit=3, after=after)


def feed_grad_kernel(second_half, hidden, low_half, grad_hidden, sets):
    model = second_half.shape[1]
    hid = hidden.shape[1] // sets

    def body(second, hide, low, grad, out):
        for s in range(sets):
            at = slice(s * hid, (s + 1) * hid)
            out[s, 0] = product_tn(low[...], grad[:, at]).astype(BF)
            out[s, 1] = product_tn(second[...], hide[:, at]).astype(BF)

    return local_kernel(
        body,
        [shape((sets, 2, model, hid))],
        (second_half, hidden, low_half, grad_hidden),
        limit=3,
    )[0]


def feed_split_kernel(second_half, hidden, low_half, grad_hidden, owners, sets, after=()):
    model = second_half.shape[1]
    hid = hidden.shape[1] // sets
    rows = model // owners
    half = hid // 2

    def body(second, hide, low, grad, keep, send, whole):
        order = Order("dp")
        for s in range(sets):
            lanes = slice(s * hid, (s + 1) * hid)
            whole[:model] = product_tn(low[...], grad[:, lanes]).astype(BF)
            whole[model:] = product_tn(second[...], hide[:, lanes]).astype(BF)
            for b in range(owners):
                out = send if b % 2 else keep
                for i in range(2):
                    at = pl.ds(pl.multiple_of(i * model + order[b] * rows, 16), rows)
                    for h in range(2):
                        to = (2 * i + h) * rows
                        out[b // 2, s, to : to + rows, :] = whole[at, h * half : (h + 1) * half]

    return local_kernel(
        body,
        [shape((owners // 2, sets, 4 * rows, half))] * 2,
        (second_half, hidden, low_half, grad_hidden),
        [pltpu.VMEM((2 * model, hid), BF)],
        limit=6, after=after)


def layer_sum_kernel(parts, after=()):
    dims = parts[0].shape

    def body(*refs):
        keep, send = refs[4:]
        keep[...] = refs[0][...].astype(F32) + refs[1][...].astype(F32)
        send[...] = (refs[2][...].astype(F32) + refs[3][...].astype(F32)).astype(BF)

    return local_kernel(body, [shape(dims, F32), shape(dims)], tuple(parts), after=after)


def feed_final_kernel(keep, got):
    high, half = keep.shape
    rows = high // 4

    def body(keep, got, grad_in, grad_down):
        total = keep[...] + got[...].astype(F32)
        for i, out in enumerate((grad_in, grad_down)):
            for h in range(2):
                at = (2 * i + h) * rows
                out[:, h * half : (h + 1) * half] = total[at : at + rows]

    return local_kernel(body, [shape((rows, 2 * half), F32)] * 2, (keep, got), limit=3)


def conv_final_kernel(keep, got, after=()):
    part, wide = keep.shape
    local = wide // 2

    def body(keep, got, grad):
        total = keep[...] + got[...].astype(F32)
        for h in range(2):
            grad[:, h * part : (h + 1) * part] = total[:, h * local : (h + 1) * local].T

    return local_kernel(body, [shape((local, 2 * part), F32)], (keep, got), limit=3, after=after)[0]


def attention_back_kernel(blocks, out_own, packed, probs, weights, after=()):
    number = len(blocks)
    high, model = blocks[0].shape
    rows = high - 16
    seq = number * rows
    heads = probs.shape[0]
    local = packed.shape[2]
    size = local // heads

    def body(*refs):
        order = Order("mp")
        blk = refs[:number]
        wo, pack, prob, w, full, grads, gains = refs[number : number + 7]
        outs = refs[number + 7 : 2 * number + 7]
        total, grad_attn = refs[2 * number + 7 :]
        sums = jnp.zeros((16, model), F32)
        for m in range(number):
            full[pl.ds(pl.multiple_of(order[m] * rows, 16), rows), :] = blk[m][:rows]
            sums = sums + blk[m][rows:].astype(F32)
        gains[...] = sums
        grad_attn[...] = product(full[...], wo[0]).astype(BF)
        for h in range(heads):
            at = slice(h * size, (h + 1) * size)
            p = prob[h].astype(F32)
            grad_probs = product_nt(grad_attn[:, at], pack[2, :, at])
            inner = jnp.sum(grad_probs * p, axis=-1, keepdims=True)
            scores = (p * (grad_probs - inner)).astype(BF)
            grads[0, :, at] = (product(scores, pack[1, :, at]) * 0.125).astype(BF)
            grads[1, :, at] = (product_tn(scores, pack[0, :, at]) * 0.125).astype(BF)
            grads[2, :, at] = product_tn(prob[h], grad_attn[:, at]).astype(BF)
        total[...] = (
            product_nt(grads[0], w[0]) + product_nt(grads[1], w[1]) + product_nt(grads[2], w[2])
        )
        spill(order, total, outs, rows)

    return local_kernel(
        body,
        [shape((seq, model)), shape((3, seq, local)), shape((16, model), F32)]
        + [shape((rows, model))] * number,
        (*blocks, out_own, packed, probs, weights),
        [pltpu.VMEM((seq, model), F32), pltpu.VMEM((seq, local), BF)],
        limit=3, after=after)


def qkv_grad_kernel(tokens, grads, first_low, attn):
    model = tokens.shape[1]
    local = attn.shape[1]

    def body(x, g, first, a, out):
        for i in range(3):
            out[i] = product_tn(x[...], g[i]).astype(BF)
        out[3] = product_tn(first[...], a[...]).astype(BF)

    return local_kernel(
        body,
        [shape((4, model, local))],
        (tokens, grads, first_low, attn),
        limit=2,
        scalars=0,
    )[0]


def qkv_split_kernel(tokens, grads, first_low, attn, gains, gain_count, owners, after=()):
    model = tokens.shape[1]
    local = attn.shape[1]
    rows = model // owners

    def body(x, g, first, a, gain, keep, send, whole, small):
        order = Order("dp")
        for i in range(3):
            whole[i] = product_tn(x[...], g[i]).astype(BF)
        whole[3] = product_tn(first[...], a[...]).astype(BF)
        small[...] = jnp.zeros_like(small)
        for d in range(owners):
            small[d, :gain_count, :rows] = gain[:gain_count, d * rows : (d + 1) * rows]
        for b in range(owners):
            out = send if b % 2 else keep
            at = pl.ds(pl.multiple_of(order[b] * rows, 16), rows)
            for i in range(4):
                to, lane = i // 2 * rows, i % 2 * local
                out[b // 2, to : to + rows, lane : lane + local] = whole[i, at, :]
            out[b // 2, 2 * rows :, :] = small[order[b]].astype(BF)

    return local_kernel(
        body,
        [shape((owners // 2, 2 * rows + 16, 2 * local))] * 2,
        (tokens, grads, first_low, attn, gains),
        [pltpu.VMEM((4, model, local), BF), pltpu.VMEM((owners, 16, 2 * local), F32)],
        limit=4, after=after)


def qkv_final_kernel(blocks, gain_shape):
    high, wide = blocks[0].shape
    rows, local = (high - 16) // 2, wide // 2
    number = len(blocks)
    gain_count, gain_cols = gain_shape

    def body(*refs):
        qkv, out, gain = refs[number:]
        total = refs[0][...].astype(F32)
        for ref in refs[1:number]:
            total = total + ref[...].astype(F32)
        qkv[0] = total[:rows, :local]
        qkv[1] = total[:rows, local:]
        qkv[2] = total[rows : 2 * rows, :local]
        out[...] = total[rows : 2 * rows, local:].T
        gain[...] = total[2 * rows : 2 * rows + gain_count, :gain_cols]

    return local_kernel(
        body,
        [shape((3, rows, local), F32), shape((local, rows), F32), shape(gain_shape, F32)],
        tuple(blocks),
        limit=3,
    )


def char_final_kernel(blocks, shapes):
    high, wide = blocks[0].shape
    rows = high // 2
    number = len(blocks)
    ih_cols, symbols, groups, bias_shape, hh_shape = shapes
    misc = wide - 128
    units = hh_shape[1]

    def body(*refs):
        ih, table, group, bias, hh = refs[number:]
        total = refs[0][...].astype(F32)
        for ref in refs[1:number]:
            total = total + ref[...].astype(F32)
        ih[...] = total[:rows, :ih_cols]
        table[...] = total[:rows, ih_cols : ih_cols + symbols]
        last = total[:rows, misc:]
        group[...] = last[:, GROUP_LANE : GROUP_LANE + groups]
        bias[...] = last[: bias_shape[0], : bias_shape[1]]
        for g in range(hh_shape[0] // rows):
            hh[g * rows : (g + 1) * rows, :] = total[rows:, g * units : (g + 1) * units]

    return local_kernel(
        body,
        [
            shape((rows, ih_cols), F32),
            shape((rows, symbols), F32),
            shape((rows, groups), F32),
            shape(bias_shape, F32),
            shape(hh_shape, F32),
        ],
        tuple(blocks),
    )


def sum_kernel(residual, parts, after=()):
    number = len(parts)

    def body(*refs):
        total = refs[0][...]
        for ref in refs[1 : number + 1]:
            total = total + ref[...].astype(F32)
        refs[number + 1][...] = total.astype(BF)

    return local_kernel(body, [shape(residual.shape)], (residual, *parts), after=after)[0]


def stack_kernel(blocks, after=()):
    number = len(blocks)

    def body(*refs):
        for i in range(number):
            refs[number][i] = refs[i][...]

    return local_kernel(body, [shape((number,) + blocks[0].shape)], tuple(blocks), after=after)[0]


def merge_kernel(keep, got, after=()):
    number = keep.shape[0]
    dims = keep.shape[1:]

    def body(keep, got, *outs):
        for i, out in enumerate(outs):
            out[...] = (keep[i].astype(F32) + got[i].astype(F32)).astype(BF)

    return local_kernel(body, [shape(dims)] * number, (keep, got), limit=4, after=after)


def merge_two_kernel(keep, got, after=()):
    dims = keep.shape[2:]

    def body(keep, got, *outs):
        for out, half, picks in zip(outs, (0, 0, 1, 1), ((0, 1), (2, 3), (0, 2), (1, 3))):
            for at, i in enumerate(picks):
                out[at] = (keep[i, half].astype(F32) + got[i, half].astype(F32)).astype(BF)

    return local_kernel(
        body, [shape((2,) + dims)] * 4, (keep, got), limit=4, after=after
    )


def relay_kernel(first_keep, first_got, second_keep, second_got, after=()):
    dims = first_keep.shape[1:]

    def body(first_keep, first_got, second_keep, second_got, *outs):
        for i, (keep, got) in enumerate(((first_keep, first_got), (second_keep, second_got))):
            for at in range(2):
                total = keep[at].astype(F32) + got[at].astype(F32)
                outs[2 * i + at][...] = total.astype(BF)

    return local_kernel(
        body,
        [shape(dims)] * 4,
        (first_keep, first_got, second_keep, second_got),
        after=after,
    )


def pack_kernel(ih, hh, bias, table, group, out, gains):
    rows, ih_cols = ih.shape
    hh_rows, units = hh.shape
    symbols, groups = table.shape[1], group.shape[1]
    lanes = -(-symbols // 128) * 128
    misc = ih_cols + lanes
    wide = misc + 128
    half, local = out.shape[0] // 2, out.shape[1]

    args = (ih, hh, bias, table, group, out, gains)

    def body(*refs):
        copies = [
            pltpu.make_async_copy(refs[i], refs[10 + i], refs[17].at[i]) for i in range(7)
        ]
        for copy in copies:
            copy.start()
        pack, top, low = refs[7:10]
        ih, hh, bias, table, group, out, gains = refs[10:17]
        top[...] = jnp.zeros_like(top)
        low[...] = jnp.zeros_like(low)
        for copy in copies:
            copy.wait()
        top[:rows, :ih_cols] = ih[...].astype(F32)
        top[:rows, ih_cols : ih_cols + symbols] = table[...].astype(F32)
        top[: bias.shape[0], misc : misc + bias.shape[1]] = bias[...].astype(F32)
        top[:rows, misc + GROUP_LANE : misc + GROUP_LANE + groups] = group[...].astype(F32)
        steps = hh[...].astype(F32)
        for g in range(hh_rows // rows):
            top[rows:, g * units : (g + 1) * units] = steps[g * rows : (g + 1) * rows]
        pack[:, :wide] = top[...].astype(BF)
        low[:half, :local] = out[:half].astype(F32)
        low[:half, local:] = out[half:].astype(F32)
        low[half : half + gains.shape[0], : gains.shape[1]] = gains[...].astype(F32)
        for g in range((half + 16) // 16):
            at = wide + g * 2 * local
            pack[:, at : at + 2 * local] = low[g * 16 : (g + 1) * 16].astype(BF)

    vmem = pl.BlockSpec(memory_space=pltpu.VMEM)
    return pl.pallas_call(
        body,
        out_shape=shape((2 * rows, wide + (half + 16) // 16 * 2 * local)),
        in_specs=[pl.BlockSpec(memory_space=pltpu.HBM)] * 7,
        out_specs=vmem,
        scratch_shapes=[pltpu.VMEM((2 * rows, wide), F32), pltpu.VMEM((half + 16, 2 * local), F32)]
        + [pltpu.VMEM(arg.shape, BF) for arg in args]
        + [pltpu.SemaphoreType.DMA((7,))],
        compiler_params=pltpu.CompilerParams(vmem_limit_bytes=5 * MB),
        name="pack_kernel",
    )(*args)


def pack_layer_kernel(ffn_in, ffn_down, conv, after):
    rows, hid = ffn_in.shape
    local, taps = conv.shape
    half, part = hid // 2, taps // 2

    def body(wi, wd, conv, out):
        for i, ref in enumerate((wi, wd)):
            for h in range(2):
                at = (2 * i + h) * rows
                out[at : at + rows, :] = ref[:, h * half : (h + 1) * half]
        both = conv[...].astype(F32).T.astype(BF)
        for h in range(2):
            out[4 * rows :, h * local : (h + 1) * local] = both[h * part : (h + 1) * part]

    return local_kernel(
        body,
        [shape((4 * rows + part, half))],
        (ffn_in, ffn_down, conv),
        limit=3,
        after=after,
    )[0]


def unpack_layer_kernel(lists, rows, after=()):
    sets, number = len(lists), len(lists[0])
    high, half = lists[0][0].shape
    part = high - 4 * rows
    local = half // 2

    def body(*refs):
        order = Order("dp")
        outs, conv = refs[sets * number : sets * number + 2], refs[sets * number + 2]
        for a in range(number):
            at = pl.ds(pl.multiple_of(order[a] * rows, 16), rows)
            for s in range(sets):
                ref = refs[s * number + a]
                for i in range(2):
                    for h in range(2):
                        to = (2 * i + h) * rows
                        outs[i][s, at, h * half : (h + 1) * half] = ref[to : to + rows, :]
                for h in range(2):
                    to = pl.ds(pl.multiple_of((order[a] * 2 + h) * part, 16), part)
                    conv[to, s * local : (s + 1) * local] = ref[
                        4 * rows :, h * local : (h + 1) * local
                    ]

    return local_kernel(
        body,
        [shape((sets, number * rows, 2 * half))] * 2
        + [shape((number * 2 * part, sets * local))],
        tuple(lists[0]) + tuple(lists[1]), after=after)


def unpack_out_kernel(lists, start, local, gain_shape):
    number = len(lists[0])
    each, high, _ = lists[0][0].shape
    depth = 2 * each
    gain_count, gain_cols = gain_shape
    rows = gain_cols
    half = rows // 2

    def body(*refs):
        order = Order("dp")
        out, gain, stack = refs[2 * number :]
        for a in range(number):
            for m in range(depth):
                ref = refs[m // each * number + a]
                for g in range(half // 16):
                    for h in range(2):
                        at = pl.ds(
                            pl.multiple_of(order[a] * rows + h * half + g * 16, 16), 16
                        )
                        lane = start + (2 * g + h) * local
                        out[m, at, :] = ref[m % each, :, lane : lane + local]
            stack[order[a]] = refs[a][0, :, start + half // 16 * 2 * local :].astype(F32)
        for d in range(number):
            gain[:, d * gain_cols : (d + 1) * gain_cols] = stack[d, :gain_count, :gain_cols]

    return local_kernel(
        body,
        [shape((depth, number * rows, local)), shape((gain_count, number * gain_cols), F32)],
        tuple(lists[0]) + tuple(lists[1]),
        [pltpu.VMEM((number, 16, 2 * local), F32)],
    )


def unpack_char_kernel(lists, units, bias_shape, misc):
    number = len(lists[0])
    each, high, _ = lists[0][0].shape
    wide = misc + 128
    depth = 2 * each
    rows = high // 2
    groups = wide // units
    ways, bias_cols = bias_shape
    total = number * depth

    def body(*refs):
        order8, order = Order("dp"), Order("mp")
        pack, hh, bias, steps, small = refs[2 * number :]
        for a in range(number):
            for m in range(depth):
                whole = refs[m // each * number + a][m % each, :, :wide].astype(F32)
                at = (a * depth + m) * rows
                if m % 2 == 0:
                    before = whole[:rows]
                else:
                    pack[at - rows : at + rows, :] = jnp.concatenate(
                        [before, whole[:rows]], 0
                    ).astype(BF)
                place = order8[a] * depth + order[m]
                small[place] = whole[:rows, misc:]
                steps[place] = jnp.concatenate(
                    [whole[rows:, g * units : (g + 1) * units] for g in range(groups)], 0
                )
        hh[...] = steps[...].reshape(total * groups * rows, units).astype(BF)
        for k in range(total):
            bias[:, k * bias_cols : (k + 1) * bias_cols] = small[k, :ways, :bias_cols]

    return local_kernel(
        body,
        [
            shape((total * rows, wide)),
            shape((total * groups * rows, units)),
            shape((ways, total * bias_cols), F32),
        ],
        tuple(lists[0]) + tuple(lists[1]),
        [
            pltpu.VMEM((total, groups * rows, units), F32),
            pltpu.VMEM((total, rows, wide - misc), F32),
        ],
        limit=6,
    )


def widen_kernel(blocks, after=()):
    number = len(blocks)
    rows, model = blocks[0].shape

    def body(*refs):
        order = Order("mp")
        out = refs[number]
        for m in range(number):
            at = pl.ds(pl.multiple_of(order[m] * rows, 16), rows)
            out[at, :] = refs[m][...].astype(F32)

    return local_kernel(
        body, [shape((number * rows, model), F32)], tuple(blocks), limit=2, after=after)[0]


def sigmoid(v):
    return 0.5 * jnp.tanh(0.5 * v) + 0.5


def one_hot(symbols, group, lanes, table_lanes):
    lane = lax.broadcasted_iota(jnp.int32, (symbols.shape[0], lanes), 1)
    hit = (lane == symbols) | (lane == table_lanes + GROUP_LANE + group)
    return hit.astype(F32).astype(BF)


def symbols_kernel(letters, counts, own_rows):
    seq = counts.shape[1]
    chars = letters.shape[1]
    every = own_rows + HALO

    def body(let, cnt, sym_all, alive_all, sym, alive):
        spot = Spot(seq)
        row = lax.broadcasted_iota(jnp.int32, (every, seq), 0)
        mine = jnp.where(
            row < own_rows, spot.own * own_rows + row, spot.beside_row - own_rows + row
        )
        line = lax.broadcasted_iota(jnp.int32, (every, seq), 1)
        sizes = cnt[...].astype(F32)
        start = jnp.sum(jnp.where(line < mine, sizes, 0.0), axis=1, keepdims=True)
        size = jnp.sum(jnp.where(line == mine, sizes, 0.0), axis=1, keepdims=True)
        letter = lax.broadcasted_iota(jnp.int32, (every, chars), 1).astype(F32)
        values = let[...].astype(F32)
        for slot in range(MAXC):
            alive_all[slot] = jnp.where(size > slot, 1.0, 0.0)
            alive[slot] = alive_all[slot, :own_rows]
            for way in range(2):
                if way == 0:
                    at = start + jnp.minimum(float(slot), size - 1.0)
                else:
                    at = start + jnp.maximum(size - 1.0 - slot, 0.0)
                found = jnp.sum(jnp.where(letter == at, values, 0.0), axis=1, keepdims=True)
                found = found.astype(jnp.int32)
                sym_all[way, slot * every : (slot + 1) * every, :] = found
                sym[way, slot * own_rows : (slot + 1) * own_rows, :] = found[:own_rows]

    return local_kernel(
        body,
        [
            shape((2, MAXC * every, 1), jnp.int32),
            shape((MAXC, every, 1), F32),
            shape((2, MAXC * own_rows, 1), jnp.int32),
            shape((MAXC, own_rows, 1), F32),
        ],
        (letters, counts),
    )


def encoder_forward(group, sym_all, alive_all, char_pack, hh_full, bias_full, table_lanes, own_rows, after=()):
    units = hh_full.shape[1]
    width = 3 * units
    lanes = table_lanes + 128
    embed = char_pack.shape[0]
    every = own_rows + HALO
    saved_shape = shape((2, MAXC, own_rows, units))

    def body(
        group_ref, sym_all, alive_all, pack, hh, bias,
        final, beside, emb, prev, rst, upd, car, fre,
        state, emb_all,
    ):
        for way in range(2):
            hits = one_hot(sym_all[way], group_ref[0], lanes, table_lanes)
            rows = product_nt(hits, pack[:, 2 * width :]).astype(BF)
            emb_all[way] = rows.reshape(MAXC, every, embed)
        emb[...] = emb_all[:, :, :own_rows]
        state[...] = jnp.zeros_like(state)

        @pl.loop(0, MAXC)
        def _(slot):
            live_col = alive_all[slot]
            for way in range(2):
                hidden = state[way]
                low = hidden.astype(BF)
                prev[way, slot] = low[:own_rows]
                gate = product(emb_all[way, slot], pack[:, way * width : (way + 1) * width])
                rec = product_nt(low, hh[way * width : (way + 1) * width])
                b_r = bias[way : way + 1, :units]
                b_z = bias[way : way + 1, units : 2 * units]
                b_n = bias[way : way + 1, 2 * units : 3 * units]
                b_c = bias[way : way + 1, 3 * units :]
                reset = sigmoid(gate[:, :units] + b_r + rec[:, :units])
                update = sigmoid(gate[:, units : 2 * units] + b_z + rec[:, units : 2 * units])
                carried = rec[:, 2 * units :] + b_c
                fresh = jnp.tanh(gate[:, 2 * units :] + b_n + reset * carried)
                rst[way, slot] = reset[:own_rows].astype(BF)
                upd[way, slot] = update[:own_rows].astype(BF)
                car[way, slot] = carried[:own_rows].astype(BF)
                fre[way, slot] = fresh[:own_rows].astype(BF)
                moved = (1.0 - update) * fresh + update * hidden
                state[way] = hidden + live_col * (moved - hidden)

        for way in range(2):
            low = state[way].astype(BF)
            final[:, way * units : (way + 1) * units] = low[:own_rows]
            beside[:, way * units : (way + 1) * units] = low[own_rows:]

    return local_kernel(
        body,
        [
            shape((own_rows, 2 * units)),
            shape((HALO, 2 * units)),
            shape((2, MAXC, own_rows, embed)),
        ]
        + [saved_shape] * 5,
        (group, sym_all, alive_all, char_pack, hh_full, bias_full),
        [
            pltpu.VMEM((2, every, units), F32),
            pltpu.VMEM((2, MAXC, every, embed), BF),
        ],
        limit=6,
        scalars=1, after=after)


def encoder_steps(grad_parts, hh_full, live, saved, after=()):
    own_rows = live.shape[1]
    units = hh_full.shape[1]
    width = 3 * units
    count = MAXC * own_rows
    pieces = len(grad_parts)

    def body(*refs):
        parts = refs[:pieces]
        hh, alive, prev, rst, upd, car, fre, low, inner_low, bias_grad, grad, sums = refs[pieces:]
        whole = parts[0][...].astype(F32)
        for part in parts[1:]:
            whole = whole + part[...].astype(F32)
        for way in range(2):
            grad[way] = whole[:, way * units : (way + 1) * units]
        sums[...] = jnp.zeros_like(sums)

        @pl.loop(0, MAXC)
        def _(step):
            slot = MAXC - 1 - step
            live_col = alive[slot]
            at = pl.ds(pl.multiple_of(slot * own_rows, 16), own_rows)
            for way in range(2):
                before = prev[way, slot].astype(F32)
                reset = rst[way, slot].astype(F32)
                update = upd[way, slot].astype(F32)
                carried = car[way, slot].astype(F32)
                fresh = fre[way, slot].astype(F32)
                g = grad[way]
                moved = live_col * g
                grad_fresh = moved * (1.0 - update)
                grad_update = moved * (before - fresh)
                grad_inner = grad_fresh * (1.0 - fresh * fresh)
                grad_carried = grad_inner * reset
                grad_reset = grad_carried * carried * (1.0 - reset)
                grad_z = grad_update * update * (1.0 - update)
                for part, what in enumerate((grad_reset, grad_z, grad_inner, grad_carried)):
                    sums[way, part] += jnp.sum(what.reshape(own_rows // 8, 8, units), 0)
                low[way, at, :units] = grad_reset.astype(BF)
                low[way, at, units : 2 * units] = grad_z.astype(BF)
                low[way, at, 2 * units :] = grad_carried.astype(BF)
                inner_low[way, at, :] = grad_inner.astype(BF)
                back = product(low[way, at, :], hh[way * width : (way + 1) * width])
                grad[way] = g - moved + moved * update + back

        for way in range(2):
            for part in range(4):
                bias_grad[way : way + 1, part * units : (part + 1) * units] = jnp.sum(
                    sums[way, part], 0, keepdims=True
                )

    return local_kernel(
        body,
        [
            shape((2, count, width)),
            shape((2, count, units)),
            shape((2, 4 * units), F32),
        ],
        (*grad_parts, hh_full, live, *saved),
        [pltpu.VMEM((2, own_rows, units), F32), pltpu.VMEM((2, 4, 8, units), F32)],
        limit=3, after=after)


def encoder_backward(
    group, split, steps_out, symbols, char_pack, embeds, previous, table_lanes, bias_cols, after=()
):
    low_all, inner_all, bias_all = steps_out
    units = inner_all.shape[2]
    width = 3 * units
    lanes = table_lanes + 128
    embed, wide = char_pack.shape
    count = low_all.shape[1]

    def body(*refs):
        group_ref = refs[0]
        sym, pack, low, inner_low, bias_grad, emb, prev = refs[1:8]
        results = refs[8 : 10 + (not split)]
        hh_grad = refs[10 + (not split)]
        if split:
            order8, order = Order("dp"), Order("mp")
            keep, send = results
            owners, depth = split
            strip = embed // owners
            steps = 2 * width // owners
            small = refs[-1]

        def pack_out(value, left):
            if not split:
                results[0][:, left : left + value.shape[1]] = value.astype(BF)
                return
            for b in range(owners):
                out = send if b % 2 else keep
                out[b // 2, 0, :, left : left + value.shape[1]] = value[
                    b * strip : (b + 1) * strip
                ].astype(BF)

        table_total = jnp.zeros((embed, lanes), F32)
        for way in range(2):
            rows = emb[way].reshape(count, embed)
            gates = low[way, :, : 2 * units]
            inner = inner_low[way]
            left = way * width
            pack_out(product_tn(rows, gates), left)
            pack_out(product_tn(rows, inner), left + 2 * units)
            embed_grad = product_nt(gates, pack[:, left : left + 2 * units]) + product_nt(
                inner, pack[:, left + 2 * units : left + width]
            )
            hits = one_hot(sym[way], group_ref[0], lanes, table_lanes)
            table_total = table_total + product_tn(embed_grad.astype(BF), hits)
            hh_grad[left : left + width] = product_tn(
                low[way], prev[way].reshape(count, units)
            ).astype(BF)
        if not split:
            pack_out(table_total, 2 * width)
            results[1][...] = hh_grad[...]
            results[2][...] = bias_grad[...]
            return
        pack_out(table_total[:, :table_lanes], 2 * width)
        small[...] = jnp.zeros_like(small)
        for k in range(owners * depth):
            small[k, :2, :bias_cols] = bias_grad[:, k * bias_cols : (k + 1) * bias_cols]
        lane = lax.broadcasted_iota(jnp.int32, (strip, 128), 1)
        for b in range(owners):
            out = send if b % 2 else keep
            mine = jnp.concatenate([small[order8[b] * depth + order[m]] for m in range(depth)], 0)
            last = table_total[b * strip : (b + 1) * strip, table_lanes:]
            out[b // 2, 0, :, wide - 128 :] = jnp.where(lane < GROUP_LANE, mine, last).astype(BF)
            for g in range(steps // strip):
                at = pl.ds(pl.multiple_of(order8[b] * steps + g * strip, 16), strip)
                out[b // 2, 1, :, g * units : (g + 1) * units] = hh_grad[at, :]

    outs = [shape(char_pack.shape), shape((2 * width, units)), shape((2, 4 * units), F32)]
    scratch = [pltpu.VMEM((2 * width, units), BF)]
    if split:
        owners, depth = split
        strip = embed // owners
        outs = [shape((owners // 2, 2, strip, wide))] * 2
        scratch.append(pltpu.VMEM((owners * depth, strip // depth, 128), F32))
    return local_kernel(
        body,
        outs,
        (group, symbols, char_pack, *steps_out, embeds, previous),
        scratch,
        limit=13.00,
        scalars=1, after=after)


def char_split_kernel(number, blocks, units, after=()):
    strip, wide = blocks[0].shape
    rows = strip // number
    groups = wide // units
    pieces = len(blocks)

    def body(*refs):
        order = Order("mp")
        outs, steps = refs[pieces : pieces + number], refs[pieces + number]
        total = refs[0][...].astype(F32) + refs[1][...].astype(F32)
        below = refs[2][...].astype(F32) + refs[3][...].astype(F32)
        for g in range(groups):
            steps[g * strip : (g + 1) * strip, :] = below[:, g * units : (g + 1) * units]
        for m, out in enumerate(outs):
            low = jnp.concatenate(
                [
                    steps[pl.ds(pl.multiple_of((order[m] * groups + g) * rows, 8), rows), :]
                    for g in range(groups)
                ],
                1,
            )
            out[...] = jnp.concatenate([total[m * rows : (m + 1) * rows], low], 0).astype(BF)

    return local_kernel(
        body,
        [shape((2 * rows, wide))] * number,
        tuple(blocks),
        [pltpu.VMEM((strip * groups, units), F32)],
        limit=2, after=after)


def per_device(
    tokens,
    char_ids,
    token_chars,
    groups,
    qkv_weight,
    out_weight,
    ffn_in,
    ffn_out,
    conv_weight,
    gains,
    ih_weight,
    hh_weight,
    gru_bias,
    char_table,
    group_table,
    token_cot,
    char_cot,
):
    dp_size, mp_size = lax.axis_size("dp"), lax.axis_size("mp")
    mp_index = lax.axis_index("mp")
    seq_len, model = tokens.shape
    local = out_weight.shape[0]
    heads = local // (model // HEADS)
    own_rows = seq_len // mp_size
    ih_rows, ih_cols = ih_weight.shape
    symbols_n, group_count = char_table.shape[0], group_table.shape[0]
    table_lanes = -(-symbols_n // 128) * 128
    misc_at = ih_cols + table_lanes
    units = hh_weight.shape[1]
    bias_cols, gain_cols = gru_bias.shape[1], gains.shape[1]
    both = ("dp", "mp")

    qkv_own = jnp.transpose(qkv_weight, (1, 0, 2))
    if quick():
        pack = pack_kernel(
            ih_weight, hh_weight, gru_bias, char_table.T, group_table.T, out_weight.T, gains
        )
        qkv_blocks = share_dp(qkv_own, held(p1=pack))
        qkv_full, packed, probs, attn_low, same, other = attention_kernel(
            tokens, qkv_blocks, heads
        )
        attn_blocks = pass_on([same, same, other, other])
        packs = share_mp(pack)
        layer_own = pack_layer_kernel(
            ffn_in, ffn_out.T, conv_weight.T, held(s5=qkv_blocks[2:3], s9=packs[1])
        )
        layer_send = layer_own
        if "s4" in HOLDS:
            layer_send = stack_kernel([layer_own], packs[1:2])[0]
        layer_blocks = share_dp_by(layer_own, ROUTES[0])
        packs_high = stack_kernel(packs[:2], held(s6=same, s7=attn_blocks[1:], s12=layer_blocks[2]))
        char_high = share_dp_by(packs_high, ROUTES[2])
        packs_low = stack_kernel(packs[2:], held(s6=same, s1=attn_blocks[1:], s13=layer_blocks[4]))
        char_low = share_dp_by(packs_low, ROUTES[3])
        layer_other = swap(layer_send, "mp", 2)
        if "s8" in HOLDS:
            layer_other = stack_kernel([layer_other], (char_high[2], char_low[4]))[0]
        layer_lists = (layer_blocks, share_dp_by(layer_other, ROUTES[1]))
        char_lists = (char_high, char_low)
        out_full, gain_rows = unpack_out_kernel(
            char_lists, misc_at + 128, local, gains.shape
        )
        char_pack, hh_full, bias_full = unpack_char_kernel(
            char_lists, units, gru_bias.shape, misc_at
        )
        in_set, down_set, conv_set = unpack_layer_kernel(
            layer_lists, ffn_in.shape[0], held(s2=attn_blocks[1:], s10=char_pack)
        )
    else:
        qkv_blocks = [lax.all_gather(qkv_own, "dp", axis=1, tiled=True)]
        qkv_full, packed, probs, attn_low, same, other = attention_kernel(
            tokens, qkv_blocks, heads
        )
        attn_blocks = pass_on([same, same, other, other])
        vocab = jnp.pad(char_table.T, ((0, 0), (0, table_lanes - symbols_n)))
        misc = jnp.pad(group_table.T, ((0, 0), (GROUP_LANE, 128 - GROUP_LANE - group_count)))
        char_pack = lax.all_gather(
            jnp.concatenate([ih_weight, vocab, misc], 1), both, axis=0, tiled=True
        )
        hh_full = lax.all_gather(hh_weight, both, axis=0, tiled=True)
        bias_full = lax.all_gather(gru_bias, both, axis=1, tiled=True).astype(F32)
        gain_rows = lax.all_gather(gains, "dp", axis=1, tiled=True).astype(F32)
        out_full = lax.all_gather(
            lax.all_gather(out_weight.T, "dp", axis=0, tiled=True), "mp", axis=0
        )
        order = jnp.stack([mp_index ^ m for m in range(mp_size)]).astype(jnp.int32)
        out_full = jnp.take(out_full, order, axis=0)
        ffn_full = lax.all_gather(jnp.stack([ffn_in, ffn_out.T]), "dp", axis=1, tiled=True)
        ffn_full = jnp.stack([ffn_full, swap(ffn_full, "mp", 2)])
        in_set, down_set = ffn_full[:, 0], ffn_full[:, 1]
        conv_set = lax.all_gather(conv_weight, "dp", axis=0, tiled=True)
        conv_set = jnp.concatenate([conv_set, swap(conv_set, "mp", 2)], 1)
    conv_set = conv_set.reshape(3, 2 * model, 2 * local)

    sym_all, alive_all, symbols, live = symbols_kernel(char_ids, token_chars, own_rows)
    final, final_beside, embeds, *saved = encoder_forward(
        groups, sym_all, alive_all, char_pack, hh_full, bias_full, table_lanes, own_rows
    )
    char_blocks = [final, swap(final, "mp", 1), final_beside]

    low_half, hidden, hidden_slope, normal_one, scale_one, base, keep, send = middle_kernel(
        attn_blocks, tokens, out_full, gain_rows, in_set, down_set, held(s3=final)
    )
    normal_two, scale_two, two_low, two_beside = second_kernel(
        keep, swap(send, "mp", 1), base, gain_rows
    )
    token_blocks = [two_low, swap(two_low, "mp", 1), two_beside]

    mixed, joined_slope, sent = joining_kernel(token_blocks, char_blocks, conv_set)
    (
        token_half, char_half, quarter, own_token, own_char, pre_half, pre_grad, gain_three, gain_four,
        keep, send,
    ) = turn_kernel(
        sent, swap(sent, "mp", 1), mixed, token_cot, char_cot, gain_rows, joined_slope, conv_set
    )
    mixed_token = [keep, swap(send, "mp", 1)]
    keep, send = char_half_kernel(pre_half, conv_set)
    mixed_char = [keep, swap(send, "mp", 1)]
    quarter = swap(quarter, "mp", 2)
    if quick():
        conv_keep, conv_send = conv_split_kernel(mixed, pre_grad, dp_size, 2)
    else:
        conv_send = conv_grad_kernel(mixed, pre_grad)
    grad_second, second_low, gain_two = norm_back_kernel(
        mixed_token, own_token, normal_two, scale_two, gain_rows, 1, (), held(b1=conv_send)
    )
    steps_out = encoder_steps(
        [own_char] + mixed_char, hh_full, live, saved, held(b2=second_low)
    )
    backward = (steps_out, symbols, char_pack, embeds, saved[0], table_lanes, bias_cols)
    hold = held(b3=steps_out[2])
    if quick():
        conv_blocks = merge_two(conv_keep, conv_send)
        hold += held(b4=conv_blocks[0])
    second_half, grad_hidden, keep, send = feed_back_kernel(
        second_low, swap(second_low, "mp", 1), hidden_slope, in_set, down_set, hold
    )
    feed_args = (second_half, hidden, low_half, grad_hidden)
    hold = ()
    if quick():
        char_keep, char_send = encoder_backward(
            groups, (dp_size, mp_size), *backward, held(b5=second_half)
        )
        hold = held(b6=char_send)
        if "b7" not in HOLDS:
            feed_keep, feed_send = feed_split_kernel(*feed_args, dp_size, 2)
            hold += held(b26=feed_send)
    grad_first, first_low, _ = norm_back_kernel(
        [keep, swap(send, "mp", 1)], grad_second, normal_one, scale_one, gain_rows, 0,
        (gain_two, gain_three, gain_four), hold,
    )
    hold = held(b25=steps_out[2])
    if quick():
        if "b7" in HOLDS:
            feed_keep, feed_send = feed_split_kernel(*feed_args, dp_size, 2, (first_low,))
        char_parts = merge_two(char_keep, char_send, held(b8=first_low))
        conv_keep, conv_send = layer_sum_kernel(spread_two(conv_blocks), held(b9=first_low))
        hold += held(b10=feed_send, b11=char_parts[0], b12=conv_keep)
        if "b13" in HOLDS:
            feed_blocks = merge_two(feed_keep, feed_send)
            hold += (feed_blocks[0],)
    first_full, grad_packed, gain_grad, *token_parts = attention_back_kernel(
        share_mp(first_low), out_full, packed, probs, qkv_full, hold
    )
    token_out, char_out = outputs_kernel(
        token_half, char_half, quarter, swap(quarter, "mp", 1), held(b14=first_full)
    )
    token_parts = pass_on(token_parts)
    hold = ()
    if quick():
        if "b13" not in HOLDS:
            feed_blocks = merge_two(feed_keep, feed_send, held(b15=token_parts[1]))
        attn_keep, attn_send = qkv_split_kernel(
            tokens, grad_packed, first_full, attn_low, gain_grad, gains.shape[0], dp_size,
            held(b16=token_parts[1]),
        )
        hold = held(b17=feed_blocks[0], b18=attn_send)
        char_parts = spread_two(char_parts)
        if "b23" in HOLDS:
            char_parts = char_split_kernel(mp_size, char_parts, units)
            hold += (char_parts[0],)
        if "b27" in HOLDS:
            conv_grad = conv_final_kernel(conv_keep, swap(conv_send, "mp", 2))
            hold += (conv_grad,)
    token_own = sum_kernel(grad_first, token_parts, hold)
    token_blocks = share_mp(token_own)
    hold = ()
    if quick():
        attn_parts = merge_dp(attn_keep, attn_send, held(b19=token_own))
        if "b23" not in HOLDS:
            char_parts = char_split_kernel(mp_size, char_parts, units, held(b20=token_blocks[1]))
        if "b27" not in HOLDS:
            conv_grad = conv_final_kernel(conv_keep, swap(conv_send, "mp", 2))
        feed_keep, feed_send = layer_sum_kernel(spread_two(feed_blocks))
        hold = held(b21=char_parts[0], b22=attn_parts[0], b24=feed_keep)
    token_grad = widen_kernel(token_blocks, hold)

    group_at = misc_at + GROUP_LANE
    table_to = ih_cols + symbols_n
    gain_count = gains.shape[0]
    if quick():
        in_grad, down_grad = feed_final_kernel(feed_keep, swap(feed_send, "mp", 2))
        conv_grad = conv_grad.T
        qkv_grad, out_grad, gain_own = qkv_final_kernel(
            spread_dp(attn_parts),
            gains.shape,
        )
        ih_grad, table_grad, group_grad, bias_own, hh_own = char_final_kernel(
            pass_on(char_parts),
            (ih_cols, symbols_n, group_count, gru_bias.shape, hh_weight.shape),
        )
        table_grad, group_grad = table_grad.T, group_grad.T
    else:

        def spread(rows, axis):
            return lax.psum_scatter(rows.astype(F32), both, scatter_dimension=axis, tiled=True)

        attn_grads = qkv_grad_kernel(tokens, grad_packed, first_full, attn_low)
        attn_grads = lax.psum_scatter(
            attn_grads.astype(F32), "dp", scatter_dimension=1, tiled=True
        )
        qkv_grad, out_grad = attn_grads[:3], attn_grads[3].T
        feed_grad = feed_grad_kernel(*feed_args, 2).astype(F32)
        feed_grad = lax.psum_scatter(
            feed_grad[0] + swap(feed_grad[1], "mp", 2), "dp", scatter_dimension=1, tiled=True
        )
        in_grad, down_grad = feed_grad[0], feed_grad[1]
        conv_grad = conv_send.reshape(-1, 2 * local).astype(F32)
        conv_grad = conv_grad[:, :local] + swap(conv_grad[:, local:], "mp", 2)
        conv_grad = lax.psum_scatter(conv_grad, "dp", scatter_dimension=0, tiled=True)
        gain_own = lax.psum_scatter(
            gain_grad[:gain_count], "dp", scatter_dimension=1, tiled=True
        )
        pack_grad, hh_grad, bias_grad = encoder_backward(groups, None, *backward)
        ih_grad = spread(pack_grad[:, :ih_cols], 0)
        hh_own = spread(hh_grad, 0)
        table_grad = spread(pack_grad[:, ih_cols:table_to].T, 1)
        group_grad = spread(pack_grad[:, group_at : group_at + group_count].T, 1)
        bias_own = spread(bias_grad, 1)
    return (
        token_out,
        char_out,
        token_grad,
        jnp.transpose(qkv_grad, (1, 0, 2)),
        out_grad,
        in_grad,
        down_grad.T,
        conv_grad,
        gain_own,
        ih_grad,
        hh_own,
        bias_own,
        table_grad,
        group_grad,
    )


def solution(mesh):
    return jax.shard_map(
        per_device,
        mesh=mesh,
        in_specs=(
            P("dp", None),
            P("dp", None),
            P("dp", None),
            P("dp"),
            P("dp", None, "mp"),
            P("mp", "dp"),
            P("dp", "mp"),
            P("mp", "dp"),
            P("dp", "mp"),
            P(None, "dp"),
            P(("dp", "mp"), None),
            P(("dp", "mp"), None),
            P(None, ("dp", "mp")),
            P(None, ("dp", "mp")),
            P(None, ("dp", "mp")),
            P("dp", None),
            P("dp", None),
        ),
        out_specs=(
            P("dp", None),
            P("dp", None),
            P("dp", None),
            P("dp", None, "mp"),
            P("mp", "dp"),
            P("dp", "mp"),
            P("mp", "dp"),
            P("dp", "mp"),
            P(None, "dp"),
            P(("dp", "mp"), None),
            P(("dp", "mp"), None),
            P(None, ("dp", "mp")),
            P(None, ("dp", "mp")),
            P(None, ("dp", "mp")),
        ),
        check_vma=False,
    )
```

```python
import jax
import jax.numpy as jnp
from jax import lax
from jax.experimental import pallas as pl
from jax.experimental.pallas import tpu as pltpu
from jax.sharding import PartitionSpec as P

COST_SCALE = 4.0
COSTS = {"attention_kernel": 2.2, "middle_kernel": 3.6, "joining_kernel": 3.0, "turn_kernel": 2.6, "char_half_kernel": 0.8, "conv_split_kernel": 2.5, "feed_back_kernel": 1.5, "feed_split_kernel": 7.5, "encoder_forward": 11.0, "encoder_steps": 7.5, "encoder_backward": 5.5, "attention_back_kernel": 2.8, "qkv_split_kernel": 6.5}
HEADS = 12
MAXC = 8
NORM_EPS = 1e-05
BF = jnp.bfloat16
F32 = jnp.float32
GROUP_LANE = 96
HALO = 32
HOLDS = frozenset(["b1", "b16", "b21", "b22", "b26", "b4", "b6", "p1", "s14", "s2", "s5", "s6"])
ROUTES = "xyxy"
MB = 1 << 20


def dot(left, right, dims):
    return lax.dot_general(left, right, (dims, ((), ())), preferred_element_type=F32)


def product(left, right):
    return dot(left, right, ((1,), (0,)))


def product_tn(left, right):
    return dot(left, right, ((0,), (0,)))


def product_nt(left, right):
    return dot(left, right, ((1,), (1,)))


def swap(rows, axis, mask):
    size = lax.axis_size(axis)
    return lax.ppermute(rows, axis, [(i, i ^ mask) for i in range(size)])


def quick():
    return lax.axis_size("dp") == 8


def held(**arrays):
    found = []
    for name, array in arrays.items():
        if name in HOLDS:
            found += list(array) if isinstance(array, (list, tuple)) else [array]
    return tuple(found)


def take(blocks, index, axis=0):
    return lax.dynamic_index_in_dim(blocks, index, axis, keepdims=False)


def share_mp(block):
    return [block] + [swap(block, "mp", m) for m in range(1, lax.axis_size("mp"))]


def pass_on(blocks):
    return [blocks[0]] + [swap(blocks[m], "mp", m) for m in range(1, len(blocks))]


def share_dp(block, after=()):
    even = [block] + [swap(block, "dp", a) for a in range(2, lax.axis_size("dp"), 2)]
    if after:
        even[-1] = stack_kernel(even[-1:], after)[0]
    blocks = []
    for got in even:
        blocks += [got, swap(got, "dp", 1)]
    return blocks


def share_dp_by(block, route):
    if route == "d":
        return share_dp(block)
    near = 2 if route == "x" else 4
    far = 6 - near
    passed = swap(block, "dp", near)
    even = {0: block, near: passed, far: swap(block, "dp", far), 6: swap(passed, "dp", far)}
    blocks = []
    for a in range(0, 8, 2):
        blocks += [even[a], swap(even[a], "dp", 1)]
    return blocks


def merge_dp(keep, send, after=()):
    return merge_kernel(keep, swap(send, "dp", 1), after)


def spread_dp(blocks):
    return [blocks[0]] + [swap(block, "dp", 2 * i + 2) for i, block in enumerate(blocks[1:])]


def merge_two(keep, send, after=()):
    return merge_two_kernel(keep, swap(send, "dp", 1), after)


def spread_two(parts, after=()):
    first_keep, first_send, second_keep, second_send = parts
    first, first_next, second, second_next = relay_kernel(
        first_keep, swap(first_send, "dp", 4), second_keep, swap(second_send, "dp", 2), after
    )
    return [first, swap(first_next, "dp", 2), second, swap(second_next, "dp", 4)]


GELU_A = 0.7978845608028654
GELU_B = 0.044715


def gelu_both(v):
    t = jnp.tanh(GELU_A * (v + GELU_B * v * v * v))
    up = 0.5 * (1.0 + t)
    slope = up + 0.5 * v * (1.0 - t * t) * (GELU_A + 3.0 * GELU_A * GELU_B * v * v)
    return v * up, slope


def norm_parts(rows_in):
    row_mean = jnp.mean(rows_in, axis=-1, keepdims=True)
    centred = rows_in - row_mean
    spread = jnp.mean(centred * centred, axis=-1, keepdims=True)
    scale = lax.rsqrt(spread + NORM_EPS)
    return centred * scale, scale


def norm_back(normal, scale, gain_row, cotangent):
    lifted = cotangent * gain_row
    inner = jnp.mean(lifted * normal, axis=-1, keepdims=True)
    grad = scale * (lifted - jnp.mean(lifted, axis=-1, keepdims=True) - normal * inner)
    return grad, jnp.sum(cotangent * normal, axis=0, keepdims=True)


def shape(dims, dtype=BF):
    return jax.ShapeDtypeStruct(dims, dtype)


class Order:
    def __init__(self, axis):
        self.axis = axis

    def __getitem__(self, mask):
        return lax.axis_index(self.axis) ^ mask


class Spot:
    def __init__(self, seq):
        own = lax.axis_index("mp")
        top, pair = own >> 1, own & 1
        self.own, self.top, self.pair = own, top, pair
        self.window = top * (seq // 2 - HALO)
        self.half = top * HALO
        self.quarter = self.half + pair * (seq // 4)
        self.partner = self.half + (1 - pair) * (seq // 4)
        self.beside = (1 - top) * (seq // 2)
        self.in_half = pair * (seq // 4)
        self.partner_in_half = (1 - pair) * (seq // 4)
        self.beside_row = seq // 2 - HALO * top


def rows_at(ref, start, rows):
    return ref[pl.ds(pl.multiple_of(start, 16), rows), :]


def local_kernel(body, outs, args, scratch=(), limit=3.0, scalars=0, after=()):
    vmem = pl.BlockSpec(memory_space=pltpu.VMEM)
    smem = pl.BlockSpec(memory_space=pltpu.SMEM)
    idle = pl.BlockSpec(memory_space=pl.ANY)
    number, skip = len(args), len(after)

    def run(*refs):
        body(*refs[:number], *refs[number + skip :])

    return pl.pallas_call(
        run,
        out_shape=outs,
        in_specs=[smem] * scalars + [vmem] * (number - scalars) + [idle] * skip,
        out_specs=[vmem] * len(outs),
        scratch_shapes=list(scratch),
        compiler_params=pltpu.CompilerParams(vmem_limit_bytes=int((limit + 1.5) * MB)),
        name=body.__qualname__.split(".")[0],
        cost_estimate=pl.CostEstimate(
            flops=int(1e9 * COST_SCALE * COSTS.get(body.__qualname__.split(".")[0], 0.5)), bytes_accessed=0, transcendentals=0
        ),
    )(*args, *after)


def block_rows(ref, at, rows):
    return ref[pl.ds(pl.multiple_of(at * rows, 16), rows), :]


def spill(order, total, outs, rows):
    for m, out in enumerate(outs):
        out[...] = block_rows(total, order[m], rows).astype(BF)


def fill(order, blocks, full, rows):
    for m, block in enumerate(blocks):
        full[pl.ds(pl.multiple_of(order[m] * rows, 16), rows), :] = block[...]


def attention_kernel(tokens, blocks, heads):
    seq, model = tokens.shape
    number = len(blocks)
    _, rows, local = blocks[0].shape
    size = local // heads
    part = (seq // 2 + HALO) // 2

    def body(x, *refs):
        order = Order("dp")
        blk = refs[:number]
        w, packed, probs, attn, same, other = refs[number:]
        spot = Spot(seq)
        for i in range(3):
            for a in range(number):
                if number == 1:
                    w[i] = blk[a][i]
                else:
                    w[i, pl.ds(pl.multiple_of(order[a] * rows, 16), rows), :] = blk[a][i]
            packed[i] = product(x[...], w[i]).astype(BF)
        for h in range(heads):
            at = slice(h * size, (h + 1) * size)
            scores = product_nt(packed[0, :, at], packed[1, :, at]) * 0.125
            raised = jnp.exp(scores - jnp.max(scores, axis=-1, keepdims=True))
            total = jnp.sum(raised, axis=-1, keepdims=True)
            prob = (raised / total).astype(BF)
            probs[h] = prob
            attn[:, at] = product(prob, packed[2, :, at]).astype(BF)
        for out, start in ((same, spot.window), (other, seq // 2 - HALO - spot.window)):
            for top in range(2):
                at = pl.ds(pl.multiple_of(start + top * part, 16), part)
                out[:, top * local : (top + 1) * local] = attn[at, :]

    return local_kernel(
        body,
        [
            shape((3, model, local)),
            shape((3, seq, local)),
            shape((heads, seq, seq)),
            shape((seq, local)),
            shape((part, 2 * local)),
            shape((part, 2 * local)),
        ],
        (tokens, *blocks),
        limit=2,
    )


def middle_kernel(blocks, tokens, out_full, gain_rows, in_set, down_set, after=()):
    seq, model = tokens.shape
    number = len(blocks)
    local = out_full.shape[2]
    sets, _, hid = in_set.shape
    half, rows = seq // 2, seq // 4
    window, part = half + HALO, (half + HALO) // 2

    def body(*refs):
        spot = Spot(seq)
        blk = refs[:number]
        x, wo, g, wi, wd = refs[number : number + 5]
        low_half, hidden_half, slope_half, normal_own, scale_own, base, keep, send = refs[
            number + 5 : number + 13
        ]
        total, scales, low, hidden, slope = refs[number + 13 :]
        for top in range(2):
            at = slice(top * part, (top + 1) * part)
            lanes = slice(top * local, (top + 1) * local)
            acc = rows_at(x, spot.window + top * part, part).astype(F32)
            for m in range(number):
                acc = acc + product_nt(blk[m][:, lanes], wo[m])
            normal, scale = norm_parts(acc)
            total[at] = normal
            scales[at] = scale
            low[at] = (normal * g[0:1]).astype(BF)
        low_half[...] = rows_at(low, spot.half, half)
        normal_own[...] = rows_at(total, spot.quarter, rows)
        scale_own[...] = rows_at(scales, spot.quarter, rows)
        base[:rows] = normal_own[...] * g[0:1]
        base[rows:] = rows_at(total, spot.beside, HALO) * g[0:1]
        for s in range(sets):
            at = slice(s * hid, (s + 1) * hid)
            value, steep = gelu_both(product(low[...], wi[s]))
            hidden[:, at] = value.astype(BF)
            slope[:, at] = steep.astype(BF)
        hidden_half[...] = rows_at(hidden, spot.half, half)
        slope_half[...] = rows_at(slope, spot.half, half)
        whole = product_nt(hidden[:, :hid], wd[0])
        for s in range(1, sets):
            whole = whole + product_nt(hidden[:, s * hid : (s + 1) * hid], wd[s])
        total[...] = whole
        beside = rows_at(total, spot.beside, HALO).astype(BF)
        for out, start in ((keep, spot.quarter), (send, spot.partner)):
            out[:rows] = rows_at(total, start, rows).astype(BF)
            out[rows:] = beside

    return local_kernel(
        body,
        [
            shape((half, model)),
            shape((half, sets * hid)),
            shape((half, sets * hid)),
            shape((rows, model), F32),
            shape((rows, 1), F32),
            shape((rows + HALO, model), F32),
            shape((rows + HALO, model)),
            shape((rows + HALO, model)),
        ],
        (*blocks, tokens, out_full, gain_rows, in_set, down_set),
        [
            pltpu.VMEM((window, model), F32),
            pltpu.VMEM((window, 1), F32),
            pltpu.VMEM((window, model), BF),
            pltpu.VMEM((window, sets * hid), BF),
            pltpu.VMEM((window, sets * hid), BF),
        ],
        limit=6, after=after)


def second_kernel(keep, got, base, gain_rows):
    high, model = base.shape
    rows = high - HALO

    def body(keep, got, base, g, normal, scale, low, beside):
        xh, r = norm_parts(base[...] + keep[...].astype(F32) + got[...].astype(F32))
        normal[...] = xh[:rows]
        scale[...] = r[:rows]
        out = (xh * g[1:2]).astype(BF)
        low[...] = out[:rows]
        beside[...] = out[rows:]

    return local_kernel(
        body,
        [
            shape((rows, model), F32),
            shape((rows, 1), F32),
            shape((rows, model)),
            shape((HALO, model)),
        ],
        (keep, got, base, gain_rows),
    )


def joining_kernel(token_blocks, char_blocks, conv_set):
    rows, model = token_blocks[0].shape
    seq = 4 * rows
    half = seq // 2
    window = half + HALO
    local = conv_set.shape[2]

    def body(*refs):
        spot = Spot(seq)
        conv, mixed, slope, sent = refs[6:]
        places = ((spot.quarter, rows), (spot.partner, rows), (spot.beside, HALO))
        for i, (start, count) in enumerate(places):
            at = pl.ds(pl.multiple_of(start, 16), count)
            mixed[at, :model] = refs[i][...]
            mixed[at, model:] = refs[3 + i][...]
        line = lax.broadcasted_iota(jnp.int32, (window, 1), 0)
        before = pltpu.roll(product(mixed[...], conv[0]), 1, 0)
        after = pltpu.roll(product(mixed[...], conv[2]), window - 1, 0)
        pre = product(mixed[...], conv[1])
        pre = pre + jnp.where(line == 0, 0.0, before) + jnp.where(line == window - 1, 0.0, after)
        value, steep = gelu_both(pre)
        slope[...] = steep.astype(BF)
        sent[...] = value.astype(BF)

    return local_kernel(
        body,
        [shape((window, 2 * model)), shape((window, local)), shape((window, local))],
        (*token_blocks, *char_blocks, conv_set),
        limit=3,
    )


def turn_kernel(joined_own, joined_got, mixed, token_cot, char_cot, gain_rows, slope, conv_set):
    seq, model = token_cot.shape
    half, rows = seq // 2, seq // 4
    window, local = joined_own.shape
    one = local // 2

    def body(
        mine, got, mix, cot_t, cot_c, g, steep, conv,
        token_half, char_half, quarter, own_t, own_c, pre_half, pre_grad, gain_t, gain_c, keep, send,
        stack, joined, total, picked, outs, pre3, parts,
    ):
        spot = Spot(seq)
        order = Order("mp")
        for m, (ref, lane) in enumerate(((mine, 0), (got, 0), (mine, one), (got, one))):
            stack[order[m]] = ref[:, lane : lane + one]
        for j in range(4):
            joined[:, j * one : (j + 1) * one] = stack[j]
        both = joined[...].astype(F32)
        line = lax.broadcasted_iota(jnp.int32, (window, 1), 0)
        is_own = (line >= spot.quarter) & (line < spot.quarter + rows)
        grad_sum = None
        for lane, cot_ref, out, own, gain, row in (
            (0, cot_t, token_half, own_t, gain_t, 2),
            (model, cot_c, char_half, own_c, gain_c, 3),
        ):
            xh, r = norm_parts(mix[:, lane : lane + model].astype(F32) + both)
            outs[...] = (xh * g[row : row + 1]).astype(BF)
            out[...] = rows_at(outs, spot.half, half)
            quarter[row - 2] = rows_at(outs, spot.quarter, rows)
            cot = rows_at(cot_ref, spot.window, window).astype(F32)
            grad, _ = norm_back(xh, r, g[row : row + 1], cot)
            gain[...] = jnp.sum(jnp.where(is_own, cot * xh, 0.0), axis=0, keepdims=True)
            total[...] = grad
            own[...] = rows_at(total, spot.quarter, rows)
            grad_sum = grad if grad_sum is None else grad_sum + grad
        for j in range(4):

            @pl.when(spot.own == j)
            def _():
                picked[:, :one] = grad_sum[:, j * one : (j + 1) * one]
                picked[:, one:] = grad_sum[:, (j ^ 2) * one : ((j ^ 2) + 1) * one]

        grad = (picked[...] * steep[...].astype(F32)).astype(BF).astype(F32)

        def fan(rows_in, out):
            out[0] = jnp.where(line == window - 1, 0.0, pltpu.roll(rows_in, window - 1, 0)).astype(BF)
            out[1] = rows_in.astype(BF)
            out[2] = jnp.where(line == 0, 0.0, pltpu.roll(rows_in, 1, 0)).astype(BF)

        fan(grad, pre3)
        at = pl.ds(pl.multiple_of(spot.half, 16), half)
        for k in range(3):
            pre_half[k] = pre3[k, at, :]
        is_half = (line >= spot.half) & (line < spot.half + half)
        fan(jnp.where(is_half, grad, 0.0), pre_grad)
        parts[...] = (
            product_nt(pre_half[0], conv[0, :model])
            + product_nt(pre_half[1], conv[1, :model])
            + product_nt(pre_half[2], conv[2, :model])
        )
        keep[...] = rows_at(parts, spot.in_half, rows).astype(BF)
        send[...] = rows_at(parts, spot.partner_in_half, rows).astype(BF)

    return local_kernel(
        body,
        [shape((half, model))] * 2
        + [shape((2, rows, model))]
        + [shape((rows, model), F32)] * 2
        + [shape((3, half, local)), shape((3, window, local))]
        + [shape((1, model), F32)] * 2
        + [shape((rows, model))] * 2,
        (joined_own, joined_got, mixed, token_cot, char_cot, gain_rows, slope, conv_set),
        [
            pltpu.VMEM((4, window, one), BF),
            pltpu.VMEM((window, model), BF),
            pltpu.VMEM((window, model), F32),
            pltpu.VMEM((window, local), F32),
            pltpu.VMEM((window, model), BF),
            pltpu.VMEM((3, window, local), BF),
            pltpu.VMEM((half, model), F32),
        ],
        limit=8,
    )


def char_half_kernel(pre_half, conv_set, after=()):
    _, half, _ = pre_half.shape
    model = conv_set.shape[1] // 2
    rows = half // 2

    def body(pre, conv, keep, send, parts):
        spot = Spot(2 * half)
        parts[...] = (
            product_nt(pre[0], conv[0, model:])
            + product_nt(pre[1], conv[1, model:])
            + product_nt(pre[2], conv[2, model:])
        )
        keep[...] = rows_at(parts, spot.in_half, rows).astype(BF)
        send[...] = rows_at(parts, spot.partner_in_half, rows).astype(BF)

    return local_kernel(
        body,
        [shape((rows, model))] * 2,
        (pre_half, conv_set),
        [pltpu.VMEM((half, model), F32)], after=after)


def conv_grad_kernel(mixed, pre_grad):
    local = pre_grad.shape[2]
    wide = mixed.shape[1]

    def body(mix, pre, grad):
        for k in range(3):
            grad[k] = product_tn(mix[...], pre[k]).astype(BF)

    return local_kernel(body, [shape((3, wide, local))], (mixed, pre_grad), limit=3)[0]


def conv_split_kernel(mixed, pre_grad, owners, sets, after=()):
    taps, _, both = pre_grad.shape
    wide = mixed.shape[1]
    local = both // sets
    rows = taps * wide // owners
    part = rows // 2

    def body(mix, pre, keep, send, whole):
        order = Order("dp")
        for k in range(taps):
            whole[k * wide : (k + 1) * wide] = product_tn(mix[...], pre[k]).astype(BF)
        for b in range(owners):
            out = send if b % 2 else keep
            for h in range(2):
                at = pl.ds(pl.multiple_of(order[b] * rows + h * part, 16), part)
                for s in range(sets):
                    out[b // 2, s, :, h * local : (h + 1) * local] = whole[
                        at, s * local : (s + 1) * local
                    ]

    return local_kernel(
        body,
        [shape((owners // 2, sets, part, 2 * local))] * 2,
        (mixed, pre_grad),
        [pltpu.VMEM((taps * wide, both), BF)],
        limit=7, after=after)


def outputs_kernel(token_half, char_half, got, passed, after=()):
    half, model = token_half.shape
    rows = half // 2

    def body(token_half, char_half, got, passed, token_out, char_out):
        spot = Spot(2 * half)
        mine = pl.ds(pl.multiple_of(spot.top * half, 16), half)
        other = (1 - spot.top) * half
        for i, (own, out) in enumerate(((token_half, token_out), (char_half, char_out))):
            out[mine, :] = own[...]
            for ref, start in ((got, spot.in_half), (passed, spot.partner_in_half)):
                out[pl.ds(pl.multiple_of(other + start, 16), rows), :] = ref[i]

    return local_kernel(
        body, [shape((2 * half, model))] * 2, (token_half, char_half, got, passed), after=after)


def norm_back_kernel(parts, residual, normal, scale, gain_rows, row, gain_parts=(), after=()):
    rows, model = residual.shape
    number = len(parts)
    extra = len(gain_parts)

    def body(*refs):
        res, xh, r, g = refs[number : number + 4]
        others = refs[number + 4 : number + 4 + extra]
        grad, low, gain = refs[number + 4 + extra :]
        total = res[...]
        for part in refs[:number]:
            total = total + part[...].astype(F32)
        out, own = norm_back(xh[...], r[...], g[row : row + 1], total)
        gain[...] = own
        grad[...] = out
        low[:rows] = out.astype(BF)
        if extra:
            line = lax.broadcasted_iota(jnp.int32, (16, model), 0)
            tail = jnp.where(line == 0, own, 0.0)
            for i, other in enumerate(others):
                tail = jnp.where(line == i + 1, other[...], tail)
            low[rows:] = tail.astype(BF)

    return local_kernel(
        body,
        [
            shape((rows, model), F32),
            shape((rows + (16 if extra else 0), model)),
            shape((1, model), F32),
        ],
        (*parts, residual, normal, scale, gain_rows, *gain_parts),
        limit=1, after=after)


def feed_back_kernel(second_own, second_got, slope, in_set, down_set, after=()):
    rows, model = second_own.shape
    half = 2 * rows
    sets, _, hid = in_set.shape

    def body(mine, got, steep, wi, wd, full, grad, keep, send, parts):
        spot = Spot(2 * half)
        full[pl.ds(pl.multiple_of(spot.in_half, 16), rows), :] = mine[...]
        full[pl.ds(pl.multiple_of(spot.partner_in_half, 16), rows), :] = got[...]
        total = None
        for s in range(sets):
            at = slice(s * hid, (s + 1) * hid)
            grad[:, at] = (product(full[...], wd[s]) * steep[:, at].astype(F32)).astype(BF)
            part = product_nt(grad[:, at], wi[s])
            total = part if total is None else total + part
        parts[...] = total
        keep[...] = rows_at(parts, spot.in_half, rows).astype(BF)
        send[...] = rows_at(parts, spot.partner_in_half, rows).astype(BF)

    return local_kernel(
        body,
        [shape((half, model)), shape((half, sets * hid))] + [shape((rows, model))] * 2,
        (second_own, second_got, slope, in_set, down_set),
        [pltpu.VMEM((half, model), F32)],
        limit=3, after=after)


def feed_grad_kernel(second_half, hidden, low_half, grad_hidden, sets):
    model = second_half.shape[1]
    hid = hidden.shape[1] // sets

    def body(second, hide, low, grad, out):
        for s in range(sets):
            at = slice(s * hid, (s + 1) * hid)
            out[s, 0] = product_tn(low[...], grad[:, at]).astype(BF)
            out[s, 1] = product_tn(second[...], hide[:, at]).astype(BF)

    return local_kernel(
        body,
        [shape((sets, 2, model, hid))],
        (second_half, hidden, low_half, grad_hidden),
        limit=3,
    )[0]


def feed_split_kernel(second_half, hidden, low_half, grad_hidden, owners, sets, after=()):
    model = second_half.shape[1]
    hid = hidden.shape[1] // sets
    rows = model // owners
    half = hid // 2

    def body(second, hide, low, grad, keep, send, whole):
        order = Order("dp")
        for s in range(sets):
            lanes = slice(s * hid, (s + 1) * hid)
            whole[:model] = product_tn(low[...], grad[:, lanes]).astype(BF)
            whole[model:] = product_tn(second[...], hide[:, lanes]).astype(BF)
            for b in range(owners):
                out = send if b % 2 else keep
                for i in range(2):
                    at = pl.ds(pl.multiple_of(i * model + order[b] * rows, 16), rows)
                    for h in range(2):
                        to = (2 * i + h) * rows
                        out[b // 2, s, to : to + rows, :] = whole[at, h * half : (h + 1) * half]

    return local_kernel(
        body,
        [shape((owners // 2, sets, 4 * rows, half))] * 2,
        (second_half, hidden, low_half, grad_hidden),
        [pltpu.VMEM((2 * model, hid), BF)],
        limit=6, after=after)


def layer_sum_kernel(parts, after=()):
    dims = parts[0].shape

    def body(*refs):
        keep, send = refs[4:]
        keep[...] = refs[0][...].astype(F32) + refs[1][...].astype(F32)
        send[...] = (refs[2][...].astype(F32) + refs[3][...].astype(F32)).astype(BF)

    return local_kernel(body, [shape(dims, F32), shape(dims)], tuple(parts), after=after)


def feed_final_kernel(keep, got):
    high, half = keep.shape
    rows = high // 4

    def body(keep, got, grad_in, grad_down):
        total = keep[...] + got[...].astype(F32)
        for i, out in enumerate((grad_in, grad_down)):
            for h in range(2):
                at = (2 * i + h) * rows
                out[:, h * half : (h + 1) * half] = total[at : at + rows]

    return local_kernel(body, [shape((rows, 2 * half), F32)] * 2, (keep, got), limit=3)


def conv_final_kernel(keep, got, after=()):
    part, wide = keep.shape
    local = wide // 2

    def body(keep, got, grad):
        total = keep[...] + got[...].astype(F32)
        for h in range(2):
            grad[:, h * part : (h + 1) * part] = total[:, h * local : (h + 1) * local].T

    return local_kernel(body, [shape((local, 2 * part), F32)], (keep, got), limit=3, after=after)[0]


def attention_back_kernel(blocks, out_own, packed, probs, weights, after=()):
    number = len(blocks)
    high, model = blocks[0].shape
    rows = high - 16
    seq = number * rows
    heads = probs.shape[0]
    local = packed.shape[2]
    size = local // heads

    def body(*refs):
        order = Order("mp")
        blk = refs[:number]
        wo, pack, prob, w, full, grads, gains = refs[number : number + 7]
        outs = refs[number + 7 : 2 * number + 7]
        total, grad_attn = refs[2 * number + 7 :]
        sums = jnp.zeros((16, model), F32)
        for m in range(number):
            full[pl.ds(pl.multiple_of(order[m] * rows, 16), rows), :] = blk[m][:rows]
            sums = sums + blk[m][rows:].astype(F32)
        gains[...] = sums
        grad_attn[...] = product(full[...], wo[0]).astype(BF)
        for h in range(heads):
            at = slice(h * size, (h + 1) * size)
            p = prob[h].astype(F32)
            grad_probs = product_nt(grad_attn[:, at], pack[2, :, at])
            inner = jnp.sum(grad_probs * p, axis=-1, keepdims=True)
            scores = (p * (grad_probs - inner)).astype(BF)
            grads[0, :, at] = (product(scores, pack[1, :, at]) * 0.125).astype(BF)
            grads[1, :, at] = (product_tn(scores, pack[0, :, at]) * 0.125).astype(BF)
            grads[2, :, at] = product_tn(prob[h], grad_attn[:, at]).astype(BF)
        total[...] = (
            product_nt(grads[0], w[0]) + product_nt(grads[1], w[1]) + product_nt(grads[2], w[2])
        )
        spill(order, total, outs, rows)

    return local_kernel(
        body,
        [shape((seq, model)), shape((3, seq, local)), shape((16, model), F32)]
        + [shape((rows, model))] * number,
        (*blocks, out_own, packed, probs, weights),
        [pltpu.VMEM((seq, model), F32), pltpu.VMEM((seq, local), BF)],
        limit=3, after=after)


def qkv_grad_kernel(tokens, grads, first_low, attn):
    model = tokens.shape[1]
    local = attn.shape[1]

    def body(x, g, first, a, out):
        for i in range(3):
            out[i] = product_tn(x[...], g[i]).astype(BF)
        out[3] = product_tn(first[...], a[...]).astype(BF)

    return local_kernel(
        body,
        [shape((4, model, local))],
        (tokens, grads, first_low, attn),
        limit=2,
        scalars=0,
    )[0]


def qkv_split_kernel(tokens, grads, first_low, attn, gains, gain_count, owners, after=()):
    model = tokens.shape[1]
    local = attn.shape[1]
    rows = model // owners

    def body(x, g, first, a, gain, keep, send, whole, small):
        order = Order("dp")
        for i in range(3):
            whole[i] = product_tn(x[...], g[i]).astype(BF)
        whole[3] = product_tn(first[...], a[...]).astype(BF)
        small[...] = jnp.zeros_like(small)
        for d in range(owners):
            small[d, :gain_count, :rows] = gain[:gain_count, d * rows : (d + 1) * rows]
        for b in range(owners):
            out = send if b % 2 else keep
            at = pl.ds(pl.multiple_of(order[b] * rows, 16), rows)
            for i in range(4):
                to, lane = i // 2 * rows, i % 2 * local
                out[b // 2, to : to + rows, lane : lane + local] = whole[i, at, :]
            out[b // 2, 2 * rows :, :] = small[order[b]].astype(BF)

    return local_kernel(
        body,
        [shape((owners // 2, 2 * rows + 16, 2 * local))] * 2,
        (tokens, grads, first_low, attn, gains),
        [pltpu.VMEM((4, model, local), BF), pltpu.VMEM((owners, 16, 2 * local), F32)],
        limit=4, after=after)


def qkv_final_kernel(blocks, gain_shape):
    high, wide = blocks[0].shape
    rows, local = (high - 16) // 2, wide // 2
    number = len(blocks)
    gain_count, gain_cols = gain_shape

    def body(*refs):
        qkv, out, gain = refs[number:]
        total = refs[0][...].astype(F32)
        for ref in refs[1:number]:
            total = total + ref[...].astype(F32)
        qkv[0] = total[:rows, :local]
        qkv[1] = total[:rows, local:]
        qkv[2] = total[rows : 2 * rows, :local]
        out[...] = total[rows : 2 * rows, local:].T
        gain[...] = total[2 * rows : 2 * rows + gain_count, :gain_cols]

    return local_kernel(
        body,
        [shape((3, rows, local), F32), shape((local, rows), F32), shape(gain_shape, F32)],
        tuple(blocks),
        limit=3,
    )


def char_final_kernel(blocks, shapes):
    high, wide = blocks[0].shape
    rows = high // 2
    number = len(blocks)
    ih_cols, symbols, groups, bias_shape, hh_shape = shapes
    misc = wide - 128
    units = hh_shape[1]

    def body(*refs):
        ih, table, group, bias, hh = refs[number:]
        total = refs[0][...].astype(F32)
        for ref in refs[1:number]:
            total = total + ref[...].astype(F32)
        ih[...] = total[:rows, :ih_cols]
        table[...] = total[:rows, ih_cols : ih_cols + symbols]
        last = total[:rows, misc:]
        group[...] = last[:, GROUP_LANE : GROUP_LANE + groups]
        bias[...] = last[: bias_shape[0], : bias_shape[1]]
        for g in range(hh_shape[0] // rows):
            hh[g * rows : (g + 1) * rows, :] = total[rows:, g * units : (g + 1) * units]

    return local_kernel(
        body,
        [
            shape((rows, ih_cols), F32),
            shape((rows, symbols), F32),
            shape((rows, groups), F32),
            shape(bias_shape, F32),
            shape(hh_shape, F32),
        ],
        tuple(blocks),
    )


def sum_kernel(residual, parts, after=()):
    number = len(parts)

    def body(*refs):
        total = refs[0][...]
        for ref in refs[1 : number + 1]:
            total = total + ref[...].astype(F32)
        refs[number + 1][...] = total.astype(BF)

    return local_kernel(body, [shape(residual.shape)], (residual, *parts), after=after)[0]


def stack_kernel(blocks, after=()):
    number = len(blocks)

    def body(*refs):
        for i in range(number):
            refs[number][i] = refs[i][...]

    return local_kernel(body, [shape((number,) + blocks[0].shape)], tuple(blocks), after=after)[0]


def merge_kernel(keep, got, after=()):
    number = keep.shape[0]
    dims = keep.shape[1:]

    def body(keep, got, *outs):
        for i, out in enumerate(outs):
            out[...] = (keep[i].astype(F32) + got[i].astype(F32)).astype(BF)

    return local_kernel(body, [shape(dims)] * number, (keep, got), limit=4, after=after)


def merge_two_kernel(keep, got, after=()):
    dims = keep.shape[2:]

    def body(keep, got, *outs):
        for out, half, picks in zip(outs, (0, 0, 1, 1), ((0, 1), (2, 3), (0, 2), (1, 3))):
            for at, i in enumerate(picks):
                out[at] = (keep[i, half].astype(F32) + got[i, half].astype(F32)).astype(BF)

    return local_kernel(
        body, [shape((2,) + dims)] * 4, (keep, got), limit=4, after=after
    )


def relay_kernel(first_keep, first_got, second_keep, second_got, after=()):
    dims = first_keep.shape[1:]

    def body(first_keep, first_got, second_keep, second_got, *outs):
        for i, (keep, got) in enumerate(((first_keep, first_got), (second_keep, second_got))):
            for at in range(2):
                total = keep[at].astype(F32) + got[at].astype(F32)
                outs[2 * i + at][...] = total.astype(BF)

    return local_kernel(
        body,
        [shape(dims)] * 4,
        (first_keep, first_got, second_keep, second_got),
        after=after,
    )


def pack_kernel(ih, hh, bias, table, group, out, gains):
    rows, ih_cols = ih.shape
    hh_rows, units = hh.shape
    symbols, groups = table.shape[1], group.shape[1]
    lanes = -(-symbols // 128) * 128
    misc = ih_cols + lanes
    wide = misc + 128
    half, local = out.shape[0] // 2, out.shape[1]

    args = (ih, hh, bias, table, group, out, gains)

    def body(*refs):
        copies = [
            pltpu.make_async_copy(refs[i], refs[10 + i], refs[17].at[i]) for i in range(7)
        ]
        for copy in copies:
            copy.start()
        pack, top, low = refs[7:10]
        ih, hh, bias, table, group, out, gains = refs[10:17]
        top[...] = jnp.zeros_like(top)
        low[...] = jnp.zeros_like(low)
        for copy in copies:
            copy.wait()
        top[:rows, :ih_cols] = ih[...].astype(F32)
        top[:rows, ih_cols : ih_cols + symbols] = table[...].astype(F32)
        top[: bias.shape[0], misc : misc + bias.shape[1]] = bias[...].astype(F32)
        top[:rows, misc + GROUP_LANE : misc + GROUP_LANE + groups] = group[...].astype(F32)
        steps = hh[...].astype(F32)
        for g in range(hh_rows // rows):
            top[rows:, g * units : (g + 1) * units] = steps[g * rows : (g + 1) * rows]
        pack[:, :wide] = top[...].astype(BF)
        low[:half, :local] = out[:half].astype(F32)
        low[:half, local:] = out[half:].astype(F32)
        low[half : half + gains.shape[0], : gains.shape[1]] = gains[...].astype(F32)
        for g in range((half + 16) // 16):
            at = wide + g * 2 * local
            pack[:, at : at + 2 * local] = low[g * 16 : (g + 1) * 16].astype(BF)

    vmem = pl.BlockSpec(memory_space=pltpu.VMEM)
    return pl.pallas_call(
        body,
        out_shape=shape((2 * rows, wide + (half + 16) // 16 * 2 * local)),
        in_specs=[pl.BlockSpec(memory_space=pltpu.HBM)] * 7,
        out_specs=vmem,
        scratch_shapes=[pltpu.VMEM((2 * rows, wide), F32), pltpu.VMEM((half + 16, 2 * local), F32)]
        + [pltpu.VMEM(arg.shape, BF) for arg in args]
        + [pltpu.SemaphoreType.DMA((7,))],
        compiler_params=pltpu.CompilerParams(vmem_limit_bytes=5 * MB),
        name="pack_kernel",
    )(*args)


def pack_layer_kernel(ffn_in, ffn_down, conv, after):
    rows, hid = ffn_in.shape
    local, taps = conv.shape
    half, part = hid // 2, taps // 2

    def body(wi, wd, conv, out):
        for i, ref in enumerate((wi, wd)):
            for h in range(2):
                at = (2 * i + h) * rows
                out[at : at + rows, :] = ref[:, h * half : (h + 1) * half]
        both = conv[...].astype(F32).T.astype(BF)
        for h in range(2):
            out[4 * rows :, h * local : (h + 1) * local] = both[h * part : (h + 1) * part]

    return local_kernel(
        body,
        [shape((4 * rows + part, half))],
        (ffn_in, ffn_down, conv),
        limit=3,
        after=after,
    )[0]


def unpack_layer_kernel(lists, rows, after=()):
    sets, number = len(lists), len(lists[0])
    high, half = lists[0][0].shape
    part = high - 4 * rows
    local = half // 2

    def body(*refs):
        order = Order("dp")
        outs, conv = refs[sets * number : sets * number + 2], refs[sets * number + 2]
        for a in range(number):
            at = pl.ds(pl.multiple_of(order[a] * rows, 16), rows)
            for s in range(sets):
                ref = refs[s * number + a]
                for i in range(2):
                    for h in range(2):
                        to = (2 * i + h) * rows
                        outs[i][s, at, h * half : (h + 1) * half] = ref[to : to + rows, :]
                for h in range(2):
                    to = pl.ds(pl.multiple_of((order[a] * 2 + h) * part, 16), part)
                    conv[to, s * local : (s + 1) * local] = ref[
                        4 * rows :, h * local : (h + 1) * local
                    ]

    return local_kernel(
        body,
        [shape((sets, number * rows, 2 * half))] * 2
        + [shape((number * 2 * part, sets * local))],
        tuple(lists[0]) + tuple(lists[1]), after=after)


def unpack_out_kernel(lists, start, local, gain_shape):
    number = len(lists[0])
    each, high, _ = lists[0][0].shape
    depth = 2 * each
    gain_count, gain_cols = gain_shape
    rows = gain_cols
    half = rows // 2

    def body(*refs):
        order = Order("dp")
        out, gain, stack = refs[2 * number :]
        for a in range(number):
            for m in range(depth):
                ref = refs[m // each * number + a]
                for g in range(half // 16):
                    for h in range(2):
                        at = pl.ds(
                            pl.multiple_of(order[a] * rows + h * half + g * 16, 16), 16
                        )
                        lane = start + (2 * g + h) * local
                        out[m, at, :] = ref[m % each, :, lane : lane + local]
            stack[order[a]] = refs[a][0, :, start + half // 16 * 2 * local :].astype(F32)
        for d in range(number):
            gain[:, d * gain_cols : (d + 1) * gain_cols] = stack[d, :gain_count, :gain_cols]

    return local_kernel(
        body,
        [shape((depth, number * rows, local)), shape((gain_count, number * gain_cols), F32)],
        tuple(lists[0]) + tuple(lists[1]),
        [pltpu.VMEM((number, 16, 2 * local), F32)],
    )


def unpack_char_kernel(lists, units, bias_shape, misc):
    number = len(lists[0])
    each, high, _ = lists[0][0].shape
    wide = misc + 128
    depth = 2 * each
    rows = high // 2
    groups = wide // units
    ways, bias_cols = bias_shape
    total = number * depth

    def body(*refs):
        order8, order = Order("dp"), Order("mp")
        pack, hh, bias, steps, small = refs[2 * number :]
        for a in range(number):
            for m in range(depth):
                whole = refs[m // each * number + a][m % each, :, :wide].astype(F32)
                at = (a * depth + m) * rows
                if m % 2 == 0:
                    before = whole[:rows]
                else:
                    pack[at - rows : at + rows, :] = jnp.concatenate(
                        [before, whole[:rows]], 0
                    ).astype(BF)
                place = order8[a] * depth + order[m]
                small[place] = whole[:rows, misc:]
                steps[place] = jnp.concatenate(
                    [whole[rows:, g * units : (g + 1) * units] for g in range(groups)], 0
                )
        hh[...] = steps[...].reshape(total * groups * rows, units).astype(BF)
        for k in range(total):
            bias[:, k * bias_cols : (k + 1) * bias_cols] = small[k, :ways, :bias_cols]

    return local_kernel(
        body,
        [
            shape((total * rows, wide)),
            shape((total * groups * rows, units)),
            shape((ways, total * bias_cols), F32),
        ],
        tuple(lists[0]) + tuple(lists[1]),
        [
            pltpu.VMEM((total, groups * rows, units), F32),
            pltpu.VMEM((total, rows, wide - misc), F32),
        ],
        limit=6,
    )


def widen_kernel(blocks, after=()):
    number = len(blocks)
    rows, model = blocks[0].shape

    def body(*refs):
        order = Order("mp")
        out = refs[number]
        for m in range(number):
            at = pl.ds(pl.multiple_of(order[m] * rows, 16), rows)
            out[at, :] = refs[m][...].astype(F32)

    return local_kernel(
        body, [shape((number * rows, model), F32)], tuple(blocks), limit=2, after=after)[0]


def sigmoid(v):
    return 0.5 * jnp.tanh(0.5 * v) + 0.5


def one_hot(symbols, group, lanes, table_lanes):
    lane = lax.broadcasted_iota(jnp.int32, (symbols.shape[0], lanes), 1)
    hit = (lane == symbols) | (lane == table_lanes + GROUP_LANE + group)
    return hit.astype(F32).astype(BF)


def symbols_kernel(group, letters, counts, own_rows, table_lanes):
    seq = counts.shape[1]
    chars = letters.shape[1]
    every = own_rows + HALO

    lanes = table_lanes + 128

    def body(group_ref, let, cnt, hits, alive_all, alive):
        spot = Spot(seq)
        row = lax.broadcasted_iota(jnp.int32, (every, seq), 0)
        mine = jnp.where(
            row < own_rows, spot.own * own_rows + row, spot.beside_row - own_rows + row
        )
        line = lax.broadcasted_iota(jnp.int32, (every, seq), 1)
        sizes = cnt[...].astype(F32)
        start = jnp.sum(jnp.where(line < mine, sizes, 0.0), axis=1, keepdims=True)
        size = jnp.sum(jnp.where(line == mine, sizes, 0.0), axis=1, keepdims=True)
        letter = lax.broadcasted_iota(jnp.int32, (every, chars), 1).astype(F32)
        values = let[...].astype(F32)
        for slot in range(MAXC):
            alive_all[slot] = jnp.where(size > slot, 1.0, 0.0)
            alive[slot] = alive_all[slot, :own_rows]
            for way in range(2):
                if way == 0:
                    at = start + jnp.minimum(float(slot), size - 1.0)
                else:
                    at = start + jnp.maximum(size - 1.0 - slot, 0.0)
                found = jnp.sum(jnp.where(letter == at, values, 0.0), axis=1, keepdims=True)
                found = found.astype(jnp.int32)
                hits[way, slot] = one_hot(found, group_ref[0], lanes, table_lanes)

    return local_kernel(
        body,
        [
            shape((2, MAXC, every, lanes)),
            shape((MAXC, every, 1), F32),
            shape((MAXC, own_rows, 1), F32),
        ],
        (group, letters, counts),
        scalars=1,
    )


def encoder_forward(hits_all, alive_all, char_pack, hh_full, bias_full, own_rows, after=()):
    units = hh_full.shape[1]
    width = 3 * units
    lanes = hits_all.shape[3]
    embed = char_pack.shape[0]
    every = own_rows + HALO
    saved_shape = shape((2, MAXC, own_rows, units))

    def body(
        hits, alive_all, pack, hh, bias,
        final, beside, emb, prev, rst, upd, car, fre,
        state, emb_all,
    ):
        for way in range(2):
            rows = product_nt(hits[way].reshape(MAXC * every, lanes), pack[:, 2 * width :]).astype(BF)
            emb_all[way] = rows.reshape(MAXC, every, embed)
        emb[...] = emb_all[:, :, :own_rows]
        state[...] = jnp.zeros_like(state)

        @pl.loop(0, MAXC)
        def _(slot):
            live_col = alive_all[slot]
            for way in range(2):
                hidden = state[way]
                low = hidden.astype(BF)
                prev[way, slot] = low[:own_rows]
                gate = product(emb_all[way, slot], pack[:, way * width : (way + 1) * width])
                rec = product_nt(low, hh[way * width : (way + 1) * width])
                b_r = bias[way : way + 1, :units]
                b_z = bias[way : way + 1, units : 2 * units]
                b_n = bias[way : way + 1, 2 * units : 3 * units]
                b_c = bias[way : way + 1, 3 * units :]
                reset = sigmoid(gate[:, :units] + b_r + rec[:, :units])
                update = sigmoid(gate[:, units : 2 * units] + b_z + rec[:, units : 2 * units])
                carried = rec[:, 2 * units :] + b_c
                fresh = jnp.tanh(gate[:, 2 * units :] + b_n + reset * carried)
                rst[way, slot] = reset[:own_rows].astype(BF)
                upd[way, slot] = update[:own_rows].astype(BF)
                car[way, slot] = carried[:own_rows].astype(BF)
                fre[way, slot] = fresh[:own_rows].astype(BF)
                moved = (1.0 - update) * fresh + update * hidden
                state[way] = hidden + live_col * (moved - hidden)

        for way in range(2):
            low = state[way].astype(BF)
            final[:, way * units : (way + 1) * units] = low[:own_rows]
            beside[:, way * units : (way + 1) * units] = low[own_rows:]

    return local_kernel(
        body,
        [
            shape((own_rows, 2 * units)),
            shape((HALO, 2 * units)),
            shape((2, MAXC, own_rows, embed)),
        ]
        + [saved_shape] * 5,
        (hits_all, alive_all, char_pack, hh_full, bias_full),
        [
            pltpu.VMEM((2, every, units), F32),
            pltpu.VMEM((2, MAXC, every, embed), BF),
        ],
        limit=6,
        after=after)


def encoder_steps(grad_parts, hh_full, live, saved, after=()):
    own_rows = live.shape[1]
    units = hh_full.shape[1]
    width = 3 * units
    count = MAXC * own_rows
    pieces = len(grad_parts)

    def body(*refs):
        parts = refs[:pieces]
        hh, alive, prev, rst, upd, car, fre, low, inner_low, bias_grad, grad, sums = refs[pieces:]
        whole = parts[0][...].astype(F32)
        for part in parts[1:]:
            whole = whole + part[...].astype(F32)
        for way in range(2):
            grad[way] = whole[:, way * units : (way + 1) * units]
        sums[...] = jnp.zeros_like(sums)

        @pl.loop(0, MAXC)
        def _(step):
            slot = MAXC - 1 - step
            live_col = alive[slot]
            at = pl.ds(pl.multiple_of(slot * own_rows, 16), own_rows)
            for way in range(2):
                before = prev[way, slot].astype(F32)
                reset = rst[way, slot].astype(F32)
                update = upd[way, slot].astype(F32)
                carried = car[way, slot].astype(F32)
                fresh = fre[way, slot].astype(F32)
                g = grad[way]
                moved = live_col * g
                grad_fresh = moved * (1.0 - update)
                grad_update = moved * (before - fresh)
                grad_inner = grad_fresh * (1.0 - fresh * fresh)
                grad_carried = grad_inner * reset
                grad_reset = grad_carried * carried * (1.0 - reset)
                grad_z = grad_update * update * (1.0 - update)
                for part, what in enumerate((grad_reset, grad_z, grad_inner, grad_carried)):
                    sums[way, part] += jnp.sum(what.reshape(own_rows // 8, 8, units), 0)
                low[way, at, :units] = grad_reset.astype(BF)
                low[way, at, units : 2 * units] = grad_z.astype(BF)
                low[way, at, 2 * units :] = grad_carried.astype(BF)
                inner_low[way, at, :] = grad_inner.astype(BF)
                back = product(low[way, at, :], hh[way * width : (way + 1) * width])
                grad[way] = g - moved + moved * update + back

        for way in range(2):
            for part in range(4):
                bias_grad[way : way + 1, part * units : (part + 1) * units] = jnp.sum(
                    sums[way, part], 0, keepdims=True
                )

    return local_kernel(
        body,
        [
            shape((2, count, width)),
            shape((2, count, units)),
            shape((2, 4 * units), F32),
        ],
        (*grad_parts, hh_full, live, *saved),
        [pltpu.VMEM((2, own_rows, units), F32), pltpu.VMEM((2, 4, 8, units), F32)],
        limit=3, after=after)


def encoder_backward(
    split, steps_out, hits_all, char_pack, embeds, previous, table_lanes, bias_cols, after=()
):
    low_all, inner_all, bias_all = steps_out
    units = inner_all.shape[2]
    width = 3 * units
    lanes = table_lanes + 128
    embed, wide = char_pack.shape
    count = low_all.shape[1]

    def body(*refs):
        sym, pack, low, inner_low, bias_grad, emb, prev = refs[:7]
        results = refs[7 : 9 + (not split)]
        hh_grad = refs[9 + (not split)]
        if split:
            order8, order = Order("dp"), Order("mp")
            keep, send = results
            owners, depth = split
            strip = embed // owners
            steps = 2 * width // owners
            small = refs[-1]

        def pack_out(value, left):
            if not split:
                results[0][:, left : left + value.shape[1]] = value.astype(BF)
                return
            for b in range(owners):
                out = send if b % 2 else keep
                out[b // 2, 0, :, left : left + value.shape[1]] = value[
                    b * strip : (b + 1) * strip
                ].astype(BF)

        table_total = jnp.zeros((embed, lanes), F32)
        for way in range(2):
            rows = emb[way].reshape(count, embed)
            gates = low[way, :, : 2 * units]
            inner = inner_low[way]
            left = way * width
            pack_out(product_tn(rows, gates), left)
            pack_out(product_tn(rows, inner), left + 2 * units)
            embed_grad = product_nt(gates, pack[:, left : left + 2 * units]) + product_nt(
                inner, pack[:, left + 2 * units : left + width]
            )
            hits = sym[way, :, : count // MAXC].reshape(count, lanes)
            table_total = table_total + product_tn(embed_grad.astype(BF), hits)
            hh_grad[left : left + width] = product_tn(
                low[way], prev[way].reshape(count, units)
            ).astype(BF)
        if not split:
            pack_out(table_total, 2 * width)
            results[1][...] = hh_grad[...]
            results[2][...] = bias_grad[...]
            return
        pack_out(table_total[:, :table_lanes], 2 * width)
        small[...] = jnp.zeros_like(small)
        for k in range(owners * depth):
            small[k, :2, :bias_cols] = bias_grad[:, k * bias_cols : (k + 1) * bias_cols]
        lane = lax.broadcasted_iota(jnp.int32, (strip, 128), 1)
        for b in range(owners):
            out = send if b % 2 else keep
            mine = jnp.concatenate([small[order8[b] * depth + order[m]] for m in range(depth)], 0)
            last = table_total[b * strip : (b + 1) * strip, table_lanes:]
            out[b // 2, 0, :, wide - 128 :] = jnp.where(lane < GROUP_LANE, mine, last).astype(BF)
            for g in range(steps // strip):
                at = pl.ds(pl.multiple_of(order8[b] * steps + g * strip, 16), strip)
                out[b // 2, 1, :, g * units : (g + 1) * units] = hh_grad[at, :]

    outs = [shape(char_pack.shape), shape((2 * width, units)), shape((2, 4 * units), F32)]
    scratch = [pltpu.VMEM((2 * width, units), BF)]
    if split:
        owners, depth = split
        strip = embed // owners
        outs = [shape((owners // 2, 2, strip, wide))] * 2
        scratch.append(pltpu.VMEM((owners * depth, strip // depth, 128), F32))
    return local_kernel(
        body,
        outs,
        (hits_all, char_pack, *steps_out, embeds, previous),
        scratch,
        limit=13.00,
        after=after)


def char_split_kernel(number, blocks, units, after=()):
    strip, wide = blocks[0].shape
    rows = strip // number
    groups = wide // units
    pieces = len(blocks)

    def body(*refs):
        order = Order("mp")
        outs, steps = refs[pieces : pieces + number], refs[pieces + number]
        total = refs[0][...].astype(F32) + refs[1][...].astype(F32)
        below = refs[2][...].astype(F32) + refs[3][...].astype(F32)
        for g in range(groups):
            steps[g * strip : (g + 1) * strip, :] = below[:, g * units : (g + 1) * units]
        for m, out in enumerate(outs):
            low = jnp.concatenate(
                [
                    steps[pl.ds(pl.multiple_of((order[m] * groups + g) * rows, 8), rows), :]
                    for g in range(groups)
                ],
                1,
            )
            out[...] = jnp.concatenate([total[m * rows : (m + 1) * rows], low], 0).astype(BF)

    return local_kernel(
        body,
        [shape((2 * rows, wide))] * number,
        tuple(blocks),
        [pltpu.VMEM((strip * groups, units), F32)],
        limit=2, after=after)


def per_device(
    tokens,
    char_ids,
    token_chars,
    groups,
    qkv_weight,
    out_weight,
    ffn_in,
    ffn_out,
    conv_weight,
    gains,
    ih_weight,
    hh_weight,
    gru_bias,
    char_table,
    group_table,
    token_cot,
    char_cot,
):
    dp_size, mp_size = lax.axis_size("dp"), lax.axis_size("mp")
    mp_index = lax.axis_index("mp")
    seq_len, model = tokens.shape
    local = out_weight.shape[0]
    heads = local // (model // HEADS)
    own_rows = seq_len // mp_size
    ih_rows, ih_cols = ih_weight.shape
    symbols_n, group_count = char_table.shape[0], group_table.shape[0]
    table_lanes = -(-symbols_n // 128) * 128
    misc_at = ih_cols + table_lanes
    units = hh_weight.shape[1]
    bias_cols, gain_cols = gru_bias.shape[1], gains.shape[1]
    both = ("dp", "mp")

    symbols, alive_all, live = symbols_kernel(
        groups, char_ids, token_chars, own_rows, table_lanes
    )

    qkv_own = jnp.transpose(qkv_weight, (1, 0, 2))
    if quick():
        pack = pack_kernel(
            ih_weight, hh_weight, gru_bias, char_table.T, group_table.T, out_weight.T, gains
        )
        qkv_blocks = share_dp(qkv_own, held(p1=pack))
        qkv_full, packed, probs, attn_low, same, other = attention_kernel(
            tokens, qkv_blocks, heads
        )
        attn_blocks = pass_on([same, same, other, other])
        packs = share_mp(pack)
        layer_own = pack_layer_kernel(
            ffn_in, ffn_out.T, conv_weight.T, held(s5=qkv_blocks[2:3], s9=packs[1])
        )
        layer_send = layer_own
        if "s4" in HOLDS:
            layer_send = stack_kernel([layer_own], packs[1:2])[0]
        layer_blocks = share_dp_by(layer_own, ROUTES[0])
        packs_high = stack_kernel(packs[:2], held(s6=same, s7=attn_blocks[1:], s12=layer_blocks[2], s14=alive_all))
        char_high = share_dp_by(packs_high, ROUTES[2])
        packs_low = stack_kernel(packs[2:], held(s6=same, s1=attn_blocks[1:], s13=layer_blocks[4]))
        char_low = share_dp_by(packs_low, ROUTES[3])
        layer_other = swap(layer_send, "mp", 2)
        if "s8" in HOLDS:
            layer_other = stack_kernel([layer_other], (char_high[2], char_low[4]))[0]
        layer_lists = (layer_blocks, share_dp_by(layer_other, ROUTES[1]))
        char_lists = (char_high, char_low)
        out_full, gain_rows = unpack_out_kernel(
            char_lists, misc_at + 128, local, gains.shape
        )
        char_pack, hh_full, bias_full = unpack_char_kernel(
            char_lists, units, gru_bias.shape, misc_at
        )
        in_set, down_set, conv_set = unpack_layer_kernel(
            layer_lists, ffn_in.shape[0], held(s2=attn_blocks[1:], s10=char_pack)
        )
    else:
        qkv_blocks = [lax.all_gather(qkv_own, "dp", axis=1, tiled=True)]
        qkv_full, packed, probs, attn_low, same, other = attention_kernel(
            tokens, qkv_blocks, heads
        )
        attn_blocks = pass_on([same, same, other, other])
        vocab = jnp.pad(char_table.T, ((0, 0), (0, table_lanes - symbols_n)))
        misc = jnp.pad(group_table.T, ((0, 0), (GROUP_LANE, 128 - GROUP_LANE - group_count)))
        char_pack = lax.all_gather(
            jnp.concatenate([ih_weight, vocab, misc], 1), both, axis=0, tiled=True
        )
        hh_full = lax.all_gather(hh_weight, both, axis=0, tiled=True)
        bias_full = lax.all_gather(gru_bias, both, axis=1, tiled=True).astype(F32)
        gain_rows = lax.all_gather(gains, "dp", axis=1, tiled=True).astype(F32)
        out_full = lax.all_gather(
            lax.all_gather(out_weight.T, "dp", axis=0, tiled=True), "mp", axis=0
        )
        order = jnp.stack([mp_index ^ m for m in range(mp_size)]).astype(jnp.int32)
        out_full = jnp.take(out_full, order, axis=0)
        ffn_full = lax.all_gather(jnp.stack([ffn_in, ffn_out.T]), "dp", axis=1, tiled=True)
        ffn_full = jnp.stack([ffn_full, swap(ffn_full, "mp", 2)])
        in_set, down_set = ffn_full[:, 0], ffn_full[:, 1]
        conv_set = lax.all_gather(conv_weight, "dp", axis=0, tiled=True)
        conv_set = jnp.concatenate([conv_set, swap(conv_set, "mp", 2)], 1)
    conv_set = conv_set.reshape(3, 2 * model, 2 * local)

    final, final_beside, embeds, *saved = encoder_forward(
        symbols, alive_all, char_pack, hh_full, bias_full, own_rows
    )
    char_blocks = [final, swap(final, "mp", 1), final_beside]

    low_half, hidden, hidden_slope, normal_one, scale_one, base, keep, send = middle_kernel(
        attn_blocks, tokens, out_full, gain_rows, in_set, down_set, held(s3=final)
    )
    normal_two, scale_two, two_low, two_beside = second_kernel(
        keep, swap(send, "mp", 1), base, gain_rows
    )
    token_blocks = [two_low, swap(two_low, "mp", 1), two_beside]

    mixed, joined_slope, sent = joining_kernel(token_blocks, char_blocks, conv_set)
    (
        token_half, char_half, quarter, own_token, own_char, pre_half, pre_grad, gain_three, gain_four,
        keep, send,
    ) = turn_kernel(
        sent, swap(sent, "mp", 1), mixed, token_cot, char_cot, gain_rows, joined_slope, conv_set
    )
    mixed_token = [keep, swap(send, "mp", 1)]
    keep, send = char_half_kernel(pre_half, conv_set)
    mixed_char = [keep, swap(send, "mp", 1)]
    quarter = swap(quarter, "mp", 2)
    if quick():
        conv_keep, conv_send = conv_split_kernel(mixed, pre_grad, dp_size, 2)
    else:
        conv_send = conv_grad_kernel(mixed, pre_grad)
    grad_second, second_low, gain_two = norm_back_kernel(
        mixed_token, own_token, normal_two, scale_two, gain_rows, 1, (), held(b1=conv_send)
    )
    steps_out = encoder_steps(
        [own_char] + mixed_char, hh_full, live, saved, held(b2=second_low)
    )
    backward = (steps_out, symbols, char_pack, embeds, saved[0], table_lanes, bias_cols)
    hold = held(b3=steps_out[2])
    if quick():
        conv_blocks = merge_two(conv_keep, conv_send)
        hold += held(b4=conv_blocks[0])
    second_half, grad_hidden, keep, send = feed_back_kernel(
        second_low, swap(second_low, "mp", 1), hidden_slope, in_set, down_set, hold
    )
    feed_args = (second_half, hidden, low_half, grad_hidden)
    hold = ()
    if quick():
        char_keep, char_send = encoder_backward(
            (dp_size, mp_size), *backward, held(b5=second_half)
        )
        hold = held(b6=char_send)
        if "b7" not in HOLDS:
            feed_keep, feed_send = feed_split_kernel(*feed_args, dp_size, 2)
            hold += held(b26=feed_send)
    grad_first, first_low, _ = norm_back_kernel(
        [keep, swap(send, "mp", 1)], grad_second, normal_one, scale_one, gain_rows, 0,
        (gain_two, gain_three, gain_four), hold,
    )
    hold = held(b25=steps_out[2])
    if quick():
        if "b7" in HOLDS:
            feed_keep, feed_send = feed_split_kernel(*feed_args, dp_size, 2, (first_low,))
        char_parts = merge_two(char_keep, char_send, held(b8=first_low))
        conv_keep, conv_send = layer_sum_kernel(spread_two(conv_blocks), held(b9=first_low))
        hold += held(b10=feed_send, b11=char_parts[0], b12=conv_keep)
        if "b13" in HOLDS:
            feed_blocks = merge_two(feed_keep, feed_send)
            hold += (feed_blocks[0],)
    first_full, grad_packed, gain_grad, *token_parts = attention_back_kernel(
        share_mp(first_low), out_full, packed, probs, qkv_full, hold
    )
    token_out, char_out = outputs_kernel(
        token_half, char_half, quarter, swap(quarter, "mp", 1), held(b14=first_full)
    )
    token_parts = pass_on(token_parts)
    hold = ()
    if quick():
        if "b13" not in HOLDS:
            feed_blocks = merge_two(feed_keep, feed_send, held(b15=token_parts[1]))
        attn_keep, attn_send = qkv_split_kernel(
            tokens, grad_packed, first_full, attn_low, gain_grad, gains.shape[0], dp_size,
            held(b16=token_parts[1]),
        )
        hold = held(b17=feed_blocks[0], b18=attn_send)
        char_parts = spread_two(char_parts)
        if "b23" in HOLDS:
            char_parts = char_split_kernel(mp_size, char_parts, units)
            hold += (char_parts[0],)
        if "b27" in HOLDS:
            conv_grad = conv_final_kernel(conv_keep, swap(conv_send, "mp", 2))
            hold += (conv_grad,)
    token_own = sum_kernel(grad_first, token_parts, hold)
    token_blocks = share_mp(token_own)
    hold = ()
    if quick():
        attn_parts = merge_dp(attn_keep, attn_send, held(b19=token_own))
        if "b23" not in HOLDS:
            char_parts = char_split_kernel(mp_size, char_parts, units, held(b20=token_blocks[1]))
        if "b27" not in HOLDS:
            conv_grad = conv_final_kernel(conv_keep, swap(conv_send, "mp", 2))
        feed_keep, feed_send = layer_sum_kernel(spread_two(feed_blocks))
        hold = held(b21=char_parts[0], b22=attn_parts[0], b24=feed_keep)
    token_grad = widen_kernel(token_blocks, hold)

    group_at = misc_at + GROUP_LANE
    table_to = ih_cols + symbols_n
    gain_count = gains.shape[0]
    if quick():
        in_grad, down_grad = feed_final_kernel(feed_keep, swap(feed_send, "mp", 2))
        conv_grad = conv_grad.T
        qkv_grad, out_grad, gain_own = qkv_final_kernel(
            spread_dp(attn_parts),
            gains.shape,
        )
        ih_grad, table_grad, group_grad, bias_own, hh_own = char_final_kernel(
            pass_on(char_parts),
            (ih_cols, symbols_n, group_count, gru_bias.shape, hh_weight.shape),
        )
        table_grad, group_grad = table_grad.T, group_grad.T
    else:

        def spread(rows, axis):
            return lax.psum_scatter(rows.astype(F32), both, scatter_dimension=axis, tiled=True)

        attn_grads = qkv_grad_kernel(tokens, grad_packed, first_full, attn_low)
        attn_grads = lax.psum_scatter(
            attn_grads.astype(F32), "dp", scatter_dimension=1, tiled=True
        )
        qkv_grad, out_grad = attn_grads[:3], attn_grads[3].T
        feed_grad = feed_grad_kernel(*feed_args, 2).astype(F32)
        feed_grad = lax.psum_scatter(
            feed_grad[0] + swap(feed_grad[1], "mp", 2), "dp", scatter_dimension=1, tiled=True
        )
        in_grad, down_grad = feed_grad[0], feed_grad[1]
        conv_grad = conv_send.reshape(-1, 2 * local).astype(F32)
        conv_grad = conv_grad[:, :local] + swap(conv_grad[:, local:], "mp", 2)
        conv_grad = lax.psum_scatter(conv_grad, "dp", scatter_dimension=0, tiled=True)
        gain_own = lax.psum_scatter(
            gain_grad[:gain_count], "dp", scatter_dimension=1, tiled=True
        )
        pack_grad, hh_grad, bias_grad = encoder_backward(None, *backward)
        ih_grad = spread(pack_grad[:, :ih_cols], 0)
        hh_own = spread(hh_grad, 0)
        table_grad = spread(pack_grad[:, ih_cols:table_to].T, 1)
        group_grad = spread(pack_grad[:, group_at : group_at + group_count].T, 1)
        bias_own = spread(bias_grad, 1)
    return (
        token_out,
        char_out,
        token_grad,
        jnp.transpose(qkv_grad, (1, 0, 2)),
        out_grad,
        in_grad,
        down_grad.T,
        conv_grad,
        gain_own,
        ih_grad,
        hh_own,
        bias_own,
        table_grad,
        group_grad,
    )


def solution(mesh):
    return jax.shard_map(
        per_device,
        mesh=mesh,
        in_specs=(
            P("dp", None),
            P("dp", None),
            P("dp", None),
            P("dp"),
            P("dp", None, "mp"),
            P("mp", "dp"),
            P("dp", "mp"),
            P("mp", "dp"),
            P("dp", "mp"),
            P(None, "dp"),
            P(("dp", "mp"), None),
            P(("dp", "mp"), None),
            P(None, ("dp", "mp")),
            P(None, ("dp", "mp")),
            P(None, ("dp", "mp")),
            P("dp", None),
            P("dp", None),
        ),
        out_specs=(
            P("dp", None),
            P("dp", None),
            P("dp", None),
            P("dp", None, "mp"),
            P("mp", "dp"),
            P("dp", "mp"),
            P("mp", "dp"),
            P("dp", "mp"),
            P(None, "dp"),
            P(("dp", "mp"), None),
            P(("dp", "mp"), None),
            P(None, ("dp", "mp")),
            P(None, ("dp", "mp")),
            P(None, ("dp", "mp")),
        ),
        check_vma=False,
    )
```
